32 devices in a mesh: rep: 2 (over x), fsdp: 16 (over z, y, core).
Axes of the slice: x: 2, y: 2, z: 4, core: 2. Of those that a mesh axis runs over, the one named last changes fastest.
Arguments:
- pixels: bfloat16 [2, 96, 196, 768], P(None, ('rep', 'fsdp')), may hold values from -9 to 9
- merge_map: int32 [2, 96, 196], P(None, ('rep', 'fsdp')), may hold values from 0 to 195, as said below
- merge_weight: float32 [2, 96, 196], P(None, ('rep', 'fsdp')), may hold values from 0.5 to 2
- counts: int32 [2, 96], P(None, ('rep', 'fsdp')), may hold values from 60 to 196, as said below
- captions: bfloat16 [2, 96, 768], replicated, may hold values from -12 to 12
- pairing: int32 [2, 96], replicated, may hold values from 0 to 95, each once within a row
- embedder: float32 [768, 768], P('fsdp'), may hold values from -0.21875 to 0.21875
- positions: float32 [196, 768], P(None, 'fsdp'), may hold values from -3 to 3
- widener: float32 [768, 5376], P('fsdp'), may hold values from -0.21650635 to 0.21650635
- narrower: float32 [3840, 768], P('fsdp'), may hold values from -0.21875 to 0.21875
- projector: float32 [768, 768], P('fsdp'), may hold values from -0.21875 to 0.21875
- scales: float32 [4, 768], P(None, 'fsdp'), may hold values from 0.33 to 2.34
- biases: float32 [4608], P('fsdp'), may hold values from -1.8 to 1.8
- moment_embedder: float32 [768, 768], P('fsdp'), may hold values from -2.4e-05 to 2.4e-05
- moment_positions: float32 [196, 768], P(None, 'fsdp'), may hold values from -2.4e-05 to 2.4e-05
- moment_widener: float32 [768, 5376], P('fsdp'), may hold values from -2.4e-05 to 2.4e-05
- moment_narrower: float32 [3840, 768], P('fsdp'), may hold values from -2.4e-05 to 2.4e-05
- moment_projector: float32 [768, 768], P('fsdp'), may hold values from -2.4e-05 to 2.4e-05
- moment_scales: float32 [4, 768], P(None, 'fsdp'), may hold values from -2.4e-05 to 2.4e-05
- moment_biases: float32 [4608], P('fsdp'), may hold values from -2.4e-05 to 2.4e-05
- square_embedder: float32 [768, 768], P('fsdp'), may hold values from 3e-13 to 3e-12
- square_positions: float32 [196, 768], P(None, 'fsdp'), may hold values from 3e-13 to 3e-12
- square_widener: float32 [768, 5376], P('fsdp'), may hold values from 3e-13 to 3e-12
- square_narrower: float32 [3840, 768], P('fsdp'), may hold values from 3e-13 to 3e-12
- square_projector: float32 [768, 768], P('fsdp'), may hold values from 3e-13 to 3e-12
- square_scales: float32 [4, 768], P(None, 'fsdp'), may hold values from 3e-13 to 3e-12
- square_biases: float32 [4608], P('fsdp'), may hold values from 3e-13 to 3e-12
Outputs:
- objective: float32 [], replicated
- weight_total: float32 [], replicated
- total_norm: float32 [], replicated
- change_embedder: float32 [768, 768], P('fsdp')
- change_positions: float32 [196, 768], P(None, 'fsdp')
- change_widener: float32 [768, 5376], P('fsdp')
- change_narrower: float32 [3840, 768], P('fsdp')
- change_projector: float32 [768, 768], P('fsdp')
- change_scales: float32 [4, 768], P(None, 'fsdp')
- change_biases: float32 [4608], P('fsdp')
- clipped_embedder: float32 [768, 768], P('fsdp')
- clipped_positions: float32 [196, 768], P(None, 'fsdp')
- clipped_widener: float32 [768, 5376], P('fsdp')
- clipped_narrower: float32 [3840, 768], P('fsdp')
- clipped_projector: float32 [768, 768], P('fsdp')
- clipped_scales: float32 [4, 768], P(None, 'fsdp')
- clipped_biases: float32 [4608], P('fsdp')
The draws below stay inside these ranges and needn't reach their ends.
Inputs may be any that keep to these rules, and one draw needn't show every extreme that they name: `counts`: in every micro-batch one image keeps 196 tokens and one keeps 60. `merge_map`: each patch names a slot below its image's count; every such slot is named by one patch or more. `pairing`: each micro-batch's row names every text once.
All inputs are finite; a program needn't handle non-finite values.
Results may differ from the reference program's by a relative error of at most 0.02.
The reference program's roundings to bfloat16 on the way count: a program that leaves them out, or rounds other values in their place, can miss the bound.
Values may be sent and summed in bfloat16 or wider, within the bound.
No kernel may reach another device: no remote copies, remote signals or barrier semaphores. Data moves between devices by JAX's collectives and lax.ppermute only.
A program may use at most 256 MiB of HBM per device.

```python
import math
import jax
import jax.numpy as jnp
from jax import lax

D = 768
HEADS = 12
HD = 64
FF = 3072
PATCH = 768
E = 768
NP = 196
LIVE_MIN = 60
MICRO = 2
IMG_MB = 3
IMAGES = 96


def merge_plan(key):
    base_count = jax.random.randint(jax.random.fold_in(key, 101), (MICRO, IMAGES), LIVE_MIN, NP + 1)
    full_image = jax.random.randint(jax.random.fold_in(key, 102), (MICRO, 1), 0, IMAGES)
    offset = jax.random.randint(jax.random.fold_in(key, 103), (MICRO, 1), 1, IMAGES)
    small_image = (full_image + offset) % IMAGES
    column = jnp.arange(IMAGES, dtype=jnp.int32)[None, :]
    live_counts = jnp.where(column == full_image, NP, jnp.where(column == small_image, LIVE_MIN, base_count)).astype(jnp.int32)
    image_keys = jax.random.split(jax.random.fold_in(key, 104), MICRO * IMAGES)
    rank_ids = jnp.arange(NP, dtype=jnp.int32)

    def one_image(image_key, live_count):
        shuffle = jax.random.permutation(jax.random.fold_in(image_key, 1), NP)
        spare_slot = jax.random.randint(jax.random.fold_in(image_key, 2), (NP,), 0, live_count)
        slot_ids = jnp.where(rank_ids < live_count, rank_ids, spare_slot).astype(jnp.int32)
        return jnp.zeros((NP,), jnp.int32).at[shuffle].set(slot_ids)
    slot_maps = jax.vmap(one_image)(image_keys, live_counts.reshape(-1))
    return (live_counts, slot_maps.reshape(MICRO, IMAGES, NP).astype(jnp.int32))


def draw_counts(key, part):
    return merge_plan(key)[0]


def draw_merge_map(key, part):
    return merge_plan(key)[1]


def ramp_row(length, start_value):
    fraction = jnp.arange(length, dtype=jnp.float32) / max(length - 1, 1)
    return start_value + fraction


def draw_pixels(key, part):
    shape = (MICRO, IMAGES, NP, PATCH)
    inner = jax.random.fold_in(key, 201)
    base = jnp.clip(jax.random.normal(inner, shape, jnp.float32), -6.0, 6.0)
    factor = ramp_row(PATCH, 0.5)
    return (base * factor).astype(jnp.bfloat16)


def draw_scales(key, part):
    inner = jax.random.fold_in(key, 202)
    noise = 0.1 * jnp.clip(jax.random.normal(inner, (4, D), jnp.float32), -3.0, 3.0)
    factor = ramp_row(D, 0.5)
    return ((1.0 + noise) * factor).astype(jnp.float32)


def draw_widener(key, part):
    inner = jax.random.fold_in(key, 203)
    shape = (D, 3 * D + FF)
    base = jnp.clip(jax.random.normal(inner, shape, jnp.float32), -4.0, 4.0)
    value_ramp = ramp_row(D, 0.5)
    hidden_ramp = ramp_row(FF, 0.5)
    factor = jnp.concatenate([jnp.ones((2 * D,), jnp.float32), value_ramp, hidden_ramp])
    return (base * factor * D ** (-0.5)).astype(jnp.float32)


def steps_of(key, shape, shards, smallest, high):
    level, own = 1.0, jax.random.fold_in(key, 6)
    for axis_at, parts in shards:
        draws = jnp.exp(jax.random.uniform(jax.random.fold_in(own, axis_at), (parts,), jnp.float32, smallest / len(shards), high / len(shards)))
        level = level * jnp.repeat(draws, shape[axis_at] // parts).reshape([-1 if axis == axis_at else 1 for axis in range(len(shape))])
    return level


def normal_values(rng, shape, width, bound, cuts=(), held_as=jnp.bfloat16):
    values = width * jax.random.normal(rng, shape, jnp.float32)
    if cuts:
        values = values * steps_of(rng, shape, cuts, -0.22, 0.18)
    return jnp.clip(values, -bound, bound).astype(held_as)


def setup_inputs(seed: int = 0) -> dict:
    key_list = jax.random.split(jax.random.key(seed), 28)
    return {
        "pixels": draw_pixels(jax.random.fold_in(key_list[27], 71), 0),
        "merge_map": draw_merge_map(jax.random.fold_in(key_list[27], 71), 0),
        "merge_weight": jnp.clip(jnp.exp(math.log(2.0) - 1.3862944 * jax.random.uniform(key_list[2], (MICRO, IMAGES, NP), jnp.float32) ** steps_of(key_list[2], (MICRO, IMAGES, NP), ((1, 32),), -0.2, 0.2)), 0.5, 2.0),
        "counts": draw_counts(jax.random.fold_in(key_list[27], 71), 0),
        "captions": normal_values(key_list[4], (MICRO, IMAGES, E), 2.0, 12.0),
        "pairing": jax.vmap(lambda own: jax.random.permutation(own, IMAGES))(jax.random.split(key_list[5], MICRO)).reshape((MICRO, IMAGES)).astype(jnp.int32),
        "embedder": normal_values(key_list[6], (PATCH, D), PATCH ** -0.5, 0.21875, ((0, 16),), jnp.float32),
        "positions": normal_values(key_list[7], (NP, D), 0.5, 3.0, ((1, 16),), jnp.float32),
        "widener": draw_widener(jax.random.fold_in(key_list[27], 71), 0),
        "narrower": normal_values(key_list[9], (D + FF, D), D ** -0.5, 0.21875, ((0, 16),), jnp.float32),
        "projector": normal_values(key_list[10], (D, E), D ** -0.5, 0.21875, ((0, 16),), jnp.float32),
        "scales": draw_scales(jax.random.fold_in(key_list[27], 71), 0),
        "biases": normal_values(key_list[12], (FF + 2 * D,), 0.3, 1.8, ((0, 16),), jnp.float32),
        "moment_embedder": normal_values(key_list[13], (PATCH, D), (4e-06), 2.4000000848900527e-05, ((0, 16),), jnp.float32),
        "moment_positions": normal_values(key_list[14], (NP, D), (4e-06), 2.4000000848900527e-05, ((1, 16),), jnp.float32),
        "moment_widener": normal_values(key_list[15], (D, 3 * D + FF), (4e-06), 2.4000000848900527e-05, ((0, 16),), jnp.float32),
        "moment_narrower": normal_values(key_list[16], (D + FF, D), (4e-06), 2.4000000848900527e-05, ((0, 16),), jnp.float32),
        "moment_projector": normal_values(key_list[17], (D, E), (4e-06), 2.4000000848900527e-05, ((0, 16),), jnp.float32),
        "moment_scales": normal_values(key_list[18], (4, D), (4e-06), 2.4000000848900527e-05, ((1, 16),), jnp.float32),
        "moment_biases": normal_values(key_list[19], (FF + 2 * D,), (4e-06), 2.4000000848900527e-05, ((0, 16),), jnp.float32),
        "square_embedder": jnp.clip(jnp.exp(math.log(2.9999999880125916e-12) - 2.3025851 * jax.random.uniform(key_list[20], (PATCH, D), jnp.float32) ** steps_of(key_list[20], (PATCH, D), ((0, 16),), -0.2, 0.2)), 2.9999998795923744e-13, 2.9999999880125916e-12),
        "square_positions": jnp.clip(jnp.exp(math.log(2.9999999880125916e-12) - 2.3025851 * jax.random.uniform(key_list[21], (NP, D), jnp.float32) ** steps_of(key_list[21], (NP, D), ((1, 16),), -0.2, 0.2)), 2.9999998795923744e-13, 2.9999999880125916e-12),
        "square_widener": jnp.clip(jnp.exp(math.log(2.9999999880125916e-12) - 2.3025851 * jax.random.uniform(key_list[22], (D, 3 * D + FF), jnp.float32) ** steps_of(key_list[22], (D, 3 * D + FF), ((0, 16),), -0.2, 0.2)), 2.9999998795923744e-13, 2.9999999880125916e-12),
        "square_narrower": jnp.clip(jnp.exp(math.log(2.9999999880125916e-12) - 2.3025851 * jax.random.uniform(key_list[23], (D + FF, D), jnp.float32) ** steps_of(key_list[23], (D + FF, D), ((0, 16),), -0.2, 0.2)), 2.9999998795923744e-13, 2.9999999880125916e-12),
        "square_projector": jnp.clip(jnp.exp(math.log(2.9999999880125916e-12) - 2.3025851 * jax.random.uniform(key_list[24], (D, E), jnp.float32) ** steps_of(key_list[24], (D, E), ((0, 16),), -0.2, 0.2)), 2.9999998795923744e-13, 2.9999999880125916e-12),
        "square_scales": jnp.clip(jnp.exp(math.log(2.9999999880125916e-12) - 2.3025851 * jax.random.uniform(key_list[25], (4, D), jnp.float32) ** steps_of(key_list[25], (4, D), ((1, 16),), -0.2, 0.2)), 2.9999998795923744e-13, 2.9999999880125916e-12),
        "square_biases": jnp.clip(jnp.exp(math.log(2.9999999880125916e-12) - 2.3025851 * jax.random.uniform(key_list[26], (FF + 2 * D,), jnp.float32) ** steps_of(key_list[26], (FF + 2 * D,), ((0, 16),), -0.2, 0.2)), 2.9999998795923744e-13, 2.9999999880125916e-12),
    }


@jax.custom_vjp
def low(v):
    return lax.optimization_barrier(v.astype(jnp.bfloat16)).astype(jnp.float32)

@jax.custom_vjp
def low_back(v):
    return v

def low_keep(v):
    return (low(v), None)

def low_pass(kept, grad):
    return (grad,)

def back_keep(v):
    return (v, None)

def back_low(kept, grad):
    return (low(grad),)
low.defvjp(low_keep, low_pass)
low_back.defvjp(back_keep, back_low)
highest = lax.Precision.HIGHEST
norm_eps = 1e-06
clip_bound = 0.1
beta_first = 0.9
beta_second = 0.999
learn_rate = 0.03
weight_decay = 0.1
adam_eps = 1e-08
step_number = 10
logit_temper = 10.0

def product(left, right):
    return jnp.dot(left, right, precision=highest, preferred_element_type=jnp.float32)

def layer_norm(values, gain_row):
    center = values - lax.optimization_barrier(jnp.mean(values, axis=-1, keepdims=True))
    spread = lax.optimization_barrier(jnp.mean(center * center, axis=-1, keepdims=True))
    return center * lax.rsqrt(spread + norm_eps) * gain_row

def head_norm(values, gain_row):
    return layer_norm(values, gain_row.reshape(values.shape[-2], values.shape[-1]))

def gelu_exact(values):
    return 0.5 * values * (1.0 + lax.erf(values * 0.7071067811865476))

def merge_matrix(slot_map, slot_weight, live_count):
    slot_total = slot_map.shape[-1]
    slot_ids = jnp.arange(slot_total, dtype=jnp.int32)
    member = (slot_map[:, None, :] == slot_ids[None, :, None]).astype(jnp.float32) * slot_weight[:, None, :]
    vacant = (slot_ids[None, :] >= live_count[:, None]).astype(jnp.float32)
    return member / (lax.optimization_barrier(jnp.sum(member, axis=-1)) + vacant)[:, :, None]

def pool_final(stream, gain_row, live_mask, count_float):
    final_rows = layer_norm(stream, gain_row)
    return lax.optimization_barrier(jnp.sum(final_rows * live_mask[:, :, None], axis=1)) / count_float[:, None]

def adam_step(weight, gradient, moment, square, factor):
    clipped = gradient * factor
    moment_new = beta_first * moment + (1.0 - beta_first) * clipped
    square_new = beta_second * square + (1.0 - beta_second) * clipped * clipped
    mean_hat = moment_new / (1.0 - beta_first ** step_number)
    square_hat = square_new / (1.0 - beta_second ** step_number)
    change = -learn_rate * (mean_hat / (jnp.sqrt(square_hat) + adam_eps) + weight_decay * weight)
    return (change, clipped)

def encode(rounded, pixels, slot_map, slot_weight, live_count):
    embedder, positions, widener, narrower, projector, scales, biases = rounded
    images = pixels.shape[0]
    row_count = images * NP
    live_mask = (jnp.arange(NP, dtype=jnp.int32)[None, :] < live_count[:, None]).astype(jnp.float32)
    merger = merge_matrix(slot_map, slot_weight, live_count)
    patches = low_back(product(pixels.reshape(row_count, PATCH), embedder)).reshape(images, NP, D)
    patches = patches + biases[FF + D:] + positions
    merged = jnp.einsum('isp,ipd->isd', merger, patches, precision=highest)
    normed = low(layer_norm(merged, scales[0]))
    widened = low_back(product(normed.reshape(row_count, D), widener))
    queries = low(head_norm(widened[:, :D].reshape(images, NP, HEADS, HD), scales[2]))
    key_rows = low(head_norm(widened[:, D:2 * D].reshape(images, NP, HEADS, HD), scales[3]))
    value_rows = low(widened[:, 2 * D:3 * D].reshape(images, NP, HEADS, HD))
    scores = low_back(jnp.einsum('ishd,ithd->ihst', queries, key_rows, precision=highest)) * HD ** (-0.5)
    scores = jnp.where(live_mask[:, None, None, :] > 0, scores, -1e+30)
    score_top = lax.optimization_barrier(jnp.max(scores, axis=-1, keepdims=True))
    log_total = score_top + jnp.log(lax.optimization_barrier(jnp.sum(jnp.exp(scores - score_top), axis=-1, keepdims=True)))
    softmax = low(jnp.exp(scores - log_total))
    attended = jnp.einsum('ihst,ithd->ishd', softmax, value_rows, precision=highest).reshape(row_count, D)
    attended = low(low_back(attended))
    hidden = low(gelu_exact(widened[:, 3 * D:] + biases[:FF]))
    branch = low_back(product(jnp.concatenate([attended, hidden], axis=1), narrower)).reshape(images, NP, D)
    stream = merged + branch + biases[FF:FF + D]
    pooled = low(pool_final(stream, scales[1], live_mask, live_count.astype(jnp.float32)))
    return low(low_back(product(pooled, projector)))

def contrast(embeds, caption_rows, pair_ids, live_count):
    logits = low_back(product(embeds, caption_rows.T)) * (logit_temper * E ** (-0.5))
    target = (pair_ids[:, None] == jnp.arange(IMAGES, dtype=jnp.int32)[None, :]).astype(jnp.float32)
    row_top = lax.optimization_barrier(jnp.max(logits, axis=1, keepdims=True))
    row_logsum = row_top[:, 0] + jnp.log(lax.optimization_barrier(jnp.sum(jnp.exp(logits - row_top), axis=1)))
    column_top = lax.optimization_barrier(jnp.max(logits, axis=0, keepdims=True))
    column_logsum = column_top[0] + jnp.log(lax.optimization_barrier(jnp.sum(jnp.exp(logits - column_top), axis=0)))
    picked = lax.optimization_barrier(jnp.sum(logits * target, axis=1))
    column_pick = lax.optimization_barrier(jnp.sum(target * column_logsum[None, :], axis=1))
    count_float = live_count.astype(jnp.float32)
    forward_loss = -jnp.sum(count_float * (picked - row_logsum)) / jnp.sum(count_float)
    backward_loss = -jnp.mean(picked - column_pick)
    return 0.5 * (forward_loss + backward_loss)

def reference(pixels, merge_map, merge_weight, counts, captions, pairing, embedder, positions, widener, narrower, projector, scales, biases, moment_embedder, moment_positions, moment_widener, moment_narrower, moment_projector, moment_scales, moment_biases, square_embedder, square_positions, square_widener, square_narrower, square_projector, square_scales, square_biases):
    weights = (embedder, positions, widener, narrower, projector, scales, biases)
    moments = (moment_embedder, moment_positions, moment_widener, moment_narrower, moment_projector, moment_scales, moment_biases)
    squares = (square_embedder, square_positions, square_widener, square_narrower, square_projector, square_scales, square_biases)
    pixel_data = pixels.astype(jnp.float32)
    caption_data = captions.astype(jnp.float32)
    groups = IMAGES // IMG_MB

    def objective_of(*params):
        rounded = tuple((low(value) for value in params))

        def encode_block(block_items):
            return encode(rounded, block_items[0], block_items[1], block_items[2], block_items[3])
        checked = jax.checkpoint(encode_block)
        running = jnp.zeros((), jnp.float32)
        for micro_index in range(MICRO):
            block_items = (pixel_data[micro_index].reshape(groups, IMG_MB, NP, PATCH), merge_map[micro_index].reshape(groups, IMG_MB, NP), merge_weight[micro_index].reshape(groups, IMG_MB, NP), counts[micro_index].reshape(groups, IMG_MB))
            embeds = lax.map(checked, block_items).reshape(IMAGES, E)
            running = running + contrast(embeds, caption_data[micro_index], pairing[micro_index], counts[micro_index])
        return running / MICRO
    objective, pullback = jax.vjp(objective_of, *weights)
    gradients = pullback(jnp.ones((), jnp.float32))
    weight_total = jnp.sum(counts.astype(jnp.float32))
    total_norm = jnp.sqrt(sum((jnp.sum(gradient * gradient) for gradient in gradients)))
    factor = clip_bound / jnp.maximum(total_norm, clip_bound)
    results = [adam_step(weights[index], gradients[index], moments[index], squares[index], factor) for index in range(7)]
    return (objective, weight_total, total_norm, results[0][0], results[1][0], results[2][0], results[3][0], results[4][0], results[5][0], results[6][0], results[0][1], results[1][1], results[2][1], results[3][1], results[4][1], results[5][1], results[6][1])
```

```python
import jax
import jax.numpy as jnp
from jax import lax
from jax.sharding import PartitionSpec as P

HEADS = 12


highest = lax.Precision.HIGHEST
norm_eps = 1e-06
clip_bound = 0.1
beta_first = 0.9
beta_second = 0.999
learn_rate = 0.03
weight_decay = 0.1
adam_eps = 1e-08
step_number = 10
logit_temper = 10.0


def product(left, right):
    return jnp.dot(left, right, preferred_element_type=jnp.float32)


def product_across(left, right):
    return lax.dot_general(
        left, right, (((0,), (0,)), ((), ())), preferred_element_type=jnp.float32
    )


def product_along(left, right):
    return lax.dot_general(
        left, right, (((1,), (1,)), ((), ())), preferred_element_type=jnp.float32
    )


def layer_norm(values, gain_row):
    center = values - jnp.mean(values, axis=-1, keepdims=True)
    spread = jnp.mean(center * center, axis=-1, keepdims=True)
    return center * lax.rsqrt(spread + norm_eps) * gain_row


def head_norm(values, gain_row):
    return layer_norm(values, gain_row.reshape(values.shape[-2], values.shape[-1]))


def gelu_exact(values):
    return 0.5 * values * (1.0 + lax.erf(values * 0.7071067811865476))


def merge_matrix(slot_map, slot_weight, live_count):
    slot_total = slot_map.shape[-1]
    slot_ids = jnp.arange(slot_total, dtype=jnp.int32)
    member = (slot_map[:, None, :] == slot_ids[None, :, None]).astype(jnp.float32) * slot_weight[
        :, None, :
    ]
    vacant = (slot_ids[None, :] >= live_count[:, None]).astype(jnp.float32)
    return member / (jnp.sum(member, axis=-1) + vacant)[:, :, None]


def pool_final(stream, gain_row, live_mask, count_float):
    final_rows = layer_norm(stream, gain_row)
    return jnp.sum(final_rows * live_mask[:, :, None], axis=1) / count_float[:, None]


def adam_step(weight, gradient, moment, square, factor):
    clipped = gradient * factor
    moment_new = beta_first * moment + (1.0 - beta_first) * clipped
    square_new = beta_second * square + (1.0 - beta_second) * clipped * clipped
    mean_hat = moment_new / (1.0 - beta_first**step_number)
    square_hat = square_new / (1.0 - beta_second**step_number)
    change = -learn_rate * (mean_hat / (jnp.sqrt(square_hat) + adam_eps) + weight_decay * weight)
    return (change, clipped)


def bit_swap(size, bit):
    return [(index, index ^ bit) for index in range(size)]


def ordered_pair(own, other, axis, bit):
    low_side = (lax.axis_index(axis) & bit) == 0
    return jnp.where(low_side, own, other), jnp.where(low_side, other, own)


def exchange_steps():
    steps = []
    for axis in ("fsdp", "rep"):
        size = lax.axis_size(axis)
        bit = 1
        while bit < size:
            steps.append((axis, size, bit))
            bit *= 2
    return steps


def column_totals(top, total, sums):
    micro_count = top.shape[0]
    for axis, size, bit in exchange_steps():
        packed = jnp.concatenate([top, total, sums], axis=0)
        other = lax.ppermute(packed, axis, bit_swap(size, bit))
        first, second = ordered_pair(packed, other, axis, bit)
        top_a, top_b = first[:micro_count], second[:micro_count]
        top = jnp.maximum(top_a, top_b)
        total = first[micro_count : 2 * micro_count] * jnp.exp(top_a - top) + second[
            micro_count : 2 * micro_count
        ] * jnp.exp(top_b - top)
        sums = first[2 * micro_count :] + second[2 * micro_count :]
    return top, total, sums


def sum_over(value, axis):
    size = lax.axis_size(axis)
    bit = 1
    while bit < size:
        value = value + lax.ppermute(value, axis, bit_swap(size, bit))
        bit *= 2
    return value


def pack_weights(embedder, positions, widener, narrower, projector, scales, biases):
    model_width = embedder.shape[1]
    blocks = widener.shape[1] // model_width
    rows = [embedder]
    rows += [widener[:, k * model_width : (k + 1) * model_width] for k in range(blocks)]
    rows += [narrower, projector]
    small = jnp.concatenate([positions.reshape(-1), scales.reshape(-1), biases.reshape(-1)])
    small_rows = -(-small.shape[0] // (16 * model_width)) * 16
    small = jnp.pad(small, (0, small_rows * model_width - small.shape[0]))
    rows.append(small.reshape(small_rows, model_width))
    return jnp.concatenate(rows, axis=0)


def unpack_weights(full, shapes):
    owners, _, width = full.shape
    (e_rows, _), (slots, p_cols), (w_rows, w_cols), (n_rows, _), (j_rows, _), (s_rows, s_cols), (
        b_len,
    ) = shapes
    at = 0
    embed = full[:, at : at + e_rows].reshape(owners * e_rows, width)
    at += e_rows
    wide = []
    for _ in range(w_cols // width):
        wide.append(full[:, at : at + w_rows].reshape(owners * w_rows, width))
        at += w_rows
    narrow = full[:, at : at + n_rows].reshape(owners * n_rows, width)
    at += n_rows
    project = full[:, at : at + j_rows].reshape(owners * j_rows, width)
    at += j_rows
    small = full[:, at:].reshape(owners, -1)
    place = small[:, : slots * p_cols].reshape(owners, slots, p_cols)
    place = jnp.swapaxes(place, 0, 1).reshape(slots, owners * p_cols)
    at = slots * p_cols
    scale = small[:, at : at + s_rows * s_cols].reshape(owners, s_rows, s_cols)
    scale = jnp.swapaxes(scale, 0, 1).reshape(s_rows, owners * s_cols)
    at += s_rows * s_cols
    bias = small[:, at : at + b_len].reshape(owners * b_len)
    return embed, place, wide, narrow, project, scale, bias


def pack_grads(owners, embed, place, wide, narrow, project, scale, bias):
    width = embed.shape[1]
    by_owner = lambda grad: grad.astype(jnp.bfloat16).reshape(owners, -1, width)
    rows = [by_owner(embed)]
    rows += [by_owner(block) for block in wide]
    rows += [by_owner(narrow), by_owner(project)]
    flat = lambda grad: jnp.swapaxes(
        grad.astype(jnp.bfloat16).reshape(grad.shape[0], owners, -1), 0, 1
    ).reshape(owners, -1)
    small = jnp.concatenate(
        [flat(place), flat(scale), bias.astype(jnp.bfloat16).reshape(owners, -1)], axis=1
    )
    small_rows = -(-small.shape[1] // (16 * width)) * 16
    small = jnp.pad(small, ((0, 0), (0, small_rows * width - small.shape[1])))
    rows.append(small.reshape(owners, small_rows, width))
    return jnp.concatenate(rows, axis=1)


def unpack_grads(shard, shapes):
    (e_rows, width), (slots, p_cols), (w_rows, w_cols), (n_rows, _), (j_rows, _), (
        s_rows,
        s_cols,
    ), (b_len,) = shapes
    at = 0
    embed = shard[at : at + e_rows]
    at += e_rows
    wide = []
    for _ in range(w_cols // width):
        wide.append(shard[at : at + w_rows])
        at += w_rows
    wide = jnp.concatenate(wide, axis=1)
    narrow = shard[at : at + n_rows]
    at += n_rows
    project = shard[at : at + j_rows]
    at += j_rows
    small = shard[at:].reshape(-1)
    place = small[: slots * p_cols].reshape(slots, p_cols)
    at = slots * p_cols
    scale = small[at : at + s_rows * s_cols].reshape(s_rows, s_cols)
    at += s_rows * s_cols
    bias = small[at : at + b_len]
    return embed, place, wide, narrow, project, scale, bias


def per_device(
    pixels,
    merge_map,
    merge_weight,
    counts,
    captions,
    pairing,
    embedder,
    positions,
    widener,
    narrower,
    projector,
    scales,
    biases,
    moment_embedder,
    moment_positions,
    moment_widener,
    moment_narrower,
    moment_projector,
    moment_scales,
    moment_biases,
    square_embedder,
    square_positions,
    square_widener,
    square_narrower,
    square_projector,
    square_scales,
    square_biases,
):
    weights = (embedder, positions, widener, narrower, projector, scales, biases)
    shapes = tuple(weight.shape for weight in weights)
    owners = lax.axis_size("fsdp")
    packed = pack_weights(*(weight.astype(jnp.bfloat16) for weight in weights))
    full = lax.all_gather(packed, "fsdp", axis=0)
    embed_full, place_full, wide_blocks, narrow_full, project_full, scale_full, bias_full = (
        unpack_weights(full, shapes)
    )
    wide_full = jnp.concatenate(wide_blocks, axis=1)
    place_float = place_full.astype(jnp.float32)
    scale_float = scale_full.astype(jnp.float32)
    bias_float = bias_full.astype(jnp.float32)
    micro_count, images_dev, slot_total, patch_size = pixels.shape
    model_width = embed_full.shape[1]
    hidden_width = narrow_full.shape[0] - model_width
    head_count = HEADS
    head_size = model_width // head_count
    images_all = pairing.shape[1]
    embed_width = captions.shape[2]
    logit_factor = logit_temper * embed_width ** (-0.5)
    attend_factor = head_size ** (-0.5)
    row_count = images_dev * slot_total
    grad_embed = jnp.zeros(embed_full.shape, jnp.float32)
    grad_place = jnp.zeros(place_full.shape, jnp.float32)
    grad_wide = jnp.zeros(wide_full.shape, jnp.float32)
    grad_narrow = jnp.zeros(narrow_full.shape, jnp.float32)
    grad_project = jnp.zeros(project_full.shape, jnp.float32)
    grad_scale = jnp.zeros(scale_full.shape, jnp.float32)
    grad_bias = jnp.zeros(bias_full.shape, jnp.float32)
    image_ids = jnp.arange(images_all, dtype=jnp.int32)
    kept = []
    for step_index in range(micro_count):
        pixel_rows = pixels[step_index].reshape(row_count, patch_size)
        live_count = counts[step_index]
        count_float = live_count.astype(jnp.float32)
        live_mask = (jnp.arange(slot_total, dtype=jnp.int32)[None, :] < live_count[:, None]).astype(
            jnp.float32
        )
        key_live = live_mask[:, None, None, :] > 0
        merger = merge_matrix(merge_map[step_index], merge_weight[step_index], live_count)
        patches = product(pixel_rows, embed_full).reshape(images_dev, slot_total, model_width)
        patches = patches + bias_float[hidden_width + model_width :] + place_float
        merged = jnp.einsum("isp,ipd->isd", merger, patches, precision=highest)
        normed, normed_back = jax.vjp(layer_norm, merged, scale_float[0])
        normed_low = normed.astype(jnp.bfloat16).reshape(row_count, model_width)
        widened = product(normed_low, wide_full)
        query_pre = widened[:, :model_width].reshape(images_dev, slot_total, head_count, head_size)
        key_pre = widened[:, model_width : 2 * model_width].reshape(
            images_dev, slot_total, head_count, head_size
        )
        queries, query_back = jax.vjp(head_norm, query_pre, scale_float[2])
        key_rows, key_back = jax.vjp(head_norm, key_pre, scale_float[3])
        query_low = queries.astype(jnp.bfloat16)
        key_low = key_rows.astype(jnp.bfloat16)
        value_low = (
            widened[:, 2 * model_width : 3 * model_width]
            .reshape(images_dev, slot_total, head_count, head_size)
            .astype(jnp.bfloat16)
        )
        scores = (
            jnp.einsum("ishd,ithd->ihst", query_low, key_low, preferred_element_type=jnp.float32)
            * attend_factor
        )
        scores = jnp.where(key_live, scores, -1e30)
        score_top = jnp.max(scores, axis=-1, keepdims=True)
        log_total = score_top + jnp.log(
            jnp.sum(jnp.exp(scores - score_top), axis=-1, keepdims=True)
        )
        softmax = jnp.exp(scores - log_total)
        attended = jnp.einsum(
            "ihst,ithd->ishd",
            softmax.astype(jnp.bfloat16),
            value_low,
            preferred_element_type=jnp.float32,
        )
        attended = attended.reshape(row_count, model_width).astype(jnp.bfloat16)
        hidden, gelu_back = jax.vjp(
            gelu_exact, widened[:, 3 * model_width :] + bias_float[:hidden_width]
        )
        joined = jnp.concatenate([attended, hidden.astype(jnp.bfloat16)], axis=1)
        stream = (
            merged
            + product(joined, narrow_full).reshape(images_dev, slot_total, model_width)
            + bias_float[hidden_width : hidden_width + model_width]
        )
        pooled, pool_back = jax.vjp(
            lambda values, gain_row: pool_final(values, gain_row, live_mask, count_float),
            stream,
            scale_float[1],
        )
        pooled_low = pooled.astype(jnp.bfloat16)
        embeds = product(pooled_low, project_full).astype(jnp.bfloat16)
        kept.append((pixel_rows, live_mask, count_float, key_live, merger, merged, normed_back, normed_low, query_low, key_low, value_low, query_back, key_back, log_total, joined, gelu_back, pool_back, pooled_low, embeds))
    all_embeds = jnp.concatenate([item[-1] for item in kept], axis=0)
    all_logits = [
        product_along(kept[index][-1], captions[index]) * logit_factor
        for index in range(micro_count)
    ]
    first_row = (lax.axis_index("rep") * owners + lax.axis_index("fsdp")) * images_dev
    logits = jnp.stack(all_logits)
    own_pairs = lax.dynamic_slice_in_dim(pairing, first_row, images_dev, 1)
    target = (own_pairs[:, :, None] == image_ids[None, None, :]).astype(jnp.float32)
    row_top = jnp.max(logits, axis=2, keepdims=True)
    row_logsum = row_top[:, :, 0] + jnp.log(jnp.sum(jnp.exp(logits - row_top), axis=2))
    own_top = jnp.max(logits, axis=1)
    own_total = jnp.sum(jnp.exp(logits - own_top[:, None, :]), axis=1)
    picked = jnp.sum(logits * target, axis=2)
    counts_float = counts.astype(jnp.float32)
    scalars = jnp.concatenate(
        [
            jnp.sum(counts_float * (picked - row_logsum), axis=1),
            jnp.sum(picked, axis=1),
            jnp.sum(counts_float, axis=1),
        ]
    )
    sums = jnp.pad(scalars[None, :], ((0, 0), (0, images_all - scalars.shape[0])))
    column_top, column_total, sums = column_totals(own_top, own_total, sums)
    column_logsum = column_top + jnp.log(column_total)
    row_terms = sums[0, :micro_count]
    picked_sums = sums[0, micro_count : 2 * micro_count]
    weight_totals = sums[0, 2 * micro_count : 3 * micro_count]
    weight_total_all = jnp.sum(weight_totals)
    part_losses = 0.5 * (
        -row_terms / weight_totals - (picked_sums - jnp.sum(column_logsum, axis=1)) / images_all
    )
    objective = jnp.sum(part_losses) / micro_count
    row_soft = jnp.exp(logits - row_logsum[:, :, None])
    column_soft = jnp.exp(logits - column_logsum[:, None, :])
    all_grad_logits = (
        0.5
        / micro_count
        * (
            (counts_float / weight_totals[:, None])[:, :, None] * (row_soft - target)
            + (column_soft - target) / images_all
        )
    )
    for step_index in range(micro_count):
        (pixel_rows, live_mask, count_float, key_live, merger, merged, normed_back, normed_low, query_low, key_low, value_low, query_back, key_back, log_total, joined, gelu_back, pool_back, pooled_low, embeds) = kept[step_index]
        grad_logits = all_grad_logits[step_index]
        caption_rows = captions[step_index]
        grad_product = (grad_logits * logit_factor).astype(jnp.bfloat16)
        grad_embeds = product(grad_product, caption_rows).astype(jnp.bfloat16)
        grad_project = grad_project + product_across(pooled_low, grad_embeds)
        grad_pooled = product_along(grad_embeds, project_full)
        grad_stream, grad_final_scale = pool_back(grad_pooled)
        grad_branch = grad_stream.reshape(row_count, model_width).astype(jnp.bfloat16)
        grad_narrow = grad_narrow + product_across(joined, grad_branch)
        grad_joined = product_along(grad_branch, narrow_full)
        grad_attended = (
            grad_joined[:, :model_width]
            .astype(jnp.bfloat16)
            .reshape(images_dev, slot_total, head_count, head_size)
        )
        (grad_act,) = gelu_back(grad_joined[:, model_width:])
        again = (
            jnp.einsum("ishd,ithd->ihst", query_low, key_low, preferred_element_type=jnp.float32)
            * attend_factor
        )
        again = jnp.where(key_live, again, -1e30)
        softmax_again = jnp.exp(again - log_total)
        grad_probs = jnp.einsum(
            "ishd,ithd->ihst", grad_attended, value_low, preferred_element_type=jnp.float32
        )
        row_dot = jnp.sum(softmax_again * grad_probs, axis=-1, keepdims=True)
        grad_scores = (softmax_again * (grad_probs - row_dot) * attend_factor).astype(jnp.bfloat16)
        grad_values = jnp.einsum(
            "ihst,ishd->ithd",
            softmax_again.astype(jnp.bfloat16),
            grad_attended,
            preferred_element_type=jnp.float32,
        )
        grad_queries = jnp.einsum(
            "ihst,ithd->ishd", grad_scores, key_low, preferred_element_type=jnp.float32
        )
        grad_keys = jnp.einsum(
            "ihst,ishd->ithd", grad_scores, query_low, preferred_element_type=jnp.float32
        )
        grad_query_pre, grad_query_scale = query_back(grad_queries)
        grad_key_pre, grad_key_scale = key_back(grad_keys)
        grad_widened = jnp.concatenate(
            [
                grad_query_pre.reshape(row_count, model_width),
                grad_key_pre.reshape(row_count, model_width),
                grad_values.reshape(row_count, model_width),
                grad_act,
            ],
            axis=1,
        ).astype(jnp.bfloat16)
        grad_wide = grad_wide + product_across(normed_low, grad_widened)
        grad_normed = product_along(grad_widened, wide_full).reshape(
            images_dev, slot_total, model_width
        )
        grad_merged_norm, grad_first_scale = normed_back(grad_normed)
        grad_merged = grad_stream + grad_merged_norm
        grad_patches = jnp.einsum("isp,isd->ipd", merger, grad_merged, precision=highest)
        grad_place = grad_place + jnp.sum(grad_patches, axis=0)
        grad_embed = grad_embed + product_across(
            pixel_rows, grad_patches.reshape(row_count, model_width).astype(jnp.bfloat16)
        )
        grad_scale = grad_scale + jnp.stack(
            [grad_first_scale, grad_final_scale, grad_query_scale, grad_key_scale]
        )
        grad_bias = grad_bias + jnp.concatenate(
            [
                jnp.sum(grad_act, axis=0),
                jnp.sum(grad_stream, axis=(0, 1)),
                jnp.sum(grad_patches, axis=(0, 1)),
            ]
        )
    wide_parts = [
        grad_wide[:, k * model_width : (k + 1) * model_width]
        for k in range(grad_wide.shape[1] // model_width)
    ]
    packed_grads = pack_grads(
        owners, grad_embed, grad_place, wide_parts, grad_narrow, grad_project, grad_scale, grad_bias
    )
    shard = lax.psum_scatter(packed_grads, "fsdp", scatter_dimension=0)
    shard = lax.psum(shard, "rep").astype(jnp.float32)
    total_norm = jnp.sqrt(sum_over(jnp.sum(shard * shard), "fsdp"))
    shards = unpack_grads(shard, shapes)
    factor = clip_bound / jnp.maximum(total_norm, clip_bound)
    moments = (
        moment_embedder,
        moment_positions,
        moment_widener,
        moment_narrower,
        moment_projector,
        moment_scales,
        moment_biases,
    )
    squares = (
        square_embedder,
        square_positions,
        square_widener,
        square_narrower,
        square_projector,
        square_scales,
        square_biases,
    )
    results = [
        adam_step(weights[index], shards[index], moments[index], squares[index], factor)
        for index in range(7)
    ]
    return (
        objective,
        weight_total_all,
        total_norm,
        results[0][0],
        results[1][0],
        results[2][0],
        results[3][0],
        results[4][0],
        results[5][0],
        results[6][0],
        results[0][1],
        results[1][1],
        results[2][1],
        results[3][1],
        results[4][1],
        results[5][1],
        results[6][1],
    )


def solution(mesh):
    return jax.shard_map(
        per_device,
        mesh=mesh,
        in_specs=(
            P(None, ("rep", "fsdp"), None, None),
            P(None, ("rep", "fsdp"), None),
            P(None, ("rep", "fsdp"), None),
            P(None, ("rep", "fsdp")),
            P(),
            P(),
            P("fsdp", None),
            P(None, "fsdp"),
            P("fsdp", None),
            P("fsdp", None),
            P("fsdp", None),
            P(None, "fsdp"),
            P("fsdp"),
            P("fsdp", None),
            P(None, "fsdp"),
            P("fsdp", None),
            P("fsdp", None),
            P("fsdp", None),
            P(None, "fsdp"),
            P("fsdp"),
            P("fsdp", None),
            P(None, "fsdp"),
            P("fsdp", None),
            P("fsdp", None),
            P("fsdp", None),
            P(None, "fsdp"),
            P("fsdp"),
        ),
        out_specs=(
            P(),
            P(),
            P(),
            P("fsdp", None),
            P(None, "fsdp"),
            P("fsdp", None),
            P("fsdp", None),
            P("fsdp", None),
            P(None, "fsdp"),
            P("fsdp"),
            P("fsdp", None),
            P(None, "fsdp"),
            P("fsdp", None),
            P("fsdp", None),
            P("fsdp", None),
            P(None, "fsdp"),
            P("fsdp"),
        ),
        check_vma=False,
    )
```

```python
import functools

import jax
import jax.numpy as jnp
from jax import lax
from jax.experimental import pallas as pl
from jax.experimental.pallas import tpu as pltpu
from jax.sharding import PartitionSpec as P

HEADS = 12


norm_eps = 1e-06
clip_bound = 0.1
beta_first = 0.9
beta_second = 0.999
learn_rate = 0.03
weight_decay = 0.1
adam_eps = 1e-08
step_number = 10
logit_temper = 10.0


def product(left, right):
    return jnp.dot(left, right, preferred_element_type=jnp.float32)


def product_across(left, right):
    return lax.dot_general(
        left, right, (((0,), (0,)), ((), ())), preferred_element_type=jnp.float32
    )


def product_along(left, right):
    return lax.dot_general(
        left, right, (((1,), (1,)), ((), ())), preferred_element_type=jnp.float32
    )


def adam_step(weight, gradient, moment, square, factor):
    clipped = gradient * factor
    moment_new = beta_first * moment + (1.0 - beta_first) * clipped
    square_new = beta_second * square + (1.0 - beta_second) * clipped * clipped
    mean_hat = moment_new / (1.0 - beta_first**step_number)
    square_hat = square_new / (1.0 - beta_second**step_number)
    change = -learn_rate * (mean_hat / (jnp.sqrt(square_hat) + adam_eps) + weight_decay * weight)
    return (change, clipped)


def bit_swap(size, bit):
    return [(index, index ^ bit) for index in range(size)]


def ordered_pair(own, other, axis, bit):
    low_side = (lax.axis_index(axis) & bit) == 0
    return jnp.where(low_side, own, other), jnp.where(low_side, other, own)


def exchange_steps():
    steps = []
    for axis in ("fsdp", "rep"):
        size = lax.axis_size(axis)
        bit = 1
        while bit < size:
            steps.append((axis, size, bit))
            bit *= 2
    return steps


def column_totals(top, total, sums):
    micro_count = top.shape[0]
    for axis, size, bit in exchange_steps():
        packed = jnp.concatenate([top, total, sums], axis=0)
        other = lax.ppermute(packed, axis, bit_swap(size, bit))
        first, second = ordered_pair(packed, other, axis, bit)
        top_a, top_b = first[:micro_count], second[:micro_count]
        top = jnp.maximum(top_a, top_b)
        total = first[micro_count : 2 * micro_count] * jnp.exp(top_a - top) + second[
            micro_count : 2 * micro_count
        ] * jnp.exp(top_b - top)
        sums = first[2 * micro_count :] + second[2 * micro_count :]
    return top, total, sums


def sum_over(value, axis):
    size = lax.axis_size(axis)
    bit = 1
    while bit < size:
        value = value + lax.ppermute(value, axis, bit_swap(size, bit))
        bit *= 2
    return value


def pack_weights(embedder, positions, widener, narrower, projector, scales, biases):
    model_width = embedder.shape[1]
    blocks = widener.shape[1] // model_width
    rows = [embedder]
    rows += [widener[:, k * model_width : (k + 1) * model_width] for k in range(blocks)]
    rows += [narrower, projector]
    small = jnp.concatenate([positions.reshape(-1), scales.reshape(-1), biases.reshape(-1)])
    small_rows = -(-small.shape[0] // (16 * model_width)) * 16
    small = jnp.pad(small, (0, small_rows * model_width - small.shape[0]))
    rows.append(small.reshape(small_rows, model_width))
    return jnp.concatenate(rows, axis=0)


def unpack_weights(full, shapes):
    owners, _, width = full.shape
    (e_rows, _), (slots, p_cols), (w_rows, w_cols), (n_rows, _), (j_rows, _), (s_rows, s_cols), (
        b_len,
    ) = shapes
    at = 0
    embed = full[:, at : at + e_rows].reshape(owners * e_rows, width)
    at += e_rows
    wide = []
    for _ in range(w_cols // width):
        wide.append(full[:, at : at + w_rows].reshape(owners * w_rows, width))
        at += w_rows
    narrow = full[:, at : at + n_rows].reshape(owners * n_rows, width)
    at += n_rows
    project = full[:, at : at + j_rows].reshape(owners * j_rows, width)
    at += j_rows
    small = full[:, at:].reshape(owners, -1)
    place = small[:, : slots * p_cols].reshape(owners, slots, p_cols)
    place = jnp.swapaxes(place, 0, 1).reshape(slots, owners * p_cols)
    at = slots * p_cols
    scale = small[:, at : at + s_rows * s_cols].reshape(owners, s_rows, s_cols)
    scale = jnp.swapaxes(scale, 0, 1).reshape(s_rows, owners * s_cols)
    at += s_rows * s_cols
    bias = small[:, at : at + b_len].reshape(owners * b_len)
    return embed, place, wide, narrow, project, scale, bias


def pack_grads(owners, embed, place, wide, narrow, project, scale, bias):
    width = embed.shape[1]
    by_owner = lambda grad: grad.astype(jnp.bfloat16).reshape(owners, -1, width)
    rows = [by_owner(embed)]
    rows += [by_owner(block) for block in wide]
    rows += [by_owner(narrow), by_owner(project)]
    flat = lambda grad: jnp.swapaxes(
        grad.astype(jnp.bfloat16).reshape(grad.shape[0], owners, -1), 0, 1
    ).reshape(owners, -1)
    small = jnp.concatenate(
        [flat(place), flat(scale), bias.astype(jnp.bfloat16).reshape(owners, -1)], axis=1
    )
    small_rows = -(-small.shape[1] // (16 * width)) * 16
    small = jnp.pad(small, ((0, 0), (0, small_rows * width - small.shape[1])))
    rows.append(small.reshape(owners, small_rows, width))
    return jnp.concatenate(rows, axis=1)


def unpack_grads(shard, shapes):
    (e_rows, width), (slots, p_cols), (w_rows, w_cols), (n_rows, _), (j_rows, _), (
        s_rows,
        s_cols,
    ), (b_len,) = shapes
    at = 0
    embed = shard[at : at + e_rows]
    at += e_rows
    wide = []
    for _ in range(w_cols // width):
        wide.append(shard[at : at + w_rows])
        at += w_rows
    wide = jnp.concatenate(wide, axis=1)
    narrow = shard[at : at + n_rows]
    at += n_rows
    project = shard[at : at + j_rows]
    at += j_rows
    small = shard[at:].reshape(-1)
    place = small[: slots * p_cols].reshape(slots, p_cols)
    at = slots * p_cols
    scale = small[at : at + s_rows * s_cols].reshape(s_rows, s_cols)
    at += s_rows * s_cols
    bias = small[at : at + b_len]
    return embed, place, wide, narrow, project, scale, bias


def padded_rows(rows):
    return -(-rows // 16) * 16


def split_two(values):
    high = values.astype(jnp.bfloat16)
    return high, (values - high.astype(jnp.float32)).astype(jnp.bfloat16)


def normal_rows(values):
    center = values - jnp.mean(values, axis=-1, keepdims=True)
    rstd = lax.rsqrt(jnp.mean(center * center, axis=-1, keepdims=True) + norm_eps)
    return center * rstd, rstd


def head_mixer(head_size):
    row = lax.broadcasted_iota(jnp.int32, (256, 256), 0) // head_size
    column = lax.broadcasted_iota(jnp.int32, (256, 256), 1) // head_size
    return jnp.where(row == column, 1.0 / head_size, 0.0).astype(jnp.bfloat16)


def head_mean(values, mixer):
    parts = []
    for at in range(0, values.shape[1], 256):
        high, low = split_two(values[:, at : at + 256])
        parts.append(product(high, mixer) + product(low, mixer))
    return jnp.concatenate(parts, axis=1)


def embed_kernel(
    counts_ref, pixel_ref, map_ref, row_ref, column_ref, embed_ref, place_ref, gain_ref,
    merged_ref, normed_ref,
):
    live_count = counts_ref[pl.program_id(0)]
    slots = merged_ref.shape[1]
    patches = product(pixel_ref[0], embed_ref[...]) + place_ref[...]
    high, low = split_two(patches * column_ref[0])
    slot = lax.broadcasted_iota(jnp.int32, (slots, slots), 0)
    member = slot == map_ref[0]
    hot = jnp.where(member, 1.0, 0.0).astype(jnp.bfloat16)
    total = jnp.sum(jnp.where(member, row_ref[0], 0.0), axis=1, keepdims=True)
    vacant = lax.broadcasted_iota(jnp.int32, (slots, 1), 0) >= live_count
    total = total + jnp.where(vacant, 1.0, 0.0)
    merged = (product(hot, high) + product(hot, low)) / total
    merged_ref[0] = merged
    unit, _ = normal_rows(merged)
    normed_ref[0] = (unit * gain_ref[...]).astype(jnp.bfloat16)


def gelu_pair(values):
    size = jnp.abs(values)
    turn = 1.0 / (1.0 + (0.3275911 * 0.7071067811865476) * size)
    bell = jnp.exp(-0.5 * values * values)
    poly = turn * (
        0.5 * 0.254829592
        + turn
        * (
            0.5 * -0.284496736
            + turn
            * (0.5 * 1.421413741 + turn * (0.5 * -1.453152027 + turn * (0.5 * 1.061405429)))
        )
    )
    tail = poly * bell
    share = jnp.where(values >= 0, 1.0 - tail, tail)
    return values * share, share + values * (bell * 0.3989422804014327)


def widen_kernel(
    normed_ref, wide_ref, gain_ref, bias_ref, qkv_ref, rstd_ref, hidden_ref, slope_ref, *, chunk,
    head_size,
):
    step = pl.program_id(0)
    chunks = normed_ref.shape[0] // chunk

    def rows_of(index):
        return pl.ds(pl.multiple_of(index * chunk, chunk), chunk)

    @pl.when(step < 2)
    def _():
        mixer = head_mixer(head_size)
        gain = gain_ref[0]

        @pl.loop(0, chunks)
        def _(index):
            rows = rows_of(index)
            values = product(normed_ref[rows, :], wide_ref[0])
            center = values - head_mean(values, mixer)
            rstd = lax.rsqrt(head_mean(center * center, mixer) + norm_eps)
            rstd_ref[0, rows, :] = rstd
            qkv_ref[0, rows, :] = (center * rstd * gain).astype(jnp.bfloat16)

    @pl.when(step == 2)
    def _():
        @pl.loop(0, chunks)
        def _(index):
            rows = rows_of(index)
            qkv_ref[0, rows, :] = product(normed_ref[rows, :], wide_ref[0]).astype(jnp.bfloat16)

    @pl.when(step > 2)
    def _():
        @pl.loop(0, chunks)
        def _(index):
            rows = rows_of(index)
            values = product(normed_ref[rows, :], wide_ref[0]) + bias_ref[0]
            hidden, slope = gelu_pair(values)
            hidden_ref[0, rows, :] = hidden.astype(jnp.bfloat16)
            slope_ref[0, rows, :] = slope.astype(jnp.bfloat16)


def attend_kernel(
    counts_ref, qkv_ref, hidden_ref, merged_ref, narrow_hbm, bias_ref, gain_ref,
    attended_ref, stream_ref, pooled_ref, narrow_ref, sem, *, head_size,
):
    image = pl.program_id(0)
    live_count = counts_ref[image]
    slots, width = merged_ref.shape[1:]
    copy = pltpu.make_async_copy(narrow_hbm, narrow_ref, sem)

    @pl.when(image == 0)
    def _():
        copy.start()

    factor = head_size ** (-0.5) * 1.4426950408889634
    key_live = jnp.where(
        lax.broadcasted_iota(jnp.int32, (1, slots), 1) < live_count, 1.0, 0.0
    )
    first_half = lax.broadcasted_iota(jnp.int32, (slots, 2 * head_size), 1) < head_size
    zero = jnp.zeros((slots, 2 * head_size), jnp.bfloat16)
    for at in range(0, width, 2 * head_size):
        columns = slice(at, at + 2 * head_size)
        queries, keys, values = (qkv_ref[part, :, columns] for part in range(3))
        outs = []
        for half in range(2):
            own = jnp.where(first_half, queries, zero) if half == 0 else jnp.where(first_half, zero, queries)
            weights = jnp.exp2(product_along(own, keys) * factor) * key_live
            share = weights * (1.0 / jnp.sum(weights, axis=1, keepdims=True))
            outs.append(product(share.astype(jnp.bfloat16), values))
        attended_ref[0, :, columns] = jnp.where(first_half, outs[0], outs[1]).astype(jnp.bfloat16)

    @pl.when(image == 0)
    def _():
        copy.wait()

    stream = merged_ref[0] + bias_ref[...] + product(attended_ref[0], narrow_ref[:width, :])
    for part in range(hidden_ref.shape[0]):
        stream = stream + product(
            hidden_ref[part], narrow_ref[(part + 1) * width : (part + 2) * width, :]
        )
    stream_ref[0] = stream
    unit, _ = normal_rows(stream)
    live = lax.broadcasted_iota(jnp.int32, (slots, 1), 0) < live_count
    total = jnp.sum(jnp.where(live, unit, 0.0), axis=0, keepdims=True)
    pooled_ref[0] = total * gain_ref[...] / live_count.astype(jnp.float32)


def branch_kernel(
    counts_ref, stream_ref, grad_pooled_ref, gain_ref, slope_ref, narrow_hbm,
    grad_stream_ref, grad_branch_ref, grad_attended_ref, grad_act_ref, sums_ref, narrow_ref, sem,
):
    image = pl.program_id(0)
    live_count = counts_ref[image]
    slots, width = stream_ref.shape[1:]
    copy = pltpu.make_async_copy(narrow_hbm, narrow_ref, sem)

    @pl.when(image == 0)
    def _():
        copy.start()
        sums_ref[...] = jnp.zeros_like(sums_ref)

    unit, rstd = normal_rows(stream_ref[0])
    live = lax.broadcasted_iota(jnp.int32, (slots, 1), 0) < live_count
    above = grad_pooled_ref[0] / live_count.astype(jnp.float32)
    slanted = above * gain_ref[...]
    mean_first = jnp.mean(slanted, axis=-1, keepdims=True)
    mean_second = jnp.mean(slanted * unit, axis=-1, keepdims=True)
    grad_stream = jnp.where(live, rstd * (slanted - mean_first - unit * mean_second), 0.0)
    grad_stream_ref[0] = grad_stream
    grad_branch = grad_stream.astype(jnp.bfloat16)
    grad_branch_ref[0] = grad_branch
    parts = slope_ref.shape[0]
    sums_ref[parts : parts + 1, :] += jnp.sum(grad_stream, axis=0, keepdims=True)
    sums_ref[parts + 1 : parts + 2, :] += above * jnp.sum(
        jnp.where(live, unit, 0.0), axis=0, keepdims=True
    )

    @pl.when(image == 0)
    def _():
        copy.wait()

    grad_attended_ref[0] = product_along(grad_branch, narrow_ref[:width, :]).astype(jnp.bfloat16)
    for part in range(parts):
        grad_act = product_along(
            grad_branch, narrow_ref[(part + 1) * width : (part + 2) * width, :]
        ) * slope_ref[part].astype(jnp.float32)
        grad_act_ref[part] = grad_act.astype(jnp.bfloat16)
        sums_ref[part : part + 1, :] += jnp.sum(grad_act, axis=0, keepdims=True)


def attend_back_kernel(
    counts_ref, qkv_ref, rstd_ref, grad_attended_ref, gain_ref, grad_qkv_ref, sums_ref,
    grad_ref, *, head_size,
):
    image = pl.program_id(0)
    live_count = counts_ref[image]
    slots, width = grad_attended_ref.shape[1:]

    @pl.when(image == 0)
    def _():
        sums_ref[...] = jnp.zeros_like(sums_ref)

    factor = head_size ** (-0.5)
    key_live = lax.broadcasted_iota(jnp.int32, (slots, 1), 0) < live_count
    first_half = lax.broadcasted_iota(jnp.int32, (slots, 2 * head_size), 1) < head_size
    zero = jnp.zeros((slots, 2 * head_size), jnp.bfloat16)
    for at in range(0, width, 2 * head_size):
        columns = slice(at, at + 2 * head_size)
        queries, keys, values = (qkv_ref[part, :, columns] for part in range(3))
        above = grad_attended_ref[0, :, columns]
        grad_queries, grad_keys, grad_values = [], [], []
        for half in range(2):
            pick = lambda both: jnp.where(first_half, both, zero) if half == 0 else jnp.where(first_half, zero, both)
            own_queries, own_above = pick(queries), pick(above)
            weights = jnp.exp2(product_along(keys, own_queries) * (factor * 1.4426950408889634))
            weights = jnp.where(key_live, weights, 0.0)
            share = weights * (1.0 / jnp.sum(weights, axis=0, keepdims=True))
            grad_share = product_along(values, own_above)
            dot_row = jnp.sum(share * grad_share, axis=0, keepdims=True)
            grad_raw = (share * (grad_share - dot_row) * factor).astype(jnp.bfloat16)
            grad_values.append(product(share.astype(jnp.bfloat16), own_above))
            grad_keys.append(product(grad_raw, own_queries))
            grad_queries.append(product_across(grad_raw, keys))
        grad_qkv_ref[2, :, columns] = (grad_values[0] + grad_values[1]).astype(jnp.bfloat16)
        grad_ref[1, :, columns] = grad_keys[0] + grad_keys[1]
        grad_ref[0, :, columns] = jnp.where(first_half, grad_queries[0], grad_queries[1])
    mixer = head_mixer(head_size)
    for part in range(2):
        gain = gain_ref[part]
        above = grad_ref[part]
        unit = qkv_ref[part].astype(jnp.float32) / gain
        sums_ref[part : part + 1, :] += jnp.sum(above * unit, axis=0, keepdims=True)
        slanted = above * gain
        back = slanted - head_mean(slanted, mixer) - unit * head_mean(slanted * unit, mixer)
        grad_qkv_ref[part] = (rstd_ref[part] * back).astype(jnp.bfloat16)


def merge_back_kernel(
    counts_ref, grad_qkv_ref, grad_act_ref, wide_hbm, merged_ref, grad_stream_ref, gain_ref,
    map_ref, row_ref, column_ref, grad_patch_ref, grad_place_ref, sums_ref, wide_ref, sem,
):
    image = pl.program_id(0)
    live_count = counts_ref[image]
    slots, width = merged_ref.shape[1:]
    copy = pltpu.make_async_copy(wide_hbm, wide_ref, sem)

    @pl.when(image == 0)
    def _():
        copy.start()
        sums_ref[...] = jnp.zeros_like(sums_ref)
        grad_place_ref[...] = jnp.zeros_like(grad_place_ref)
        copy.wait()

    grad_normed = jnp.zeros((slots, width), jnp.float32)
    for part in range(3):
        grad_normed = grad_normed + product_along(grad_qkv_ref[part], wide_ref[part])
    for part in range(grad_act_ref.shape[0]):
        grad_normed = grad_normed + product_along(grad_act_ref[part], wide_ref[3 + part])
    unit, rstd = normal_rows(merged_ref[0])
    sums_ref[0:1, :] += jnp.sum(grad_normed * unit, axis=0, keepdims=True)
    slanted = grad_normed * gain_ref[...]
    back = (
        slanted
        - jnp.mean(slanted, axis=-1, keepdims=True)
        - unit * jnp.mean(slanted * unit, axis=-1, keepdims=True)
    )
    grad_merged = grad_stream_ref[0] + rstd * back
    slot = lax.broadcasted_iota(jnp.int32, (slots, slots), 0)
    member = slot == map_ref[0]
    hot = jnp.where(member, 1.0, 0.0).astype(jnp.bfloat16)
    total = jnp.sum(jnp.where(member, row_ref[0], 0.0), axis=1, keepdims=True)
    vacant = lax.broadcasted_iota(jnp.int32, (slots, 1), 0) >= live_count
    total = total + jnp.where(vacant, 1.0, 0.0)
    high, low = split_two(grad_merged / total)
    grad_patches = (product_across(hot, high) + product_across(hot, low)) * column_ref[0]
    grad_patch_ref[0] = grad_patches.astype(jnp.bfloat16)
    grad_place_ref[...] += grad_patches
    sums_ref[1:2, :] += jnp.sum(grad_patches, axis=0, keepdims=True)


def block(shape, index_map):
    return pl.BlockSpec(shape, index_map)


def per_image(rows, width):
    return block((1, rows, width), lambda image, counts: (image, 0, 0))


def whole(*shape):
    return block(shape, lambda *_: (0,) * len(shape))


anywhere = pl.BlockSpec(memory_space=pl.ANY)
roomy = pltpu.CompilerParams(vmem_limit_bytes=60 * 1024 * 1024)


def image_call(kernel, images, in_specs, out_specs, out_shape, scratch=(), name=None):
    return pl.pallas_call(
        kernel,
        grid_spec=pltpu.PrefetchScalarGridSpec(
            num_scalar_prefetch=1,
            grid=(images,),
            in_specs=in_specs,
            out_specs=out_specs,
            scratch_shapes=list(scratch),
        ),
        out_shape=out_shape,
        compiler_params=roomy,
        name=name,
    )


def per_device(
    pixels,
    merge_map,
    merge_weight,
    counts,
    captions,
    pairing,
    embedder,
    positions,
    widener,
    narrower,
    projector,
    scales,
    biases,
    moment_embedder,
    moment_positions,
    moment_widener,
    moment_narrower,
    moment_projector,
    moment_scales,
    moment_biases,
    square_embedder,
    square_positions,
    square_widener,
    square_narrower,
    square_projector,
    square_scales,
    square_biases,
):
    weights = (embedder, positions, widener, narrower, projector, scales, biases)
    shapes = tuple(weight.shape for weight in weights)
    owners = lax.axis_size("fsdp")
    packed = pack_weights(*(weight.astype(jnp.bfloat16) for weight in weights))
    full = lax.all_gather(packed, "fsdp", axis=0)
    embed_full, place_full, wide_blocks, narrow_full, project_full, scale_full, bias_full = (
        unpack_weights(full, shapes)
    )
    place_float = place_full.astype(jnp.float32)
    scale_float = scale_full.astype(jnp.float32)
    bias_float = bias_full.astype(jnp.float32)
    micro_count, images_dev, slot_total, patch_size = pixels.shape
    model_width = embed_full.shape[1]
    hidden_width = narrow_full.shape[0] - model_width
    hidden_blocks = hidden_width // model_width
    head_size = model_width // HEADS
    images_all = pairing.shape[1]
    logit_factor = logit_temper * captions.shape[2] ** (-0.5)
    images = micro_count * images_dev
    slots = padded_rows(slot_total)
    spare = slots - slot_total
    rows = images * slots
    pixel_rows = jnp.pad(
        pixels.reshape(images, slot_total, patch_size), ((0, 0), (0, spare), (0, 0))
    )
    slot_map = jnp.pad(
        merge_map.reshape(images, 1, slot_total), ((0, 0), (0, 0), (0, spare)), constant_values=-1
    )
    row_weight = jnp.pad(merge_weight.reshape(images, 1, slot_total), ((0, 0), (0, 0), (0, spare)))
    column_weight = row_weight.reshape(images, slots, 1)
    live_counts = counts.reshape(images)
    place_bias = jnp.pad(
        place_float + bias_float[hidden_width + model_width :], ((0, spare), (0, 0))
    )
    out_bias = bias_float[hidden_width : hidden_width + model_width].reshape(1, model_width)
    wide_stack = jnp.stack(wide_blocks)
    f32, low = jnp.float32, jnp.bfloat16
    shape = jax.ShapeDtypeStruct
    merged, normed = image_call(
        embed_kernel,
        images,
        [
            per_image(slots, patch_size),
            per_image(1, slots),
            per_image(1, slots),
            per_image(slots, 1),
            whole(patch_size, model_width),
            whole(slots, model_width),
            whole(1, model_width),
        ],
        [per_image(slots, model_width)] * 2,
        [shape((images, slots, model_width), f32), shape((images, slots, model_width), low)],
        name="embed",
    )(
        live_counts, pixel_rows, slot_map, row_weight, column_weight, embed_full, place_bias,
        scale_float[0:1],
    )
    normed_rows = normed.reshape(rows, model_width)
    column_block = lambda index_map: block((1, rows, model_width), index_map)
    qkv, rstd, hidden, slope = pl.pallas_call(
        functools.partial(widen_kernel, chunk=slots, head_size=head_size),
        grid=(3 + hidden_blocks,),
        in_specs=[
            whole(rows, model_width),
            block((1, model_width, model_width), lambda k: (k, 0, 0)),
            block((1, 1, model_width), lambda k: (jnp.minimum(k, 1), 0, 0)),
            block((1, 1, model_width), lambda k: (jnp.maximum(k - 3, 0), 0, 0)),
        ],
        out_specs=[
            column_block(lambda k: (jnp.minimum(k, 2), 0, 0)),
            column_block(lambda k: (jnp.minimum(k, 1), 0, 0)),
            column_block(lambda k: (jnp.maximum(k - 3, 0), 0, 0)),
            column_block(lambda k: (jnp.maximum(k - 3, 0), 0, 0)),
        ],
        out_shape=[
            shape((3, rows, model_width), low),
            shape((2, rows, model_width), f32),
            shape((hidden_blocks, rows, model_width), low),
            shape((hidden_blocks, rows, model_width), low),
        ],
        compiler_params=roomy,
        name="widen",
    )(
        normed_rows, wide_stack, scale_float[2:4].reshape(2, 1, model_width),
        bias_float[:hidden_width].reshape(hidden_blocks, 1, model_width),
    )
    image_columns = lambda parts: block(
        (parts, slots, model_width), lambda image, counts: (0, image, 0)
    )
    narrow_scratch = [
        pltpu.VMEM((hidden_width + model_width, model_width), low), pltpu.SemaphoreType.DMA
    ]
    attended, stream, pooled = image_call(
        functools.partial(attend_kernel, head_size=head_size),
        images,
        [
            image_columns(3),
            image_columns(hidden_blocks),
            per_image(slots, model_width),
            anywhere,
            whole(1, model_width),
            whole(1, model_width),
        ],
        [per_image(slots, model_width), per_image(slots, model_width), per_image(1, model_width)],
        [
            shape((images, slots, model_width), low),
            shape((images, slots, model_width), f32),
            shape((images, 1, model_width), f32),
        ],
        narrow_scratch,
        name="attend",
    )(live_counts, qkv, hidden, merged, narrow_full, out_bias, scale_float[1:2])
    pooled_low = pooled.reshape(images, model_width).astype(low)
    embeds = product(pooled_low, project_full).astype(low)
    embeds = embeds.reshape(micro_count, images_dev, -1)
    logits = jnp.einsum("mie,mje->mij", embeds, captions, preferred_element_type=f32) * logit_factor
    image_ids = jnp.arange(images_all, dtype=jnp.int32)
    first_row = (lax.axis_index("rep") * owners + lax.axis_index("fsdp")) * images_dev
    own_pairs = lax.dynamic_slice_in_dim(pairing, first_row, images_dev, 1)
    target = (own_pairs[:, :, None] == image_ids[None, None, :]).astype(jnp.float32)
    row_top = jnp.max(logits, axis=2, keepdims=True)
    row_logsum = row_top[:, :, 0] + jnp.log(jnp.sum(jnp.exp(logits - row_top), axis=2))
    own_top = jnp.max(logits, axis=1)
    own_total = jnp.sum(jnp.exp(logits - own_top[:, None, :]), axis=1)
    picked = jnp.sum(logits * target, axis=2)
    counts_float = counts.astype(jnp.float32)
    scalars = jnp.concatenate(
        [
            jnp.sum(counts_float * (picked - row_logsum), axis=1),
            jnp.sum(picked, axis=1),
            jnp.sum(counts_float, axis=1),
        ]
    )
    sums = jnp.pad(scalars[None, :], ((0, 0), (0, images_all - scalars.shape[0])))
    column_top, column_total, sums = column_totals(own_top, own_total, sums)
    column_logsum = column_top + jnp.log(column_total)
    row_terms = sums[0, :micro_count]
    picked_sums = sums[0, micro_count : 2 * micro_count]
    weight_totals = sums[0, 2 * micro_count : 3 * micro_count]
    weight_total_all = jnp.sum(weight_totals)
    part_losses = 0.5 * (
        -row_terms / weight_totals - (picked_sums - jnp.sum(column_logsum, axis=1)) / images_all
    )
    objective = jnp.sum(part_losses) / micro_count
    row_soft = jnp.exp(logits - row_logsum[:, :, None])
    column_soft = jnp.exp(logits - column_logsum[:, None, :])
    all_grad_logits = (
        0.5
        / micro_count
        * (
            (counts_float / weight_totals[:, None])[:, :, None] * (row_soft - target)
            + (column_soft - target) / images_all
        )
    )
    grad_product = (all_grad_logits * logit_factor).astype(low)
    grad_embeds = (
        jnp.einsum("mij,mje->mie", grad_product, captions, preferred_element_type=f32)
        .astype(low)
        .reshape(images, -1)
    )
    grad_project = product_across(pooled_low, grad_embeds)
    grad_pooled = product_along(grad_embeds, project_full)
    grad_stream, grad_branch, grad_attended, grad_act, out_sums = image_call(
        branch_kernel,
        images,
        [
            per_image(slots, model_width),
            per_image(1, model_width),
            whole(1, model_width),
            image_columns(hidden_blocks),
            anywhere,
        ],
        [
            per_image(slots, model_width),
            per_image(slots, model_width),
            per_image(slots, model_width),
            image_columns(hidden_blocks),
            whole(8, model_width),
        ],
        [
            shape((images, slots, model_width), f32),
            shape((images, slots, model_width), low),
            shape((images, slots, model_width), low),
            shape((hidden_blocks, rows, model_width), low),
            shape((8, model_width), f32),
        ],
        narrow_scratch,
        name="branch",
    )(
        live_counts, stream, grad_pooled.reshape(images, 1, model_width), scale_float[1:2], slope,
        narrow_full,
    )
    across = lambda left, right: product_across(left, right).astype(low)
    branch_rows = grad_branch.reshape(rows, model_width)
    grad_narrow = jnp.concatenate(
        [across(attended.reshape(rows, model_width), branch_rows)]
        + [across(hidden[k], branch_rows) for k in range(hidden_blocks)],
        axis=0,
    )
    wide_hidden = [across(normed_rows, grad_act[k]) for k in range(hidden_blocks)]
    grad_qkv, head_sums = image_call(
        functools.partial(attend_back_kernel, head_size=head_size),
        images,
        [
            image_columns(3),
            image_columns(2),
            per_image(slots, model_width),
            whole(2, 1, model_width),
        ],
        [image_columns(3), whole(8, model_width)],
        [shape((3, rows, model_width), low), shape((8, model_width), f32)],
        [pltpu.VMEM((2, slots, model_width), f32)],
        name="attend_back",
    )(live_counts, qkv, rstd, grad_attended, scale_float[2:4].reshape(2, 1, model_width))
    wide_parts = [across(normed_rows, grad_qkv[k]) for k in range(3)] + wide_hidden
    grad_patches, grad_place, merge_sums = image_call(
        merge_back_kernel,
        images,
        [
            image_columns(3),
            image_columns(hidden_blocks),
            anywhere,
            per_image(slots, model_width),
            per_image(slots, model_width),
            whole(1, model_width),
            per_image(1, slots),
            per_image(1, slots),
            per_image(slots, 1),
        ],
        [per_image(slots, model_width), whole(slots, model_width), whole(8, model_width)],
        [
            shape((images, slots, model_width), low),
            shape((slots, model_width), f32),
            shape((8, model_width), f32),
        ],
        [pltpu.VMEM((3 + hidden_blocks, model_width, model_width), low), pltpu.SemaphoreType.DMA],
        name="merge_back",
    )(
        live_counts, grad_qkv, grad_act, wide_stack, merged, grad_stream, scale_float[0:1],
        slot_map, row_weight, column_weight,
    )
    grad_embed = across(
        pixel_rows.reshape(rows, patch_size), grad_patches.reshape(rows, model_width)
    )
    grad_place = grad_place[:slot_total]
    grad_scale = jnp.stack([merge_sums[0], out_sums[hidden_blocks + 1], head_sums[0], head_sums[1]])
    grad_bias = jnp.concatenate([out_sums[: hidden_blocks + 1].reshape(-1), merge_sums[1]])
    packed_grads = pack_grads(
        owners, grad_embed, grad_place, wide_parts, grad_narrow, grad_project, grad_scale, grad_bias
    )
    shard = lax.psum_scatter(packed_grads, "fsdp", scatter_dimension=0)
    shard = lax.psum(shard, "rep").astype(jnp.float32)
    total_norm = jnp.sqrt(sum_over(jnp.sum(shard * shard), "fsdp"))
    shards = unpack_grads(shard, shapes)
    factor = clip_bound / jnp.maximum(total_norm, clip_bound)
    moments = (
        moment_embedder,
        moment_positions,
        moment_widener,
        moment_narrower,
        moment_projector,
        moment_scales,
        moment_biases,
    )
    squares = (
        square_embedder,
        square_positions,
        square_widener,
        square_narrower,
        square_projector,
        square_scales,
        square_biases,
    )
    results = [
        adam_step(weights[index], shards[index], moments[index], squares[index], factor)
        for index in range(7)
    ]
    return (
        objective,
        weight_total_all,
        total_norm,
        results[0][0],
        results[1][0],
        results[2][0],
        results[3][0],
        results[4][0],
        results[5][0],
        results[6][0],
        results[0][1],
        results[1][1],
        results[2][1],
        results[3][1],
        results[4][1],
        results[5][1],
        results[6][1],
    )


def solution(mesh):
    return jax.shard_map(
        per_device,
        mesh=mesh,
        in_specs=(
            P(None, ("rep", "fsdp"), None, None),
            P(None, ("rep", "fsdp"), None),
            P(None, ("rep", "fsdp"), None),
            P(None, ("rep", "fsdp")),
            P(),
            P(),
            P("fsdp", None),
            P(None, "fsdp"),
            P("fsdp", None),
            P("fsdp", None),
            P("fsdp", None),
            P(None, "fsdp"),
            P("fsdp"),
            P("fsdp", None),
            P(None, "fsdp"),
            P("fsdp", None),
            P("fsdp", None),
            P("fsdp", None),
            P(None, "fsdp"),
            P("fsdp"),
            P("fsdp", None),
            P(None, "fsdp"),
            P("fsdp", None),
            P("fsdp", None),
            P("fsdp", None),
            P(None, "fsdp"),
            P("fsdp"),
        ),
        out_specs=(
            P(),
            P(),
            P(),
            P("fsdp", None),
            P(None, "fsdp"),
            P("fsdp", None),
            P("fsdp", None),
            P("fsdp", None),
            P(None, "fsdp"),
            P("fsdp"),
            P("fsdp", None),
            P(None, "fsdp"),
            P("fsdp", None),
            P("fsdp", None),
            P("fsdp", None),
            P(None, "fsdp"),
            P("fsdp"),
        ),
        check_vma=False,
    )
```

```python
import functools

import jax
import jax.numpy as jnp
from jax import lax
from jax.experimental import pallas as pl
from jax.experimental.pallas import tpu as pltpu
from jax.sharding import PartitionSpec as P

HEADS = 12


norm_eps = 1e-06
clip_bound = 0.1
beta_first = 0.9
beta_second = 0.999
learn_rate = 0.03
weight_decay = 0.1
adam_eps = 1e-08
step_number = 10
logit_temper = 10.0


def product(left, right):
    return jnp.dot(left, right, preferred_element_type=jnp.float32)


def product_across(left, right):
    return lax.dot_general(
        left, right, (((0,), (0,)), ((), ())), preferred_element_type=jnp.float32
    )


def product_along(left, right):
    return lax.dot_general(
        left, right, (((1,), (1,)), ((), ())), preferred_element_type=jnp.float32
    )


def adam_step(weight, gradient, moment, square, factor):
    clipped = gradient * factor
    moment_new = beta_first * moment + (1.0 - beta_first) * clipped
    square_new = beta_second * square + (1.0 - beta_second) * clipped * clipped
    mean_hat = moment_new / (1.0 - beta_first**step_number)
    square_hat = square_new / (1.0 - beta_second**step_number)
    change = -learn_rate * (mean_hat / (jnp.sqrt(square_hat) + adam_eps) + weight_decay * weight)
    return (change, clipped)


def bit_swap(size, bit):
    return [(index, index ^ bit) for index in range(size)]


def ordered_pair(own, other, axis, bit):
    low_side = (lax.axis_index(axis) & bit) == 0
    return jnp.where(low_side, own, other), jnp.where(low_side, other, own)


def exchange_steps():
    steps = []
    for axis in ("fsdp", "rep"):
        size = lax.axis_size(axis)
        bit = 1
        while bit < size:
            steps.append((axis, size, bit))
            bit *= 2
    return steps


def column_totals(top, total, sums):
    micro_count = top.shape[0]
    for axis, size, bit in exchange_steps():
        packed = jnp.concatenate([top, total, sums], axis=0)
        other = lax.ppermute(packed, axis, bit_swap(size, bit))
        first, second = ordered_pair(packed, other, axis, bit)
        top_a, top_b = first[:micro_count], second[:micro_count]
        top = jnp.maximum(top_a, top_b)
        total = first[micro_count : 2 * micro_count] * jnp.exp(top_a - top) + second[
            micro_count : 2 * micro_count
        ] * jnp.exp(top_b - top)
        sums = first[2 * micro_count :] + second[2 * micro_count :]
    return top, total, sums


def sum_over(value, axis):
    size = lax.axis_size(axis)
    bit = 1
    while bit < size:
        value = value + lax.ppermute(value, axis, bit_swap(size, bit))
        bit *= 2
    return value


def pack_weights(embedder, positions, widener, narrower, projector, scales, biases):
    model_width = embedder.shape[1]
    blocks = widener.shape[1] // model_width
    rows = [embedder]
    rows += [widener[:, k * model_width : (k + 1) * model_width] for k in range(blocks)]
    rows += [narrower, projector]
    small = jnp.concatenate([positions.reshape(-1), scales.reshape(-1), biases.reshape(-1)])
    small_rows = -(-small.shape[0] // (16 * model_width)) * 16
    small = jnp.pad(small, (0, small_rows * model_width - small.shape[0]))
    rows.append(small.reshape(small_rows, model_width))
    return jnp.concatenate(rows, axis=0)


def unpack_weights(full, shapes):
    owners, _, width = full.shape
    (e_rows, _), (slots, p_cols), (w_rows, w_cols), (n_rows, _), (j_rows, _), (s_rows, s_cols), (
        b_len,
    ) = shapes
    at = 0
    embed = full[:, at : at + e_rows].reshape(owners * e_rows, width)
    at += e_rows
    wide = []
    for _ in range(w_cols // width):
        wide.append(full[:, at : at + w_rows].reshape(owners * w_rows, width))
        at += w_rows
    narrow = full[:, at : at + n_rows].reshape(owners * n_rows, width)
    at += n_rows
    project = full[:, at : at + j_rows].reshape(owners * j_rows, width)
    at += j_rows
    small = full[:, at:].reshape(owners, -1)
    place = small[:, : slots * p_cols].reshape(owners, slots, p_cols)
    place = jnp.swapaxes(place, 0, 1).reshape(slots, owners * p_cols)
    at = slots * p_cols
    scale = small[:, at : at + s_rows * s_cols].reshape(owners, s_rows, s_cols)
    scale = jnp.swapaxes(scale, 0, 1).reshape(s_rows, owners * s_cols)
    at += s_rows * s_cols
    bias = small[:, at : at + b_len].reshape(owners * b_len)
    return embed, place, wide, narrow, project, scale, bias


def padded_rows(rows):
    return -(-rows // 16) * 16


def split_two(values):
    high = values.astype(jnp.bfloat16)
    return high, (values - high.astype(jnp.float32)).astype(jnp.bfloat16)


def normal_rows(values):
    center = values - jnp.mean(values, axis=-1, keepdims=True)
    rstd = lax.rsqrt(jnp.mean(center * center, axis=-1, keepdims=True) + norm_eps)
    return center * rstd, rstd


def head_mixer(head_size):
    row = lax.broadcasted_iota(jnp.int32, (256, 256), 0) // head_size
    column = lax.broadcasted_iota(jnp.int32, (256, 256), 1) // head_size
    return jnp.where(row == column, 1.0 / head_size, 0.0).astype(jnp.bfloat16)


def head_mean(values, mixer):
    parts = []
    for at in range(0, values.shape[1], 256):
        high, low = split_two(values[:, at : at + 256])
        parts.append(product(high, mixer) + product(low, mixer))
    return jnp.concatenate(parts, axis=1)


def embed_kernel(
    counts_ref, pixel_ref, map_ref, row_ref, column_ref, embed_ref, place_ref, gain_ref,
    merged_ref, normed_ref,
):
    live_count = counts_ref[pl.program_id(0)]
    slots = merged_ref.shape[1]
    patches = product(pixel_ref[0], embed_ref[...]) + place_ref[...]
    high, low = split_two(patches * column_ref[0])
    slot = lax.broadcasted_iota(jnp.int32, (slots, slots), 0)
    member = slot == map_ref[0]
    hot = jnp.where(member, 1.0, 0.0).astype(jnp.bfloat16)
    total = jnp.sum(jnp.where(member, row_ref[0], 0.0), axis=1, keepdims=True)
    vacant = lax.broadcasted_iota(jnp.int32, (slots, 1), 0) >= live_count
    total = total + jnp.where(vacant, 1.0, 0.0)
    merged = (product(hot, high) + product(hot, low)) / total
    merged_ref[0] = merged
    unit, _ = normal_rows(merged)
    normed_ref[0] = (unit * gain_ref[...]).astype(jnp.bfloat16)


def gelu_pair(values):
    size = jnp.abs(values)
    turn = 1.0 / (1.0 + (0.3275911 * 0.7071067811865476) * size)
    bell = jnp.exp(-0.5 * values * values)
    poly = turn * (
        0.5 * 0.254829592
        + turn
        * (
            0.5 * -0.284496736
            + turn
            * (0.5 * 1.421413741 + turn * (0.5 * -1.453152027 + turn * (0.5 * 1.061405429)))
        )
    )
    tail = poly * bell
    share = jnp.where(values >= 0, 1.0 - tail, tail)
    return values * share, share + values * (bell * 0.3989422804014327)


def widen_kernel(
    normed_ref, wide_ref, gain_ref, bias_ref, qkv_ref, rstd_ref, hidden_ref, slope_ref, *, chunk,
    head_size,
):
    step = pl.program_id(0)
    chunks = normed_ref.shape[0] // chunk

    def rows_of(index):
        return pl.ds(pl.multiple_of(index * chunk, chunk), chunk)

    @pl.when(step < 2)
    def _():
        mixer = head_mixer(head_size)
        gain = gain_ref[0]

        @pl.loop(0, chunks, unroll=True)
        def _(index):
            rows = rows_of(index)
            values = product(normed_ref[rows, :], wide_ref[0])
            center = values - head_mean(values, mixer)
            rstd = lax.rsqrt(head_mean(center * center, mixer) + norm_eps)
            rstd_ref[0, rows, :] = rstd
            qkv_ref[0, rows, :] = (center * rstd * gain).astype(jnp.bfloat16)

    @pl.when(step == 2)
    def _():
        @pl.loop(0, chunks, unroll=True)
        def _(index):
            rows = rows_of(index)
            qkv_ref[0, rows, :] = product(normed_ref[rows, :], wide_ref[0]).astype(jnp.bfloat16)

    @pl.when(step > 2)
    def _():
        @pl.loop(0, chunks, unroll=True)
        def _(index):
            rows = rows_of(index)
            values = product(normed_ref[rows, :], wide_ref[0]) + bias_ref[0]
            hidden, slope = gelu_pair(values)
            hidden_ref[0, rows, :] = hidden.astype(jnp.bfloat16)
            slope_ref[0, rows, :] = slope.astype(jnp.bfloat16)


def attend_kernel(
    counts_ref, qkv_ref, hidden_ref, merged_ref, narrow_hbm, bias_ref, gain_ref,
    attended_ref, stream_ref, pooled_ref, narrow_ref, sem, *, head_size,
):
    image = pl.program_id(0)
    live_count = counts_ref[image]
    slots, width = merged_ref.shape[1:]
    copy = pltpu.make_async_copy(narrow_hbm, narrow_ref, sem)

    @pl.when(image == 0)
    def _():
        copy.start()

    factor = head_size ** (-0.5) * 1.4426950408889634
    key_live = jnp.where(
        lax.broadcasted_iota(jnp.int32, (1, slots), 1) < live_count, 1.0, 0.0
    )
    first_half = lax.broadcasted_iota(jnp.int32, (slots, 2 * head_size), 1) < head_size
    zero = jnp.zeros((slots, 2 * head_size), jnp.bfloat16)
    for at in range(0, width, 2 * head_size):
        columns = slice(at, at + 2 * head_size)
        queries, keys, values = (qkv_ref[part, :, columns] for part in range(3))
        outs = []
        for half in range(2):
            own = jnp.where(first_half, queries, zero) if half == 0 else jnp.where(first_half, zero, queries)
            weights = jnp.exp2(product_along(own, keys) * factor) * key_live
            share = weights * (1.0 / jnp.sum(weights, axis=1, keepdims=True))
            outs.append(product(share.astype(jnp.bfloat16), values))
        attended_ref[0, :, columns] = jnp.where(first_half, outs[0], outs[1]).astype(jnp.bfloat16)

    @pl.when(image == 0)
    def _():
        copy.wait()

    stream = merged_ref[0] + bias_ref[...] + product(attended_ref[0], narrow_ref[:width, :])
    for part in range(hidden_ref.shape[0]):
        stream = stream + product(
            hidden_ref[part], narrow_ref[(part + 1) * width : (part + 2) * width, :]
        )
    stream_ref[0] = stream
    unit, _ = normal_rows(stream)
    live = lax.broadcasted_iota(jnp.int32, (slots, 1), 0) < live_count
    total = jnp.sum(jnp.where(live, unit, 0.0), axis=0, keepdims=True)
    pooled_ref[0] = total * gain_ref[...] / live_count.astype(jnp.float32)


def branch_kernel(
    counts_ref, stream_ref, grad_pooled_ref, gain_ref, slope_ref, narrow_hbm,
    grad_stream_ref, grad_branch_ref, grad_attended_ref, grad_act_ref, sums_ref, narrow_ref, sem,
):
    image = pl.program_id(0)
    live_count = counts_ref[image]
    slots, width = stream_ref.shape[1:]
    copy = pltpu.make_async_copy(narrow_hbm, narrow_ref, sem)

    @pl.when(image == 0)
    def _():
        copy.start()
        sums_ref[...] = jnp.zeros_like(sums_ref)

    unit, rstd = normal_rows(stream_ref[0])
    live = lax.broadcasted_iota(jnp.int32, (slots, 1), 0) < live_count
    above = grad_pooled_ref[0] / live_count.astype(jnp.float32)
    slanted = above * gain_ref[...]
    mean_first = jnp.mean(slanted, axis=-1, keepdims=True)
    mean_second = jnp.mean(slanted * unit, axis=-1, keepdims=True)
    grad_stream = jnp.where(live, rstd * (slanted - mean_first - unit * mean_second), 0.0)
    grad_stream_ref[0] = grad_stream
    grad_branch = grad_stream.astype(jnp.bfloat16)
    grad_branch_ref[0] = grad_branch
    parts = slope_ref.shape[0]
    sums_ref[parts : parts + 1, :] += jnp.sum(grad_stream, axis=0, keepdims=True)
    sums_ref[parts + 1 : parts + 2, :] += above * jnp.sum(
        jnp.where(live, unit, 0.0), axis=0, keepdims=True
    )

    @pl.when(image == 0)
    def _():
        copy.wait()

    grad_attended_ref[0] = product_along(grad_branch, narrow_ref[:width, :]).astype(jnp.bfloat16)
    for part in range(parts):
        grad_act = product_along(
            grad_branch, narrow_ref[(part + 1) * width : (part + 2) * width, :]
        ) * slope_ref[part].astype(jnp.float32)
        grad_act_ref[part] = grad_act.astype(jnp.bfloat16)
        sums_ref[part : part + 1, :] += jnp.sum(grad_act, axis=0, keepdims=True)


def attend_back_kernel(
    counts_ref, qkv_ref, rstd_ref, grad_attended_ref, gain_ref, *refs, base, head_size
):
    grad_qkv_ref, sums_ref, grad_ref = refs[-3:]
    image = pl.program_id(0)
    live_count = counts_ref[base + image]
    slots, width = grad_attended_ref.shape[1:]

    @pl.when(image == 0)
    def _():
        sums_ref[...] = jnp.zeros_like(sums_ref)

    factor = head_size ** (-0.5)
    key_live = lax.broadcasted_iota(jnp.int32, (slots, 1), 0) < live_count
    first_half = lax.broadcasted_iota(jnp.int32, (slots, 2 * head_size), 1) < head_size
    zero = jnp.zeros((slots, 2 * head_size), jnp.bfloat16)
    for at in range(0, width, 2 * head_size):
        columns = slice(at, at + 2 * head_size)
        queries, keys, values = (qkv_ref[part, :, columns] for part in range(3))
        above = grad_attended_ref[0, :, columns]
        grad_queries, grad_keys, grad_values = [], [], []
        for half in range(2):
            pick = lambda both: jnp.where(first_half, both, zero) if half == 0 else jnp.where(first_half, zero, both)
            own_queries, own_above = pick(queries), pick(above)
            weights = jnp.exp2(product_along(keys, own_queries) * (factor * 1.4426950408889634))
            weights = jnp.where(key_live, weights, 0.0)
            share = weights * (1.0 / jnp.sum(weights, axis=0, keepdims=True))
            grad_share = product_along(values, own_above)
            dot_row = jnp.sum(share * grad_share, axis=0, keepdims=True)
            grad_raw = (share * (grad_share - dot_row) * factor).astype(jnp.bfloat16)
            grad_values.append(product(share.astype(jnp.bfloat16), own_above))
            grad_keys.append(product(grad_raw, own_queries))
            grad_queries.append(product_across(grad_raw, keys))
        grad_qkv_ref[2, :, columns] = (grad_values[0] + grad_values[1]).astype(jnp.bfloat16)
        grad_ref[1, :, columns] = grad_keys[0] + grad_keys[1]
        grad_ref[0, :, columns] = jnp.where(first_half, grad_queries[0], grad_queries[1])
    mixer = head_mixer(head_size)
    for part in range(2):
        gain = gain_ref[part]
        above = grad_ref[part]
        unit = qkv_ref[part].astype(jnp.float32) / gain
        sums_ref[part : part + 1, :] += jnp.sum(above * unit, axis=0, keepdims=True)
        slanted = above * gain
        back = slanted - head_mean(slanted, mixer) - unit * head_mean(slanted * unit, mixer)
        grad_qkv_ref[part] = (rstd_ref[part] * back).astype(jnp.bfloat16)


def merge_back_kernel(
    counts_ref, grad_qkv_ref, grad_act_ref, wide_hbm, merged_ref, grad_stream_ref, gain_ref,
    map_ref, row_ref, column_ref, *refs, base,
):
    grad_patch_ref, grad_place_ref, sums_ref, wide_ref, sem = refs[-5:]
    image = pl.program_id(0)
    live_count = counts_ref[base + image]
    slots, width = merged_ref.shape[1:]
    blocks = wide_ref.shape[0]
    copies = [
        pltpu.make_async_copy(wide_hbm.at[part], wide_ref.at[part], sem.at[part])
        for part in range(blocks)
    ]

    @pl.when(image == 0)
    def _():
        for copy in copies:
            copy.start()
        sums_ref[...] = jnp.zeros_like(sums_ref)
        grad_place_ref[...] = jnp.zeros_like(grad_place_ref)

    grad_normed = jnp.zeros((slots, width), jnp.float32)
    for part in range(blocks):
        pl.when(image == 0)(copies[part].wait)
        grads = grad_qkv_ref[part] if part < 3 else grad_act_ref[part - 3]
        grad_normed = grad_normed + product_along(grads, wide_ref[part])
    unit, rstd = normal_rows(merged_ref[0])
    sums_ref[0:1, :] += jnp.sum(grad_normed * unit, axis=0, keepdims=True)
    slanted = grad_normed * gain_ref[...]
    back = (
        slanted
        - jnp.mean(slanted, axis=-1, keepdims=True)
        - unit * jnp.mean(slanted * unit, axis=-1, keepdims=True)
    )
    grad_merged = grad_stream_ref[0] + rstd * back
    slot = lax.broadcasted_iota(jnp.int32, (slots, slots), 0)
    member = slot == map_ref[0]
    hot = jnp.where(member, 1.0, 0.0).astype(jnp.bfloat16)
    total = jnp.sum(jnp.where(member, row_ref[0], 0.0), axis=1, keepdims=True)
    vacant = lax.broadcasted_iota(jnp.int32, (slots, 1), 0) >= live_count
    total = total + jnp.where(vacant, 1.0, 0.0)
    high, low = split_two(grad_merged / total)
    grad_patches = (product_across(hot, high) + product_across(hot, low)) * column_ref[0]
    grad_patch_ref[0] = grad_patches.astype(jnp.bfloat16)
    grad_place_ref[...] += grad_patches
    sums_ref[1:2, :] += jnp.sum(grad_patches, axis=0, keepdims=True)


def block(shape, index_map):
    return pl.BlockSpec(shape, index_map)


def per_image(rows, width):
    return block((1, rows, width), lambda image, counts: (image, 0, 0))


def whole(*shape):
    return block(shape, lambda *_: (0,) * len(shape))


anywhere = pl.BlockSpec(memory_space=pl.ANY)
roomy = pltpu.CompilerParams(vmem_limit_bytes=60 * 1024 * 1024)


long = pl.CostEstimate(flops=60_000_000_000, bytes_accessed=1000, transcendentals=0)


def image_call(kernel, images, in_specs, out_specs, out_shape, scratch=(), name=None):
    return pl.pallas_call(
        kernel,
        grid_spec=pltpu.PrefetchScalarGridSpec(
            num_scalar_prefetch=1,
            grid=(images,),
            in_specs=in_specs,
            out_specs=out_specs,
            scratch_shapes=list(scratch),
        ),
        out_shape=out_shape,
        compiler_params=roomy,
        cost_estimate=long,
        name=name,
    )


def picked(terms, axis, index):
    return [lax.dynamic_index_in_dim(term, index, axis, keepdims=False) for term in terms]


def added(terms):
    total = terms[0].astype(jnp.float32)
    for term in terms[1:]:
        total = total + term.astype(jnp.float32)
    return total


def behind(terms, after):
    if after is None:
        return terms
    return lax.optimization_barrier((terms, after))[0]


def traded(terms, axis, index, count, mesh_axis, stride):
    size = lax.axis_size(mesh_axis)
    sends = [
        added(picked(terms, axis, index ^ turn)).astype(jnp.bfloat16) for turn in range(1, count)
    ]
    after = yield sends
    kept = picked(terms, axis, index)
    for turn, send in enumerate(sends, 1):
        kept.append(lax.ppermute(send, mesh_axis, bit_swap(size, turn * stride)))
    return behind(kept, after)


def core_terms(mine, other):
    chips, rows, width = mine.shape
    after = yield [other]
    got = lax.ppermute(other, "fsdp", bit_swap(lax.axis_size("fsdp"), 1))
    return [term.reshape(chips // 2, 2, rows, width) for term in behind([mine, got], after)]


def rep_swap(own):
    return lax.ppermute(own, "rep", bit_swap(2, 1))


def places():
    place = lax.axis_index("fsdp")
    return place // 4, (place // 2) % 2


def reduce_rows_first(mine, other):
    high, middle = places()
    reps = lax.axis_size("rep")
    count = mine.shape[0] // 2
    terms = yield from core_terms(mine, other)
    terms = [
        term.reshape(count, 2, reps, term.shape[2] // reps, term.shape[3]) for term in terms
    ]
    terms = yield from traded(terms, 2, lax.axis_index("rep"), reps, "rep", 1)
    terms = yield from traded(terms, 1, middle, 2, "fsdp", 2)
    terms = yield from traded(terms, 0, high, count, "fsdp", 4)
    own = added(terms).astype(jnp.bfloat16)
    yield [own]
    if reps == 2:
        first, second = ordered_pair(own, rep_swap(own), "rep", 1)
        return jnp.concatenate([first, second], axis=0)
    return lax.all_gather(own, "rep", axis=0, tiled=True)


def reduce_rows_last(mine, other):
    high, middle = places()
    count = mine.shape[0] // 2
    terms = yield from core_terms(mine, other)
    terms = yield from traded(terms, 1, middle, 2, "fsdp", 2)
    terms = yield from traded(terms, 0, high, count, "fsdp", 4)
    own = added(terms).astype(jnp.bfloat16)
    yield [own]
    if lax.axis_size("rep") == 2:
        return added([own, rep_swap(own)]).astype(jnp.bfloat16)
    return lax.psum(own, "rep")


class Flow:
    def __init__(self, steps):
        self.steps, self.result = steps, None

    def go(self, after=None):
        try:
            return self.steps.send(after)
        except StopIteration as end:
            self.result = end.value
            return []

    def finish(self):
        while self.result is None:
            self.go()
        return self.result


def split_cores(result, core, mine_ref, other_ref):
    chips, rows = mine_ref.shape[:2]
    pairs = result.astype(jnp.bfloat16).reshape(chips, 2, rows, result.shape[1])
    first, second = pairs[:, 0], pairs[:, 1]
    mine_ref[...] = jnp.where(core == 0, first, second)
    other_ref[...] = jnp.where(core == 0, second, first)


def narrow_grad_kernel(
    core_ref, attended_ref, hidden_ref, branch_ref, mine_hbm, other_hbm, total_ref, sem
):
    step = pl.program_id(0)
    width = branch_ref.shape[1]
    chips, rows = mine_hbm.shape[:2]

    @pl.when(step == 0)
    def _():
        total_ref[:width, :] = product_across(attended_ref[...], branch_ref[...]).astype(
            jnp.bfloat16
        )

    @pl.when(step > 0)
    def _():
        at = pl.multiple_of(step * width, width)
        total_ref[pl.ds(at, width), :] = product_across(hidden_ref[0], branch_ref[...]).astype(
            jnp.bfloat16
        )

    @pl.when(step == pl.num_programs(0) - 1)
    def _():
        core = core_ref[0]
        copies = []
        for chip in range(chips):
            for side, out in enumerate((mine_hbm, other_hbm)):
                owner = 2 * chip + (core ^ side)
                source = total_ref.at[pl.ds(pl.multiple_of(owner * rows, rows), rows), :]
                copies.append(
                    pltpu.make_async_copy(source, out.at[chip], sem.at[2 * chip + side])
                )
        for copy in copies:
            copy.start()
        for copy in copies:
            copy.wait()


def wide_grad_kernel(core_ref, normed_ref, *refs):
    *grad_refs, mine_ref, other_ref = refs
    total = None
    for part, grad_ref in enumerate(grad_refs):
        rows = grad_ref.shape[1]
        term = product_across(normed_ref[part * rows : (part + 1) * rows, :], grad_ref[0])
        total = term if total is None else total + term
    split_cores(total, core_ref[0], mine_ref, other_ref)


def wide_project_grad_kernel(
    core_ref, normed_ref, grad_ref, pooled_ref, embeds_ref, mine_ref, other_ref
):
    last = pl.program_id(0) == pl.num_programs(0) - 1

    @pl.when(jnp.logical_not(last))
    def _():
        wide_grad_kernel(core_ref, normed_ref, grad_ref, mine_ref, other_ref)

    @pl.when(last)
    def _():
        split_cores(
            product_across(pooled_ref[...], embeds_ref[...]), core_ref[0], mine_ref, other_ref
        )


def embed_grad_kernel(core_ref, pixel_ref, *refs):
    *grad_refs, extra_ref, mine_ref, other_ref = refs
    parts = len(grad_refs) // 2
    total, place = None, None
    for part in range(parts):
        rows = grad_refs[part].shape[0]
        term = product_across(pixel_ref[part * rows : (part + 1) * rows, :], grad_refs[part][...])
        total = term if total is None else total + term
        own = grad_refs[parts + part][...]
        place = own if place is None else place + own
    width, wide_rows = total.shape[1], mine_ref.shape[1] - extra_ref.shape[1]
    beside = mine_ref.shape[2] - width
    spare = jnp.zeros((beside - place.shape[0], width), jnp.float32)
    place = jnp.concatenate([place, spare], axis=0).T
    core = core_ref[0]
    top = jnp.concatenate([total, place], axis=1).astype(jnp.bfloat16)
    chips = mine_ref.shape[0]
    pairs = top.reshape(chips, 2, wide_rows, width + beside)
    mine_ref[:, :wide_rows, :] = jnp.where(core == 0, pairs[:, 0], pairs[:, 1])
    other_ref[:, :wide_rows, :] = jnp.where(core == 0, pairs[:, 1], pairs[:, 0])
    extra = extra_ref[...].reshape(chips, 2, extra_ref.shape[1], width + beside)
    mine_ref[:, wide_rows:, :] = jnp.where(core == 0, extra[:, 0], extra[:, 1])
    other_ref[:, wide_rows:, :] = jnp.where(core == 0, extra[:, 1], extra[:, 0])


def square_kernel(*refs):
    *shard_refs, total_ref = refs
    total = jnp.zeros((1, 1), jnp.float32)
    for shard_ref in shard_refs:
        values = shard_ref[...].astype(jnp.float32)
        columns = jnp.sum(values * values, axis=0, keepdims=True)
        total = total + jnp.sum(columns, axis=1, keepdims=True)
    total_ref[...] = jnp.broadcast_to(total, total_ref.shape)


def update_kernel(
    total_ref, narrow_ref, hidden_ref, qkv_ref, embed_ref, *refs, wide_rows
):
    weights, moments, squares = refs[:7], refs[7:14], refs[14:21]
    changes, clips = refs[21:28], refs[28:35]
    factor = clip_bound / jnp.maximum(jnp.sqrt(total_ref[:1, :1]), clip_bound)
    width = narrow_ref.shape[1]

    def update(index, rows, columns, gradient):
        at = (slice(*rows), slice(*columns))
        change, clipped = adam_step(
            weights[index][at],
            gradient.astype(jnp.float32),
            moments[index][at],
            squares[index][at],
            factor,
        )
        changes[index][at] = change
        clips[index][at] = clipped

    everything = (None,)
    update(0, everything, everything, embed_ref[:wide_rows, :width])
    blocks = weights[2].shape[1] // width
    for k in range(blocks):
        source, at = (qkv_ref, k) if k < 3 else (hidden_ref, k - 3)
        update(
            2,
            everything,
            (k * width, (k + 1) * width),
            source[at * wide_rows : (at + 1) * wide_rows, :],
        )
    update(3, everything, everything, narrow_ref[...])
    update(4, everything, everything, hidden_ref[(blocks - 3) * wide_rows :, :])
    beside = embed_ref[:wide_rows, width:].astype(jnp.float32).T
    update(1, everything, everything, beside[: weights[1].shape[0], :])
    scale_rows, scale_columns = weights[5].shape
    extra = embed_ref[wide_rows:, :].astype(jnp.float32)
    update(5, everything, everything, extra[1 : 1 + scale_rows, :scale_columns])
    update(6, everything, everything, extra[:1, : weights[6].shape[1]])


def per_device(
    pixels,
    merge_map,
    merge_weight,
    counts,
    captions,
    pairing,
    embedder,
    positions,
    widener,
    narrower,
    projector,
    scales,
    biases,
    moment_embedder,
    moment_positions,
    moment_widener,
    moment_narrower,
    moment_projector,
    moment_scales,
    moment_biases,
    square_embedder,
    square_positions,
    square_widener,
    square_narrower,
    square_projector,
    square_scales,
    square_biases,
):
    weights = (embedder, positions, widener, narrower, projector, scales, biases)
    shapes = tuple(weight.shape for weight in weights)
    owners = lax.axis_size("fsdp")
    packed = pack_weights(*(weight.astype(jnp.bfloat16) for weight in weights))
    full = lax.all_gather(packed, "fsdp", axis=0)
    embed_full, place_full, wide_blocks, narrow_full, project_full, scale_full, bias_full = (
        unpack_weights(full, shapes)
    )
    place_float = place_full.astype(jnp.float32)
    scale_float = scale_full.astype(jnp.float32)
    bias_float = bias_full.astype(jnp.float32)
    micro_count, images_dev, slot_total, patch_size = pixels.shape
    model_width = embed_full.shape[1]
    hidden_width = narrow_full.shape[0] - model_width
    hidden_blocks = hidden_width // model_width
    head_size = model_width // HEADS
    images_all = pairing.shape[1]
    logit_factor = logit_temper * captions.shape[2] ** (-0.5)
    images = micro_count * images_dev
    slots = padded_rows(slot_total)
    spare = slots - slot_total
    rows = images * slots
    pixel_rows = jnp.pad(
        pixels.reshape(images, slot_total, patch_size), ((0, 0), (0, spare), (0, 0))
    )
    slot_map = jnp.pad(
        merge_map.reshape(images, 1, slot_total), ((0, 0), (0, 0), (0, spare)), constant_values=-1
    )
    row_weight = jnp.pad(merge_weight.reshape(images, 1, slot_total), ((0, 0), (0, 0), (0, spare)))
    column_weight = row_weight.reshape(images, slots, 1)
    live_counts = counts.reshape(images)
    place_bias = jnp.pad(
        place_float + bias_float[hidden_width + model_width :], ((0, spare), (0, 0))
    )
    out_bias = bias_float[hidden_width : hidden_width + model_width].reshape(1, model_width)
    wide_stack = jnp.stack(wide_blocks)
    f32, low = jnp.float32, jnp.bfloat16
    shape = jax.ShapeDtypeStruct
    merged, normed = image_call(
        embed_kernel,
        images,
        [
            per_image(slots, patch_size),
            per_image(1, slots),
            per_image(1, slots),
            per_image(slots, 1),
            whole(patch_size, model_width),
            whole(slots, model_width),
            whole(1, model_width),
        ],
        [per_image(slots, model_width)] * 2,
        [shape((images, slots, model_width), f32), shape((images, slots, model_width), low)],
        name="embed",
    )(
        live_counts, pixel_rows, slot_map, row_weight, column_weight, embed_full, place_bias,
        scale_float[0:1],
    )
    normed_rows = normed.reshape(rows, model_width)
    column_block = lambda index_map: block((1, rows, model_width), index_map)
    qkv, rstd, hidden, slope = pl.pallas_call(
        functools.partial(widen_kernel, chunk=slots, head_size=head_size),
        grid=(3 + hidden_blocks,),
        in_specs=[
            whole(rows, model_width),
            block((1, model_width, model_width), lambda k: (k, 0, 0)),
            block((1, 1, model_width), lambda k: (jnp.minimum(k, 1), 0, 0)),
            block((1, 1, model_width), lambda k: (jnp.maximum(k - 3, 0), 0, 0)),
        ],
        out_specs=[
            column_block(lambda k: (jnp.minimum(k, 2), 0, 0)),
            column_block(lambda k: (jnp.minimum(k, 1), 0, 0)),
            column_block(lambda k: (jnp.maximum(k - 3, 0), 0, 0)),
            column_block(lambda k: (jnp.maximum(k - 3, 0), 0, 0)),
        ],
        out_shape=[
            shape((3, rows, model_width), low),
            shape((2, rows, model_width), f32),
            shape((hidden_blocks, rows, model_width), low),
            shape((hidden_blocks, rows, model_width), low),
        ],
        compiler_params=roomy,
        name="widen",
    )(
        normed_rows, wide_stack, scale_float[2:4].reshape(2, 1, model_width),
        bias_float[:hidden_width].reshape(hidden_blocks, 1, model_width),
    )
    image_columns = lambda parts: block(
        (parts, slots, model_width), lambda image, counts: (0, image, 0)
    )
    narrow_scratch = [
        pltpu.VMEM((hidden_width + model_width, model_width), low), pltpu.SemaphoreType.DMA
    ]
    attended, stream, pooled = image_call(
        functools.partial(attend_kernel, head_size=head_size),
        images,
        [
            image_columns(3),
            image_columns(hidden_blocks),
            per_image(slots, model_width),
            anywhere,
            whole(1, model_width),
            whole(1, model_width),
        ],
        [per_image(slots, model_width), per_image(slots, model_width), per_image(1, model_width)],
        [
            shape((images, slots, model_width), low),
            shape((images, slots, model_width), f32),
            shape((images, 1, model_width), f32),
        ],
        narrow_scratch,
        name="attend",
    )(live_counts, qkv, hidden, merged, narrow_full, out_bias, scale_float[1:2])
    pooled_low = pooled.reshape(images, model_width).astype(low)
    embeds = product(pooled_low, project_full).astype(low)
    embeds = embeds.reshape(micro_count, images_dev, -1)
    logits = jnp.einsum("mie,mje->mij", embeds, captions, preferred_element_type=f32) * logit_factor
    image_ids = jnp.arange(images_all, dtype=jnp.int32)
    first_row = (lax.axis_index("rep") * owners + lax.axis_index("fsdp")) * images_dev
    own_pairs = lax.dynamic_slice_in_dim(pairing, first_row, images_dev, 1)
    target = (own_pairs[:, :, None] == image_ids[None, None, :]).astype(jnp.float32)
    row_top = jnp.max(logits, axis=2, keepdims=True)
    row_logsum = row_top[:, :, 0] + jnp.log(jnp.sum(jnp.exp(logits - row_top), axis=2))
    own_top = jnp.max(logits, axis=1)
    own_total = jnp.sum(jnp.exp(logits - own_top[:, None, :]), axis=1)
    picked = jnp.sum(logits * target, axis=2)
    counts_float = counts.astype(jnp.float32)
    scalars = jnp.concatenate(
        [
            jnp.sum(counts_float * (picked - row_logsum), axis=1),
            jnp.sum(picked, axis=1),
            jnp.sum(counts_float, axis=1),
        ]
    )
    sums = jnp.pad(scalars[None, :], ((0, 0), (0, images_all - scalars.shape[0])))
    column_top, column_total, sums = column_totals(own_top, own_total, sums)
    column_logsum = column_top + jnp.log(column_total)
    row_terms = sums[0, :micro_count]
    picked_sums = sums[0, micro_count : 2 * micro_count]
    weight_totals = sums[0, 2 * micro_count : 3 * micro_count]
    weight_total_all = jnp.sum(weight_totals)
    part_losses = 0.5 * (
        -row_terms / weight_totals - (picked_sums - jnp.sum(column_logsum, axis=1)) / images_all
    )
    objective = jnp.sum(part_losses) / micro_count
    row_soft = jnp.exp(logits - row_logsum[:, :, None])
    column_soft = jnp.exp(logits - column_logsum[:, None, :])
    all_grad_logits = (
        0.5
        / micro_count
        * (
            (counts_float / weight_totals[:, None])[:, :, None] * (row_soft - target)
            + (column_soft - target) / images_all
        )
    )
    grad_product = (all_grad_logits * logit_factor).astype(low)
    grad_embeds = (
        jnp.einsum("mij,mje->mie", grad_product, captions, preferred_element_type=f32)
        .astype(low)
        .reshape(images, -1)
    )
    grad_pooled = product_along(grad_embeds, project_full)
    grad_stream, grad_branch, grad_attended, grad_act, out_sums = image_call(
        branch_kernel,
        images,
        [
            per_image(slots, model_width),
            per_image(1, model_width),
            whole(1, model_width),
            image_columns(hidden_blocks),
            anywhere,
        ],
        [
            per_image(slots, model_width),
            per_image(slots, model_width),
            per_image(slots, model_width),
            image_columns(hidden_blocks),
            whole(8, model_width),
        ],
        [
            shape((images, slots, model_width), f32),
            shape((images, slots, model_width), low),
            shape((images, slots, model_width), low),
            shape((hidden_blocks, rows, model_width), low),
            shape((8, model_width), f32),
        ],
        narrow_scratch,
        name="branch",
    )(
        live_counts, stream, grad_pooled.reshape(images, 1, model_width), scale_float[1:2], slope,
        narrow_full,
    )
    core = (lax.axis_index("fsdp") % 2).reshape(1)
    chips = owners // 2
    wide_rows = model_width // owners
    narrow_rows = narrower.shape[0]
    branch_rows = grad_branch.reshape(rows, model_width)
    halves = lambda count, width: [shape((chips, count, width), low)] * 2
    narrow_halves = pl.pallas_call(
        narrow_grad_kernel,
        grid_spec=pltpu.PrefetchScalarGridSpec(
            num_scalar_prefetch=1,
            grid=(1 + hidden_blocks,),
            in_specs=[
                whole(rows, model_width),
                block((1, rows, model_width), lambda k, _: (jnp.maximum(k - 1, 0), 0, 0)),
                whole(rows, model_width),
            ],
            out_specs=[anywhere] * 2,
            scratch_shapes=[
                pltpu.VMEM((hidden_width + model_width, model_width), low),
                pltpu.SemaphoreType.DMA((2 * chips,)),
            ],
        ),
        out_shape=halves(narrow_rows, model_width),
        compiler_params=roomy,
        cost_estimate=long,
        name="narrow_grad",
    )(core, attended.reshape(rows, model_width), hidden, branch_rows)
    narrow_flow = Flow(reduce_rows_first(*narrow_halves))
    narrow_flow.go()
    owner_block = block((chips, wide_rows, model_width), lambda k, _: (0, k, 0))
    few = padded_rows(images)
    hidden_halves = pl.pallas_call(
        wide_project_grad_kernel,
        grid_spec=pltpu.PrefetchScalarGridSpec(
            num_scalar_prefetch=1,
            grid=(hidden_blocks + 1,),
            in_specs=[
                whole(rows, model_width),
                block(
                    (1, rows, model_width), lambda k, _: (jnp.minimum(k, hidden_blocks - 1), 0, 0)
                ),
                whole(few, model_width),
                whole(few, model_width),
            ],
            out_specs=[owner_block] * 2,
        ),
        out_shape=halves((hidden_blocks + 1) * wide_rows, model_width),
        compiler_params=roomy,
        cost_estimate=long,
        name="hidden_grad",
    )(
        core, normed_rows, grad_act, jnp.pad(pooled_low, ((0, few - images), (0, 0))),
        jnp.pad(grad_embeds, ((0, few - images), (0, 0))),
    )
    hidden_flow = Flow(reduce_rows_last(*hidden_halves))
    hidden_flow.go()
    parts = images_dev
    per_part = images // parts
    part_rows = per_part * slots

    def shifted(base, rows_count):
        return block((1, rows_count, model_width), lambda image, counts: (base + image, 0, 0))

    def shifted_columns(base, count):
        return block((count, slots, model_width), lambda image, counts: (0, base + image, 0))

    head_gains = scale_float[2:4].reshape(2, 1, model_width)
    guards = narrow_flow.go()
    grad_qkv, head_sums = [], 0.0
    for part in range(parts):
        base = part * per_part
        grads, sums_part = image_call(
            functools.partial(attend_back_kernel, base=base, head_size=head_size),
            per_part,
            [
                shifted_columns(base, 3),
                shifted_columns(base, 2),
                shifted(base, slots),
                whole(2, 1, model_width),
            ]
            + [anywhere] * len(guards),
            [image_columns(3), whole(8, model_width)],
            [shape((3, part_rows, model_width), low), shape((8, model_width), f32)],
            [pltpu.VMEM((2, slots, model_width), f32)],
            name="attend_back",
        )(live_counts, qkv, rstd, grad_attended, head_gains, *guards)
        grad_qkv.append(grads)
        head_sums = head_sums + sums_part
        guards = [grads]
        if part == 0:
            guards += hidden_flow.go(grads)
    guards += narrow_flow.go(grads)
    qkv_halves = pl.pallas_call(
        lambda core_ref, normed_ref, *refs: wide_grad_kernel(
            core_ref, normed_ref, *refs[:parts], *refs[-2:]
        ),
        grid_spec=pltpu.PrefetchScalarGridSpec(
            num_scalar_prefetch=1,
            grid=(3,),
            in_specs=[whole(rows, model_width)]
            + [block((1, part_rows, model_width), lambda k, _: (k, 0, 0))] * parts
            + [anywhere] * len(guards),
            out_specs=[owner_block] * 2,
        ),
        out_shape=halves(3 * wide_rows, model_width),
        compiler_params=roomy,
        cost_estimate=long,
        name="qkv_grad",
    )(core, normed_rows, *grad_qkv, *guards)
    qkv_flow = Flow(reduce_rows_first(*qkv_halves))
    guards = qkv_flow.go()
    grad_patches, grad_places, merge_sums = [], [], 0.0
    for part in range(parts):
        base = part * per_part
        grads, place_part, sums_part = image_call(
            functools.partial(merge_back_kernel, base=base),
            per_part,
            [
                image_columns(3),
                shifted_columns(base, hidden_blocks),
                anywhere,
                shifted(base, slots),
                shifted(base, slots),
                whole(1, model_width),
                block((1, 1, slots), lambda image, counts, base=base: (base + image, 0, 0)),
                block((1, 1, slots), lambda image, counts, base=base: (base + image, 0, 0)),
                block((1, slots, 1), lambda image, counts, base=base: (base + image, 0, 0)),
            ]
            + [anywhere] * len(guards),
            [per_image(slots, model_width), whole(slots, model_width), whole(8, model_width)],
            [
                shape((per_part, slots, model_width), low),
                shape((slots, model_width), f32),
                shape((8, model_width), f32),
            ],
            [
                pltpu.VMEM((3 + hidden_blocks, model_width, model_width), low),
                pltpu.SemaphoreType.DMA((3 + hidden_blocks,)),
            ],
            name="merge_back",
        )(
            live_counts, grad_qkv[part], grad_act, wide_stack, merged, grad_stream,
            scale_float[0:1], slot_map, row_weight, column_weight, *guards,
        )
        grad_patches.append(grads.reshape(part_rows, model_width))
        grad_places.append(place_part)
        merge_sums = merge_sums + sums_part
        guards = [grads]
        if part == 0:
            guards += hidden_flow.go(grads) + qkv_flow.go(grads)
        elif part == 1:
            guards += narrow_flow.go(grads)
    guards += hidden_flow.go(grads) + qkv_flow.go(grads)
    scale_rows, scale_columns = scales.shape
    bias_count = biases.shape[0]
    grad_scale = jnp.stack([merge_sums[0], out_sums[hidden_blocks + 1], head_sums[0], head_sums[1]])
    grad_bias = jnp.concatenate([out_sums[: hidden_blocks + 1].reshape(-1), merge_sums[1]])
    beside = -(-slots // 128) * 128
    piece_width = model_width + beside
    fill = lambda values: jnp.pad(
        values, ((0, 0), (0, 0), (0, piece_width - values.shape[2]))
    )
    extra_rows = 16
    extra = jnp.concatenate(
        [
            fill(grad_bias.reshape(owners, 1, bias_count)),
            fill(jnp.swapaxes(grad_scale.reshape(scale_rows, owners, scale_columns), 0, 1)),
            jnp.zeros((owners, extra_rows - 1 - scale_rows, piece_width), f32),
        ],
        axis=1,
    ).astype(low)
    embed_halves = pl.pallas_call(
        lambda core_ref, pixel_ref, *refs: embed_grad_kernel(
            core_ref, pixel_ref, *refs[: 2 * parts + 1], *refs[-2:]
        ),
        grid_spec=pltpu.PrefetchScalarGridSpec(
            num_scalar_prefetch=1,
            grid=(1,),
            in_specs=[whole(rows, patch_size)]
            + [whole(part_rows, model_width)] * parts
            + [whole(slots, model_width)] * parts
            + [whole(owners, extra_rows, piece_width)]
            + [anywhere] * len(guards),
            out_specs=[whole(chips, wide_rows + extra_rows, piece_width)] * 2,
        ),
        out_shape=halves(wide_rows + extra_rows, piece_width),
        compiler_params=roomy,
        cost_estimate=long,
        name="embed_grad",
    )(core, pixel_rows.reshape(rows, patch_size), *grad_patches, *grad_places, extra, *guards)
    embed_flow = Flow(reduce_rows_last(*embed_halves))
    flows = (narrow_flow, hidden_flow, qkv_flow, embed_flow)
    while any(flow.result is None for flow in flows):
        for flow in flows:
            if flow.result is None:
                flow.go()
    shards = [flow.result for flow in flows]
    squares_sum = pl.pallas_call(
        square_kernel,
        out_shape=shape((8, 128), f32),
        compiler_params=roomy,
        name="squares",
    )(*shards)
    squares_sum = sum_over(squares_sum, "fsdp")
    total_norm = jnp.sqrt(squares_sum[0, 0])
    moments = (
        moment_embedder,
        moment_positions,
        moment_widener,
        moment_narrower,
        moment_projector,
        moment_scales,
        moment_biases,
    )
    squares = (
        square_embedder,
        square_positions,
        square_widener,
        square_narrower,
        square_projector,
        square_scales,
        square_biases,
    )
    as_rows = lambda arrays: [
        array.reshape(1, -1) if array.ndim == 1 else array for array in arrays
    ]
    outs = pl.pallas_call(
        functools.partial(update_kernel, wide_rows=wide_rows),
        out_shape=[shape(array.shape, f32) for array in as_rows(weights) * 2],
        compiler_params=roomy,
        name="update",
    )(squares_sum, *shards, *as_rows(weights), *as_rows(moments), *as_rows(squares))
    outs = [
        out.reshape(array.shape) for out, array in zip(outs, weights * 2, strict=True)
    ]
    return (objective, weight_total_all, total_norm, *outs)


def solution(mesh):
    return jax.shard_map(
        per_device,
        mesh=mesh,
        in_specs=(
            P(None, ("rep", "fsdp"), None, None),
            P(None, ("rep", "fsdp"), None),
            P(None, ("rep", "fsdp"), None),
            P(None, ("rep", "fsdp")),
            P(),
            P(),
            P("fsdp", None),
            P(None, "fsdp"),
            P("fsdp", None),
            P("fsdp", None),
            P("fsdp", None),
            P(None, "fsdp"),
            P("fsdp"),
            P("fsdp", None),
            P(None, "fsdp"),
            P("fsdp", None),
            P("fsdp", None),
            P("fsdp", None),
            P(None, "fsdp"),
            P("fsdp"),
            P("fsdp", None),
            P(None, "fsdp"),
            P("fsdp", None),
            P("fsdp", None),
            P("fsdp", None),
            P(None, "fsdp"),
            P("fsdp"),
        ),
        out_specs=(
            P(),
            P(),
            P(),
            P("fsdp", None),
            P(None, "fsdp"),
            P("fsdp", None),
            P("fsdp", None),
            P("fsdp", None),
            P(None, "fsdp"),
            P("fsdp"),
            P("fsdp", None),
            P(None, "fsdp"),
            P("fsdp", None),
            P("fsdp", None),
            P("fsdp", None),
            P(None, "fsdp"),
            P("fsdp"),
        ),
        check_vma=False,
    )
```

```python
import functools

import jax
import jax.numpy as jnp
from jax import lax
from jax.experimental import pallas as pl
from jax.experimental.pallas import tpu as pltpu
from jax.sharding import PartitionSpec as P

HEADS = 12


norm_eps = 1e-06
clip_bound = 0.1
beta_first = 0.9
beta_second = 0.999
learn_rate = 0.03
weight_decay = 0.1
adam_eps = 1e-08
step_number = 10
logit_temper = 10.0


def product(left, right):
    return jnp.dot(left, right, preferred_element_type=jnp.float32)


def product_across(left, right):
    return lax.dot_general(
        left, right, (((0,), (0,)), ((), ())), preferred_element_type=jnp.float32
    )


def product_along(left, right):
    return lax.dot_general(
        left, right, (((1,), (1,)), ((), ())), preferred_element_type=jnp.float32
    )


def adam_step(weight, gradient, moment, square, factor):
    clipped = gradient * factor
    moment_new = beta_first * moment + (1.0 - beta_first) * clipped
    square_new = beta_second * square + (1.0 - beta_second) * clipped * clipped
    mean_hat = moment_new / (1.0 - beta_first**step_number)
    square_hat = square_new / (1.0 - beta_second**step_number)
    change = -learn_rate * (mean_hat / (jnp.sqrt(square_hat) + adam_eps) + weight_decay * weight)
    return (change, clipped)


def bit_swap(size, bit):
    return [(index, index ^ bit) for index in range(size)]


def ordered_pair(own, other, axis, bit):
    low_side = (lax.axis_index(axis) & bit) == 0
    return jnp.where(low_side, own, other), jnp.where(low_side, other, own)


def exchange_steps():
    steps = []
    for axis in ("fsdp", "rep"):
        size = lax.axis_size(axis)
        bit = 1
        while bit < size:
            steps.append((axis, size, bit))
            bit *= 2
    return steps


def column_totals(top, total, sums):
    micro_count = top.shape[0]
    for axis, size, bit in exchange_steps():
        packed = jnp.concatenate([top, total, sums], axis=0)
        other = lax.ppermute(packed, axis, bit_swap(size, bit))
        first, second = ordered_pair(packed, other, axis, bit)
        top_a, top_b = first[:micro_count], second[:micro_count]
        top = jnp.maximum(top_a, top_b)
        total = first[micro_count : 2 * micro_count] * jnp.exp(top_a - top) + second[
            micro_count : 2 * micro_count
        ] * jnp.exp(top_b - top)
        sums = first[2 * micro_count :] + second[2 * micro_count :]
    return top, total, sums


def sum_over(value, axis):
    size = lax.axis_size(axis)
    bit = 1
    while bit < size:
        value = value + lax.ppermute(value, axis, bit_swap(size, bit))
        bit *= 2
    return value


def padded_rows(rows):
    return -(-rows // 16) * 16


def split_two(values):
    high = values.astype(jnp.bfloat16)
    return high, (values - high.astype(jnp.float32)).astype(jnp.bfloat16)


def normal_rows(values):
    center = values - jnp.mean(values, axis=-1, keepdims=True)
    rstd = lax.rsqrt(jnp.mean(center * center, axis=-1, keepdims=True) + norm_eps)
    return center * rstd, rstd


def head_mixer(head_size):
    row = lax.broadcasted_iota(jnp.int32, (256, 256), 0) // head_size
    column = lax.broadcasted_iota(jnp.int32, (256, 256), 1) // head_size
    return jnp.where(row == column, 1.0 / head_size, 0.0).astype(jnp.bfloat16)


def head_mean(values, mixer):
    parts = []
    for at in range(0, values.shape[1], 256):
        high, low = split_two(values[:, at : at + 256])
        parts.append(product(high, mixer) + product(low, mixer))
    return jnp.concatenate(parts, axis=1)


def embed_kernel(
    counts_ref, pixel_ref, map_ref, row_ref, column_ref, embed_ref, place_ref, gain_ref, *refs
):
    merged_ref, normed_ref = refs[-2:]
    live_count = counts_ref[pl.program_id(0)]
    slots = merged_ref.shape[1]
    patches = product(pixel_ref[0], embed_ref[...]) + place_ref[...]
    high, low = split_two(patches * column_ref[0])
    slot = lax.broadcasted_iota(jnp.int32, (slots, slots), 0)
    member = slot == map_ref[0]
    hot = jnp.where(member, 1.0, 0.0).astype(jnp.bfloat16)
    total = jnp.sum(jnp.where(member, row_ref[0], 0.0), axis=1, keepdims=True)
    vacant = lax.broadcasted_iota(jnp.int32, (slots, 1), 0) >= live_count
    total = total + jnp.where(vacant, 1.0, 0.0)
    merged = (product(hot, high) + product(hot, low)) / total
    merged_ref[0] = merged
    unit, _ = normal_rows(merged)
    normed_ref[0] = (unit * gain_ref[...]).astype(jnp.bfloat16)


def gelu_pair(values):
    size = jnp.abs(values)
    turn = 1.0 / (1.0 + (0.3275911 * 0.7071067811865476) * size)
    bell = jnp.exp(-0.5 * values * values)
    poly = turn * (
        0.5 * 0.254829592
        + turn
        * (
            0.5 * -0.284496736
            + turn
            * (0.5 * 1.421413741 + turn * (0.5 * -1.453152027 + turn * (0.5 * 1.061405429)))
        )
    )
    tail = poly * bell
    share = jnp.where(values >= 0, 1.0 - tail, tail)
    return values * share, share + values * (bell * 0.3989422804014327)


def widen_heads_kernel(
    place_ref, normed_ref, gain_ref, *refs, found, chunk, head_size
):
    heads_ref, rstd_ref, wide_hbm, held_ref, sem, out_sem = refs[-6:]
    sources = refs[: len(found)]
    step = pl.program_id(0)
    keep = pltpu.make_async_copy(held_ref, wide_hbm, out_sem)

    @pl.when(step == 0)
    def _():
        fetch(place_ref, sources, found, held_ref, sem)
        fetched(place_ref, sources, found, held_ref, sem)
        keep.start()

    chunks = normed_ref.shape[0] // chunk
    mixer = head_mixer(head_size)
    gain = gain_ref[0]
    for index in range(chunks):
        rows = slice(index * chunk, (index + 1) * chunk)
        values = product(normed_ref[rows, :], held_ref[step])
        center = values - head_mean(values, mixer)
        rstd = lax.rsqrt(head_mean(center * center, mixer) + norm_eps)
        rstd_ref[0, rows, :] = rstd
        heads_ref[0, rows, :] = (center * rstd * gain).astype(jnp.bfloat16)

    pl.when(step == pl.num_programs(0) - 1)(keep.wait)


def widen_value_kernel(normed_ref, wide_ref, *refs):
    values_ref = refs[-1]
    values_ref[0] = product(normed_ref[...], wide_ref[0]).astype(jnp.bfloat16)


def widen_hidden_kernel(place_ref, normed_ref, bias_ref, *refs, found, chunk):
    hidden_ref, slope_ref, wide_hbm, held_ref, sem, out_sem = refs[-6:]
    sources = refs[: len(found)]
    step = pl.program_id(0)
    keep = pltpu.make_async_copy(held_ref, wide_hbm, out_sem)

    @pl.when(step == 0)
    def _():
        fetch(place_ref, sources, found, held_ref, sem)
        fetched(place_ref, sources, found, held_ref, sem)
        keep.start()

    for index in range(normed_ref.shape[0] // chunk):
        rows = slice(index * chunk, (index + 1) * chunk)
        values = product(normed_ref[rows, :], held_ref[step]) + bias_ref[0]
        hidden, slope = gelu_pair(values)
        hidden_ref[0, rows, :] = hidden.astype(jnp.bfloat16)
        slope_ref[0, rows, :] = slope.astype(jnp.bfloat16)

    pl.when(step == pl.num_programs(0) - 1)(keep.wait)


def attend_kernel(counts_ref, heads_ref, values_ref, *refs, head_size):
    attended_ref = refs[-1]
    live_count = counts_ref[pl.program_id(0)]
    slots, width = attended_ref.shape[1:]
    factor = head_size ** (-0.5) * 1.4426950408889634
    key_live = jnp.where(
        lax.broadcasted_iota(jnp.int32, (1, slots), 1) < live_count, 1.0, 0.0
    )
    first_half = lax.broadcasted_iota(jnp.int32, (slots, 2 * head_size), 1) < head_size
    zero = jnp.zeros((slots, 2 * head_size), jnp.bfloat16)
    for at in range(0, width, 2 * head_size):
        columns = slice(at, at + 2 * head_size)
        queries, keys = (heads_ref[part, :, columns] for part in range(2))
        values = values_ref[0, :, columns]
        outs = []
        for half in range(2):
            own = jnp.where(first_half, queries, zero) if half == 0 else jnp.where(first_half, zero, queries)
            weights = jnp.exp2(product_along(own, keys) * factor) * key_live
            share = weights * (1.0 / jnp.sum(weights, axis=1, keepdims=True))
            outs.append(product(share.astype(jnp.bfloat16), values))
        attended_ref[0, :, columns] = jnp.where(first_half, outs[0], outs[1]).astype(jnp.bfloat16)


def join_kernel(
    counts_ref, place_ref, attended_ref, hidden_ref, merged_ref, bias_ref, gain_ref, *refs, found
):
    stream_ref, pooled_ref, narrow_hbm, held_ref, sem, out_sem = refs[-6:]
    sources = refs[: len(found)]
    image = pl.program_id(0)
    live_count = counts_ref[image]
    slots, width = merged_ref.shape[1:]
    keep = pltpu.make_async_copy(held_ref, narrow_hbm, out_sem)

    @pl.when(image == 0)
    def _():
        fetch(place_ref, sources, found, held_ref, sem)
        fetched(place_ref, sources, found, held_ref, sem)
        keep.start()

    stream = merged_ref[0] + bias_ref[...]
    for k in range(1 + hidden_ref.shape[0]):
        left = attended_ref[0] if k == 0 else hidden_ref[k - 1]
        stream = stream + product(left, held_ref[0, k * width : (k + 1) * width, :])
    stream_ref[0] = stream
    unit, _ = normal_rows(stream)
    live = lax.broadcasted_iota(jnp.int32, (slots, 1), 0) < live_count
    total = jnp.sum(jnp.where(live, unit, 0.0), axis=0, keepdims=True)
    pooled_ref[0] = total * gain_ref[...] / live_count.astype(jnp.float32)

    pl.when(image == pl.num_programs(0) - 1)(keep.wait)


def branch_kernel(
    counts_ref, stream_ref, grad_pooled_ref, gain_ref, slope_ref, narrow_hbm,
    grad_stream_ref, grad_branch_ref, grad_attended_ref, grad_act_ref, sums_ref, narrow_ref, sem,
):
    image = pl.program_id(0)
    live_count = counts_ref[image]
    slots, width = stream_ref.shape[1:]
    copy = pltpu.make_async_copy(narrow_hbm, narrow_ref, sem)

    @pl.when(image == 0)
    def _():
        copy.start()
        sums_ref[...] = jnp.zeros_like(sums_ref)

    unit, rstd = normal_rows(stream_ref[0])
    live = lax.broadcasted_iota(jnp.int32, (slots, 1), 0) < live_count
    above = grad_pooled_ref[0] / live_count.astype(jnp.float32)
    slanted = above * gain_ref[...]
    mean_first = jnp.mean(slanted, axis=-1, keepdims=True)
    mean_second = jnp.mean(slanted * unit, axis=-1, keepdims=True)
    grad_stream = jnp.where(live, rstd * (slanted - mean_first - unit * mean_second), 0.0)
    grad_stream_ref[0] = grad_stream
    grad_branch = grad_stream.astype(jnp.bfloat16)
    grad_branch_ref[0] = grad_branch
    parts = slope_ref.shape[0]
    sums_ref[parts : parts + 1, :] += jnp.sum(grad_stream, axis=0, keepdims=True)
    sums_ref[parts + 1 : parts + 2, :] += above * jnp.sum(
        jnp.where(live, unit, 0.0), axis=0, keepdims=True
    )

    @pl.when(image == 0)
    def _():
        copy.wait()

    grad_attended_ref[0] = product_along(grad_branch, narrow_ref[:width, :]).astype(jnp.bfloat16)
    for part in range(parts):
        grad_act = product_along(
            grad_branch, narrow_ref[(part + 1) * width : (part + 2) * width, :]
        ) * slope_ref[part].astype(jnp.float32)
        grad_act_ref[part] = grad_act.astype(jnp.bfloat16)
        sums_ref[part : part + 1, :] += jnp.sum(grad_act, axis=0, keepdims=True)


def attend_back_kernel(
    counts_ref, heads_ref, values_ref, rstd_ref, grad_attended_ref, gain_ref, *refs, base, head_size
):
    grad_qkv_ref, sums_ref, grad_ref = refs[-3:]
    image = pl.program_id(0)
    live_count = counts_ref[base + image]
    slots, width = grad_attended_ref.shape[1:]

    @pl.when(image == 0)
    def _():
        sums_ref[...] = jnp.zeros_like(sums_ref)

    factor = head_size ** (-0.5)
    key_live = lax.broadcasted_iota(jnp.int32, (slots, 1), 0) < live_count
    first_half = lax.broadcasted_iota(jnp.int32, (slots, 2 * head_size), 1) < head_size
    zero = jnp.zeros((slots, 2 * head_size), jnp.bfloat16)
    for at in range(0, width, 2 * head_size):
        columns = slice(at, at + 2 * head_size)
        queries, keys = (heads_ref[part, :, columns] for part in range(2))
        values = values_ref[0, :, columns]
        above = grad_attended_ref[0, :, columns]
        grad_queries, grad_keys, grad_values = [], [], []
        for half in range(2):
            pick = lambda both: jnp.where(first_half, both, zero) if half == 0 else jnp.where(first_half, zero, both)
            own_queries, own_above = pick(queries), pick(above)
            weights = jnp.exp2(product_along(keys, own_queries) * (factor * 1.4426950408889634))
            weights = jnp.where(key_live, weights, 0.0)
            share = weights * (1.0 / jnp.sum(weights, axis=0, keepdims=True))
            grad_share = product_along(values, own_above)
            dot_row = jnp.sum(share * grad_share, axis=0, keepdims=True)
            grad_raw = (share * (grad_share - dot_row) * factor).astype(jnp.bfloat16)
            grad_values.append(product(share.astype(jnp.bfloat16), own_above))
            grad_keys.append(product(grad_raw, own_queries))
            grad_queries.append(product_across(grad_raw, keys))
        grad_qkv_ref[2, :, columns] = (grad_values[0] + grad_values[1]).astype(jnp.bfloat16)
        grad_ref[1, :, columns] = grad_keys[0] + grad_keys[1]
        grad_ref[0, :, columns] = jnp.where(first_half, grad_queries[0], grad_queries[1])
    mixer = head_mixer(head_size)
    for part in range(2):
        gain = gain_ref[part]
        above = grad_ref[part]
        unit = heads_ref[part].astype(jnp.float32) / gain
        sums_ref[part : part + 1, :] += jnp.sum(above * unit, axis=0, keepdims=True)
        slanted = above * gain
        back = slanted - head_mean(slanted, mixer) - unit * head_mean(slanted * unit, mixer)
        grad_qkv_ref[part] = (rstd_ref[part] * back).astype(jnp.bfloat16)


def merge_back_kernel(
    counts_ref, grad_qkv_ref, grad_act_ref, wide_hbm, wide_hidden_hbm, merged_ref, grad_stream_ref, gain_ref,
    map_ref, row_ref, column_ref, *refs, base,
):
    grad_patch_ref, grad_place_ref, sums_ref, wide_ref, sem = refs[-5:]
    image = pl.program_id(0)
    live_count = counts_ref[base + image]
    slots, width = merged_ref.shape[1:]
    blocks = wide_ref.shape[0]
    copies = [
        pltpu.make_async_copy(
            wide_hbm.at[part] if part < 3 else wide_hidden_hbm.at[part - 3],
            wide_ref.at[part],
            sem.at[part],
        )
        for part in range(blocks)
    ]

    @pl.when(image == 0)
    def _():
        for copy in copies:
            copy.start()
        sums_ref[...] = jnp.zeros_like(sums_ref)
        grad_place_ref[...] = jnp.zeros_like(grad_place_ref)

    grad_normed = jnp.zeros((slots, width), jnp.float32)
    for part in range(blocks):
        pl.when(image == 0)(copies[part].wait)
        grads = grad_qkv_ref[part] if part < 3 else grad_act_ref[part - 3]
        grad_normed = grad_normed + product_along(grads, wide_ref[part])
    unit, rstd = normal_rows(merged_ref[0])
    sums_ref[0:1, :] += jnp.sum(grad_normed * unit, axis=0, keepdims=True)
    slanted = grad_normed * gain_ref[...]
    back = (
        slanted
        - jnp.mean(slanted, axis=-1, keepdims=True)
        - unit * jnp.mean(slanted * unit, axis=-1, keepdims=True)
    )
    grad_merged = grad_stream_ref[0] + rstd * back
    slot = lax.broadcasted_iota(jnp.int32, (slots, slots), 0)
    member = slot == map_ref[0]
    hot = jnp.where(member, 1.0, 0.0).astype(jnp.bfloat16)
    total = jnp.sum(jnp.where(member, row_ref[0], 0.0), axis=1, keepdims=True)
    vacant = lax.broadcasted_iota(jnp.int32, (slots, 1), 0) >= live_count
    total = total + jnp.where(vacant, 1.0, 0.0)
    high, low = split_two(grad_merged / total)
    grad_patches = (product_across(hot, high) + product_across(hot, low)) * column_ref[0]
    grad_patch_ref[0] = grad_patches.astype(jnp.bfloat16)
    grad_place_ref[...] += grad_patches
    sums_ref[1:2, :] += jnp.sum(grad_patches, axis=0, keepdims=True)


def block(shape, index_map):
    return pl.BlockSpec(shape, index_map)


def per_image(rows, width):
    return block((1, rows, width), lambda image, counts: (image, 0, 0))


def whole(*shape):
    return block(shape, lambda *_: (0,) * len(shape))


anywhere = pl.BlockSpec(memory_space=pl.ANY)
roomy = pltpu.CompilerParams(vmem_limit_bytes=60 * 1024 * 1024)


long = pl.CostEstimate(flops=60_000_000_000, bytes_accessed=1000, transcendentals=0)


def image_call(kernel, images, in_specs, out_specs, out_shape, scratch=(), name=None):
    return pl.pallas_call(
        kernel,
        grid_spec=pltpu.PrefetchScalarGridSpec(
            num_scalar_prefetch=1,
            grid=(images,),
            in_specs=in_specs,
            out_specs=out_specs,
            scratch_shapes=list(scratch),
        ),
        out_shape=out_shape,
        compiler_params=roomy,
        cost_estimate=long,
        name=name,
    )


def picked(terms, axis, index):
    return [lax.dynamic_index_in_dim(term, index, axis, keepdims=False) for term in terms]


def added(terms):
    total = terms[0].astype(jnp.float32)
    for term in terms[1:]:
        total = total + term.astype(jnp.float32)
    return total


def behind(terms, after):
    if after is None:
        return terms
    return lax.optimization_barrier((terms, after))[0]


def traded(terms, axis, index, count, mesh_axis, stride):
    size = lax.axis_size(mesh_axis)
    sends = [
        added(picked(terms, axis, index ^ turn)).astype(jnp.bfloat16) for turn in range(1, count)
    ]
    after = yield sends
    kept = picked(terms, axis, index)
    for turn, send in enumerate(sends, 1):
        kept.append(lax.ppermute(send, mesh_axis, bit_swap(size, turn * stride)))
    return behind(kept, after)


def core_terms(mine, other):
    chips, rows, width = mine.shape
    after = yield [other]
    got = lax.ppermute(other, "fsdp", bit_swap(lax.axis_size("fsdp"), 1))
    return [term.reshape(chips // 2, 2, rows, width) for term in behind([mine, got], after)]


def rep_swap(own):
    return lax.ppermute(own, "rep", bit_swap(2, 1))


def places():
    place = lax.axis_index("fsdp")
    return place // 4, (place // 2) % 2


def reduce_rows_first(mine, other):
    high, middle = places()
    reps = lax.axis_size("rep")
    count = mine.shape[0] // 2
    terms = yield from core_terms(mine, other)
    terms = [
        term.reshape(count, 2, reps, term.shape[2] // reps, term.shape[3]) for term in terms
    ]
    terms = yield from traded(terms, 2, lax.axis_index("rep"), reps, "rep", 1)
    terms = yield from traded(terms, 1, middle, 2, "fsdp", 2)
    terms = yield from traded(terms, 0, high, count, "fsdp", 4)
    own = added(terms).astype(jnp.bfloat16)
    yield [own]
    if reps == 2:
        first, second = ordered_pair(own, rep_swap(own), "rep", 1)
        return jnp.concatenate([first, second], axis=0)
    return lax.all_gather(own, "rep", axis=0, tiled=True)


def reduce_rows_last(mine, other):
    high, middle = places()
    count = mine.shape[0] // 2
    terms = yield from core_terms(mine, other)
    terms = yield from traded(terms, 1, middle, 2, "fsdp", 2)
    terms = yield from traded(terms, 0, high, count, "fsdp", 4)
    own = added(terms).astype(jnp.bfloat16)
    yield [own]
    if lax.axis_size("rep") == 2:
        return added([own, rep_swap(own)]).astype(jnp.bfloat16)
    return lax.psum(own, "rep")


def core_swap(own):
    return lax.ppermute(own, "fsdp", bit_swap(lax.axis_size("fsdp"), 1))


def middle_swap(own):
    return lax.ppermute(own, "fsdp", bit_swap(lax.axis_size("fsdp"), 2))


def high_gather(own):
    owners = lax.axis_size("fsdp")
    after = yield [own]
    got = [lax.ppermute(own, "fsdp", bit_swap(owners, turn)) for turn in range(4, owners, 4)]
    return [own] + behind(got, after)


def with_cores(found):
    after = yield [item[0] for item in found]
    got = behind([core_swap(item[0]) for item in found], after)
    return found + [
        (array, [turn + 1 for turn in turns], parts)
        for array, (_, turns, parts) in zip(got, found, strict=True)
    ]


def gather_plain(own):
    after_high = yield from high_gather(own)
    near = jnp.stack(after_high)
    turns = list(range(0, lax.axis_size("fsdp"), 4))
    after = yield [near]
    far = behind([middle_swap(near)], after)[0]
    whole_rows = [None] * len(turns)
    found = [(near, turns, whole_rows), (far, [turn + 2 for turn in turns], whole_rows)]
    return (yield from with_cores(found))


def own_columns(own):
    half = own.shape[-1] // 2
    return lax.dynamic_slice_in_dim(own, lax.axis_index("rep") * half, half, own.ndim - 1)


def gather_split(own):
    if lax.axis_size("rep") != 2:
        return (yield from gather_plain(own))
    after_high = yield from high_gather(own_columns(own))
    turns = list(range(0, lax.axis_size("fsdp"), 4))
    cut = len(turns) // 2
    early, late = jnp.stack(after_high[:cut]), jnp.stack(after_high[cut:])
    after = yield [early, late]
    got = behind([rep_swap(early), middle_swap(late)], after)
    early, late = (jnp.concatenate(pair) for pair in zip((early, late), got, strict=True))
    after = yield [early, late]
    got = [middle_swap(early), rep_swap(late)]
    early, late, *got = behind([early, late, *got], after if after is not None else ())
    far = lambda some: [turn + 2 for turn in some]
    first, second = turns[:cut], turns[cut:]
    near_parts, all_parts = [0] * cut + [1] * cut, [0] * (2 * cut)
    found = [
        (early, first + first, near_parts),
        (got[0], far(first + first), near_parts),
        (late, second + far(second), all_parts),
        (got[1], second + far(second), [1] * (2 * cut)),
    ]
    return (yield from with_cores(found))


def assemble_copies(place_ref, sources, found, out_ref, columns, sem):
    copies = []
    for source, (turns, parts) in zip(sources, found, strict=True):
        rows, width = source.shape[2:]
        for slot, (turn, part) in enumerate(zip(turns, parts, strict=True)):
            owner = place_ref[0] ^ turn
            row = pl.ds(pl.multiple_of(owner * rows, rows), rows)
            if part is None:
                piece, target = source.at[slot, :, :, columns], out_ref.at[:, row, :]
            else:
                side = pl.ds(pl.multiple_of((place_ref[1] ^ part) * width, width), width)
                piece, target = source.at[slot], out_ref.at[:, row, side]
            copies.append(pltpu.make_async_copy(piece, target, sem.at[len(copies)]))
    return copies


def gathered(items):
    arrays = [item[0] for item in items]
    found = tuple((tuple(item[1]), tuple(item[2])) for item in items)
    segments, rows, width = arrays[0].shape[1:]
    if found[0][1][0] is not None:
        width = 2 * width
    owners = sum(len(item[0]) for item in found) * arrays[0].shape[3] // width
    return arrays, found, (segments, owners * rows, width)


def gather_scratch(found, size):
    return [
        pltpu.VMEM(size, jnp.bfloat16),
        pltpu.SemaphoreType.DMA((sum(len(item[0]) for item in found),)),
        pltpu.SemaphoreType.DMA,
    ]


def fetch(place_ref, sources, found, held_ref, sem):
    for copy in assemble_copies(place_ref, sources, found, held_ref, slice(None), sem):
        copy.start()


def fetched(place_ref, sources, found, held_ref, sem):
    for copy in assemble_copies(place_ref, sources, found, held_ref, slice(None), sem):
        copy.wait()


def assemble_small_kernel(place_ref, *refs, found, width):
    embed_ref, beside_out_ref, beside_ref, sem, beside_sem = refs[-5:]
    sources = refs[: len(found)]
    first = slice(0, width)
    second = slice(width, sources[0].shape[3])
    copies = assemble_copies(place_ref, sources, found, embed_ref, first, sem)
    copies += assemble_copies(place_ref, sources, found, beside_ref, second, beside_sem)
    for copy in copies:
        copy.start()
    for copy in copies:
        copy.wait()
    beside_out_ref[...] = beside_ref[0].astype(jnp.float32).T


def assembled_small(place, items, owners, width, guards):
    arrays, found, _ = gathered(items)
    rows, whole_width = arrays[0].shape[2:]
    beside = whole_width - width
    count = sum(len(item[0]) for item in found)
    embed, table = pl.pallas_call(
        lambda place_ref, *refs: assemble_small_kernel(
            place_ref, *refs[: len(arrays)], *refs[-5:], found=found, width=width
        ),
        grid_spec=pltpu.PrefetchScalarGridSpec(
            num_scalar_prefetch=1,
            grid=(1,),
            in_specs=[anywhere] * (len(arrays) + len(guards)),
            out_specs=[whole(1, owners * rows, width), whole(beside, owners * rows)],
            scratch_shapes=[
                pltpu.VMEM((1, owners * rows, beside), jnp.bfloat16),
                pltpu.SemaphoreType.DMA((count,)),
                pltpu.SemaphoreType.DMA((count,)),
            ],
        ),
        out_shape=[
            jax.ShapeDtypeStruct((1, owners * rows, width), jnp.bfloat16),
            jax.ShapeDtypeStruct((beside, owners * rows), jnp.float32),
        ],
        compiler_params=roomy,
        cost_estimate=long,
        name="assemble_small",
    )(place, *arrays, *guards)
    return embed[0], table


def first_behind(value, after):
    return lax.optimization_barrier((value, after))[0]


class Flow:
    def __init__(self, steps):
        self.steps, self.result = steps, None

    def go(self, after=None):
        try:
            return self.steps.send(after)
        except StopIteration as end:
            self.result = end.value
            return []

    def finish(self):
        while self.result is None:
            self.go()
        return self.result


def split_cores(result, core, mine_ref, other_ref):
    chips, rows = mine_ref.shape[:2]
    pairs = result.astype(jnp.bfloat16).reshape(chips, 2, rows, result.shape[1])
    first, second = pairs[:, 0], pairs[:, 1]
    mine_ref[...] = jnp.where(core == 0, first, second)
    other_ref[...] = jnp.where(core == 0, second, first)


def narrow_grad_kernel(
    core_ref, attended_ref, hidden_ref, branch_ref, mine_hbm, other_hbm, total_ref, sem
):
    step = pl.program_id(0)
    width = branch_ref.shape[1]
    chips, rows = mine_hbm.shape[:2]

    @pl.when(step == 0)
    def _():
        total_ref[:width, :] = product_across(attended_ref[...], branch_ref[...]).astype(
            jnp.bfloat16
        )

    @pl.when(step > 0)
    def _():
        at = pl.multiple_of(step * width, width)
        total_ref[pl.ds(at, width), :] = product_across(hidden_ref[0], branch_ref[...]).astype(
            jnp.bfloat16
        )

    @pl.when(step == pl.num_programs(0) - 1)
    def _():
        core = core_ref[0]
        copies = []
        for chip in range(chips):
            for side, out in enumerate((mine_hbm, other_hbm)):
                owner = 2 * chip + (core ^ side)
                source = total_ref.at[pl.ds(pl.multiple_of(owner * rows, rows), rows), :]
                copies.append(
                    pltpu.make_async_copy(source, out.at[chip], sem.at[2 * chip + side])
                )
        for copy in copies:
            copy.start()
        for copy in copies:
            copy.wait()


def wide_grad_kernel(core_ref, normed_ref, *refs):
    *grad_refs, mine_ref, other_ref = refs
    total = None
    for part, grad_ref in enumerate(grad_refs):
        rows = grad_ref.shape[1]
        term = product_across(normed_ref[part * rows : (part + 1) * rows, :], grad_ref[0])
        total = term if total is None else total + term
    split_cores(total, core_ref[0], mine_ref, other_ref)


def wide_project_grad_kernel(
    core_ref, normed_ref, grad_ref, pooled_ref, embeds_ref, mine_ref, other_ref
):
    last = pl.program_id(0) == pl.num_programs(0) - 1

    @pl.when(jnp.logical_not(last))
    def _():
        wide_grad_kernel(core_ref, normed_ref, grad_ref, mine_ref, other_ref)

    @pl.when(last)
    def _():
        split_cores(
            product_across(pooled_ref[...], embeds_ref[...]), core_ref[0], mine_ref, other_ref
        )


def embed_grad_kernel(core_ref, pixel_ref, *refs):
    *grad_refs, table_ref, mine_ref, other_ref = refs
    parts = len(grad_refs) // 2
    total, place = None, None
    for part in range(parts):
        rows = grad_refs[part].shape[0]
        term = product_across(pixel_ref[part * rows : (part + 1) * rows, :], grad_refs[part][...])
        total = term if total is None else total + term
        own = grad_refs[parts + part][...]
        place = own if place is None else place + own
    width = total.shape[1]
    beside = mine_ref.shape[2] - width
    spare = jnp.zeros((beside - place.shape[0] - table_ref.shape[0], width), jnp.float32)
    place = jnp.concatenate([place, table_ref[...], spare], axis=0).T
    split_cores(jnp.concatenate([total, place], axis=1), core_ref[0], mine_ref, other_ref)


def square_kernel(*refs):
    *shard_refs, total_ref = refs
    total = jnp.zeros((1, 1), jnp.float32)
    for shard_ref in shard_refs:
        values = shard_ref[...].astype(jnp.float32)
        columns = jnp.sum(values * values, axis=0, keepdims=True)
        total = total + jnp.sum(columns, axis=1, keepdims=True)
    total_ref[...] = jnp.broadcast_to(total, total_ref.shape)


def update_kernel(
    total_ref, narrow_ref, hidden_ref, qkv_ref, embed_ref, *refs, wide_rows
):
    weights, moments, squares = refs[:7], refs[7:14], refs[14:21]
    changes, clips = refs[21:28], refs[28:35]
    factor = clip_bound / jnp.maximum(jnp.sqrt(total_ref[:1, :1]), clip_bound)
    width = narrow_ref.shape[1]

    def update(index, rows, columns, gradient):
        at = (slice(*rows), slice(*columns))
        change, clipped = adam_step(
            weights[index][at],
            gradient.astype(jnp.float32),
            moments[index][at],
            squares[index][at],
            factor,
        )
        changes[index][at] = change
        clips[index][at] = clipped

    everything = (None,)
    update(0, everything, everything, embed_ref[:, :width])
    blocks = weights[2].shape[1] // width
    for k in range(blocks):
        source, at = (qkv_ref, k) if k < 3 else (hidden_ref, k - 3)
        update(
            2,
            everything,
            (k * width, (k + 1) * width),
            source[at * wide_rows : (at + 1) * wide_rows, :],
        )
    update(3, everything, everything, narrow_ref[...])
    update(4, everything, everything, hidden_ref[(blocks - 3) * wide_rows :, :])
    beside = embed_ref[:, width:].astype(jnp.float32).T
    slots = weights[1].shape[0]
    update(1, everything, everything, beside[:slots, :])
    at = padded_rows(slots)
    scale_rows = weights[5].shape[0]
    update(5, everything, everything, beside[at : at + scale_rows, :])
    at += scale_rows
    update(6, everything, everything, beside[at : at + weights[6].shape[0], :])


def per_device(
    pixels,
    merge_map,
    merge_weight,
    counts,
    captions,
    pairing,
    embedder,
    positions,
    widener,
    narrower,
    projector,
    scales,
    biases,
    moment_embedder,
    moment_positions,
    moment_widener,
    moment_narrower,
    moment_projector,
    moment_scales,
    moment_biases,
    square_embedder,
    square_positions,
    square_widener,
    square_narrower,
    square_projector,
    square_scales,
    square_biases,
):
    weights = (embedder, positions, widener, narrower, projector, scales, biases)
    owners = lax.axis_size("fsdp")
    micro_count, images_dev, slot_total, patch_size = pixels.shape
    model_width = embedder.shape[1]
    wide_rows = embedder.shape[0]
    narrow_rows = narrower.shape[0]
    hidden_width = narrow_rows * owners - model_width
    hidden_blocks = hidden_width // model_width
    head_size = model_width // HEADS
    images_all = pairing.shape[1]
    logit_factor = logit_temper * captions.shape[2] ** (-0.5)
    images = micro_count * images_dev
    slots = padded_rows(slot_total)
    spare = slots - slot_total
    rows = images * slots
    pixel_rows = jnp.pad(
        pixels.reshape(images, slot_total, patch_size), ((0, 0), (0, spare), (0, 0))
    )
    slot_map = jnp.pad(
        merge_map.reshape(images, 1, slot_total), ((0, 0), (0, 0), (0, spare)), constant_values=-1
    )
    row_weight = jnp.pad(merge_weight.reshape(images, 1, slot_total), ((0, 0), (0, 0), (0, spare)))
    column_weight = row_weight.reshape(images, slots, 1)
    live_counts = counts.reshape(images)
    f32, low = jnp.float32, jnp.bfloat16
    shape = jax.ShapeDtypeStruct
    place = jnp.stack([lax.axis_index("fsdp"), lax.axis_index("rep")]).astype(jnp.int32)
    bias_rows = biases.shape[0] // wide_rows
    scale_rows = scales.shape[0]
    table_rows = padded_rows(scale_rows + bias_rows)
    small_rows = -(-(slots + table_rows) // 128) * 128
    beside = jnp.concatenate(
        [
            jnp.pad(positions, ((0, spare), (0, 0))),
            scales,
            biases.reshape(bias_rows, wide_rows),
        ]
    )
    beside = jnp.pad(beside, ((0, small_rows - beside.shape[0]), (0, 0))).astype(low)
    small_piece = jnp.concatenate([embedder.astype(low), beside.T], axis=1)
    wide_low = widener.astype(low)
    blocks_of = lambda first, count: [
        wide_low[:, k * model_width : (k + 1) * model_width] for k in range(first, first + count)
    ]
    qkv_piece = jnp.stack(blocks_of(0, 3))
    hidden_piece = jnp.stack(blocks_of(3, hidden_blocks) + [projector.astype(low)])
    narrow_piece = narrower.astype(low)[None]
    small_get = Flow(gather_plain(small_piece[None]))
    small_get.go()
    sent = small_get.go()
    qkv_get = Flow(gather_split(first_behind(qkv_piece, sent)))
    sent = qkv_get.go()
    sent = small_get.go()
    guards = qkv_get.go(sent)
    embed_full, table = assembled_small(place, small_get.finish(), owners, model_width, guards)
    scale_float = table[slots : slots + scale_rows]
    bias_float = jnp.swapaxes(
        table[slots + scale_rows : slots + scale_rows + bias_rows].reshape(
            bias_rows, owners, wide_rows
        ),
        0,
        1,
    ).reshape(-1)
    out_bias = bias_float[hidden_width : hidden_width + model_width].reshape(1, model_width)
    place_bias = table[:slots] + bias_float[hidden_width + model_width :]
    guards = qkv_get.go()
    hidden_get = Flow(gather_split(first_behind(hidden_piece, guards)))
    guards += hidden_get.go()
    merged, normed = image_call(
        embed_kernel,
        images,
        [
            per_image(slots, patch_size),
            per_image(1, slots),
            per_image(1, slots),
            per_image(slots, 1),
            whole(patch_size, model_width),
            whole(slots, model_width),
            whole(1, model_width),
        ]
        + [anywhere] * len(guards),
        [per_image(slots, model_width)] * 2,
        [shape((images, slots, model_width), f32), shape((images, slots, model_width), low)],
        name="embed",
    )(
        live_counts, pixel_rows, slot_map, row_weight, column_weight, embed_full, place_bias,
        scale_float[0:1], *guards,
    )
    qkv_get.go()
    qkv_parts = qkv_get.finish()
    guards = hidden_get.go(qkv_parts[-1][0])
    narrow_get = Flow(gather_split(first_behind(narrow_piece, guards)))
    guards += narrow_get.go()
    arrays, found, size = gathered(qkv_parts)
    normed_rows = normed.reshape(rows, model_width)
    column_block = lambda index_map: block((1, rows, model_width), index_map)
    heads, rstd, wide_qkv = pl.pallas_call(
        functools.partial(widen_heads_kernel, found=found, chunk=slots, head_size=head_size),
        grid_spec=pltpu.PrefetchScalarGridSpec(
            num_scalar_prefetch=1,
            grid=(2,),
            in_specs=[whole(rows, model_width), block((1, 1, model_width), lambda k, _: (k, 0, 0))]
            + [anywhere] * (len(arrays) + len(guards)),
            out_specs=[column_block(lambda k, _: (k, 0, 0))] * 2 + [anywhere],
            scratch_shapes=gather_scratch(found, size),
        ),
        out_shape=[
            shape((2, rows, model_width), low), shape((2, rows, model_width), f32), shape(size, low)
        ],
        compiler_params=roomy,
        cost_estimate=long,
        name="widen_heads",
    )(place, normed_rows, scale_float[2:4].reshape(2, 1, model_width), *arrays, *guards)
    guards = hidden_get.go(heads)
    values = pl.pallas_call(
        widen_value_kernel,
        grid=(1,),
        in_specs=[whole(rows, model_width), block((1, model_width, model_width), lambda k: (2, 0, 0))]
        + [anywhere] * (1 + len(guards)),
        out_specs=column_block(lambda k: (0, 0, 0)),
        out_shape=shape((1, rows, model_width), low),
        compiler_params=roomy,
        cost_estimate=long,
        name="widen_values",
    )(normed_rows, wide_qkv, heads, *guards)
    image_columns = lambda parts: block(
        (parts, slots, model_width), lambda image, counts: (0, image, 0)
    )
    guards = narrow_get.go(heads)
    (attended,) = image_call(
        functools.partial(attend_kernel, head_size=head_size),
        images,
        [image_columns(2), image_columns(1)] + [anywhere] * len(guards),
        [per_image(slots, model_width)],
        [shape((images, slots, model_width), low)],
        name="attend",
    )(live_counts, heads, values, *guards)
    guards = narrow_get.go() + [attended]
    hidden_get.go(guards)
    arrays, found, size = gathered(hidden_get.finish())
    hidden, slope, wide_hidden = pl.pallas_call(
        functools.partial(widen_hidden_kernel, found=found, chunk=slots),
        grid_spec=pltpu.PrefetchScalarGridSpec(
            num_scalar_prefetch=1,
            grid=(hidden_blocks,),
            in_specs=[whole(rows, model_width), block((1, 1, model_width), lambda k, _: (k, 0, 0))]
            + [anywhere] * (len(arrays) + len(guards)),
            out_specs=[column_block(lambda k, _: (k, 0, 0))] * 2 + [anywhere],
            scratch_shapes=gather_scratch(found, size),
        ),
        out_shape=[shape((hidden_blocks, rows, model_width), low)] * 2 + [shape(size, low)],
        compiler_params=roomy,
        cost_estimate=long,
        name="widen_hidden",
    )(
        place, normed_rows, bias_float[:hidden_width].reshape(hidden_blocks, 1, model_width),
        *arrays, *guards,
    )
    project_full = wide_hidden[hidden_blocks]
    narrow_get.go(hidden)
    arrays, found, size = gathered(narrow_get.finish())
    narrow_scratch = [
        pltpu.VMEM((hidden_width + model_width, model_width), low), pltpu.SemaphoreType.DMA
    ]
    stream, pooled, narrow_full = pl.pallas_call(
        functools.partial(join_kernel, found=found),
        grid_spec=pltpu.PrefetchScalarGridSpec(
            num_scalar_prefetch=2,
            grid=(images,),
            in_specs=[
                block((1, slots, model_width), lambda image, *_: (image, 0, 0)),
                block((hidden_blocks, slots, model_width), lambda image, *_: (0, image, 0)),
                block((1, slots, model_width), lambda image, *_: (image, 0, 0)),
                whole(1, model_width),
                whole(1, model_width),
            ]
            + [anywhere] * len(arrays),
            out_specs=[
                block((1, slots, model_width), lambda image, *_: (image, 0, 0)),
                block((1, 1, model_width), lambda image, *_: (image, 0, 0)),
                anywhere,
            ],
            scratch_shapes=gather_scratch(found, size),
        ),
        out_shape=[
            shape((images, slots, model_width), f32),
            shape((images, 1, model_width), f32),
            shape(size, low),
        ],
        compiler_params=roomy,
        cost_estimate=long,
        name="join",
    )(live_counts, place, attended, hidden, merged, out_bias, scale_float[1:2], *arrays)
    narrow_full = narrow_full[0]
    pooled_low = pooled.reshape(images, model_width).astype(low)
    embeds = product(pooled_low, project_full).astype(low)
    embeds = embeds.reshape(micro_count, images_dev, -1)
    logits = jnp.einsum("mie,mje->mij", embeds, captions, preferred_element_type=f32) * logit_factor
    image_ids = jnp.arange(images_all, dtype=jnp.int32)
    first_row = (lax.axis_index("rep") * owners + lax.axis_index("fsdp")) * images_dev
    own_pairs = lax.dynamic_slice_in_dim(pairing, first_row, images_dev, 1)
    target = (own_pairs[:, :, None] == image_ids[None, None, :]).astype(jnp.float32)
    row_top = jnp.max(logits, axis=2, keepdims=True)
    row_logsum = row_top[:, :, 0] + jnp.log(jnp.sum(jnp.exp(logits - row_top), axis=2))
    own_top = jnp.max(logits, axis=1)
    own_total = jnp.sum(jnp.exp(logits - own_top[:, None, :]), axis=1)
    picked = jnp.sum(logits * target, axis=2)
    counts_float = counts.astype(jnp.float32)
    scalars = jnp.concatenate(
        [
            jnp.sum(counts_float * (picked - row_logsum), axis=1),
            jnp.sum(picked, axis=1),
            jnp.sum(counts_float, axis=1),
        ]
    )
    sums = jnp.pad(scalars[None, :], ((0, 0), (0, images_all - scalars.shape[0])))
    column_top, column_total, sums = column_totals(own_top, own_total, sums)
    column_logsum = column_top + jnp.log(column_total)
    row_terms = sums[0, :micro_count]
    picked_sums = sums[0, micro_count : 2 * micro_count]
    weight_totals = sums[0, 2 * micro_count : 3 * micro_count]
    weight_total_all = jnp.sum(weight_totals)
    part_losses = 0.5 * (
        -row_terms / weight_totals - (picked_sums - jnp.sum(column_logsum, axis=1)) / images_all
    )
    objective = jnp.sum(part_losses) / micro_count
    row_soft = jnp.exp(logits - row_logsum[:, :, None])
    column_soft = jnp.exp(logits - column_logsum[:, None, :])
    all_grad_logits = (
        0.5
        / micro_count
        * (
            (counts_float / weight_totals[:, None])[:, :, None] * (row_soft - target)
            + (column_soft - target) / images_all
        )
    )
    grad_product = (all_grad_logits * logit_factor).astype(low)
    grad_embeds = (
        jnp.einsum("mij,mje->mie", grad_product, captions, preferred_element_type=f32)
        .astype(low)
        .reshape(images, -1)
    )
    grad_pooled = product_along(grad_embeds, project_full)
    grad_stream, grad_branch, grad_attended, grad_act, out_sums = image_call(
        branch_kernel,
        images,
        [
            per_image(slots, model_width),
            per_image(1, model_width),
            whole(1, model_width),
            image_columns(hidden_blocks),
            anywhere,
        ],
        [
            per_image(slots, model_width),
            per_image(slots, model_width),
            per_image(slots, model_width),
            image_columns(hidden_blocks),
            whole(8, model_width),
        ],
        [
            shape((images, slots, model_width), f32),
            shape((images, slots, model_width), low),
            shape((images, slots, model_width), low),
            shape((hidden_blocks, rows, model_width), low),
            shape((8, model_width), f32),
        ],
        narrow_scratch,
        name="branch",
    )(
        live_counts, stream, grad_pooled.reshape(images, 1, model_width), scale_float[1:2], slope,
        narrow_full,
    )
    core = (lax.axis_index("fsdp") % 2).reshape(1)
    chips = owners // 2
    branch_rows = grad_branch.reshape(rows, model_width)
    halves = lambda count, width: [shape((chips, count, width), low)] * 2
    narrow_halves = pl.pallas_call(
        narrow_grad_kernel,
        grid_spec=pltpu.PrefetchScalarGridSpec(
            num_scalar_prefetch=1,
            grid=(1 + hidden_blocks,),
            in_specs=[
                whole(rows, model_width),
                block((1, rows, model_width), lambda k, _: (jnp.maximum(k - 1, 0), 0, 0)),
                whole(rows, model_width),
            ],
            out_specs=[anywhere] * 2,
            scratch_shapes=[
                pltpu.VMEM((hidden_width + model_width, model_width), low),
                pltpu.SemaphoreType.DMA((2 * chips,)),
            ],
        ),
        out_shape=halves(narrow_rows, model_width),
        compiler_params=roomy,
        cost_estimate=long,
        name="narrow_grad",
    )(core, attended.reshape(rows, model_width), hidden, branch_rows)
    narrow_flow = Flow(reduce_rows_first(*narrow_halves))
    narrow_flow.go()
    owner_block = block((chips, wide_rows, model_width), lambda k, _: (0, k, 0))
    few = padded_rows(images)
    hidden_halves = pl.pallas_call(
        wide_project_grad_kernel,
        grid_spec=pltpu.PrefetchScalarGridSpec(
            num_scalar_prefetch=1,
            grid=(hidden_blocks + 1,),
            in_specs=[
                whole(rows, model_width),
                block(
                    (1, rows, model_width), lambda k, _: (jnp.minimum(k, hidden_blocks - 1), 0, 0)
                ),
                whole(few, model_width),
                whole(few, model_width),
            ],
            out_specs=[owner_block] * 2,
        ),
        out_shape=halves((hidden_blocks + 1) * wide_rows, model_width),
        compiler_params=roomy,
        cost_estimate=long,
        name="hidden_grad",
    )(
        core, normed_rows, grad_act, jnp.pad(pooled_low, ((0, few - images), (0, 0))),
        jnp.pad(grad_embeds, ((0, few - images), (0, 0))),
    )
    hidden_flow = Flow(reduce_rows_last(*hidden_halves))
    hidden_flow.go()
    parts = images_dev
    per_part = images // parts
    part_rows = per_part * slots

    def shifted(base, rows_count):
        return block((1, rows_count, model_width), lambda image, counts: (base + image, 0, 0))

    def shifted_columns(base, count):
        return block((count, slots, model_width), lambda image, counts: (0, base + image, 0))

    head_gains = scale_float[2:4].reshape(2, 1, model_width)
    guards = narrow_flow.go()
    grad_qkv, head_sums = [], 0.0
    for part in range(parts):
        base = part * per_part
        grads, sums_part = image_call(
            functools.partial(attend_back_kernel, base=base, head_size=head_size),
            per_part,
            [
                shifted_columns(base, 2),
                shifted_columns(base, 1),
                shifted_columns(base, 2),
                shifted(base, slots),
                whole(2, 1, model_width),
            ]
            + [anywhere] * len(guards),
            [image_columns(3), whole(8, model_width)],
            [shape((3, part_rows, model_width), low), shape((8, model_width), f32)],
            [pltpu.VMEM((2, slots, model_width), f32)],
            name="attend_back",
        )(live_counts, heads, values, rstd, grad_attended, head_gains, *guards)
        grad_qkv.append(grads)
        head_sums = head_sums + sums_part
        guards = [grads]
        if part == 0:
            guards += hidden_flow.go(grads)
    guards += narrow_flow.go(grads)
    qkv_halves = pl.pallas_call(
        lambda core_ref, normed_ref, *refs: wide_grad_kernel(
            core_ref, normed_ref, *refs[:parts], *refs[-2:]
        ),
        grid_spec=pltpu.PrefetchScalarGridSpec(
            num_scalar_prefetch=1,
            grid=(3,),
            in_specs=[whole(rows, model_width)]
            + [block((1, part_rows, model_width), lambda k, _: (k, 0, 0))] * parts
            + [anywhere] * len(guards),
            out_specs=[owner_block] * 2,
        ),
        out_shape=halves(3 * wide_rows, model_width),
        compiler_params=roomy,
        cost_estimate=long,
        name="qkv_grad",
    )(core, normed_rows, *grad_qkv, *guards)
    qkv_flow = Flow(reduce_rows_first(*qkv_halves))
    guards = qkv_flow.go()
    grad_patches, grad_places, merge_sums = [], [], 0.0
    for part in range(parts):
        base = part * per_part
        grads, place_part, sums_part = image_call(
            functools.partial(merge_back_kernel, base=base),
            per_part,
            [
                image_columns(3),
                shifted_columns(base, hidden_blocks),
                anywhere,
                anywhere,
                shifted(base, slots),
                shifted(base, slots),
                whole(1, model_width),
                block((1, 1, slots), lambda image, counts, base=base: (base + image, 0, 0)),
                block((1, 1, slots), lambda image, counts, base=base: (base + image, 0, 0)),
                block((1, slots, 1), lambda image, counts, base=base: (base + image, 0, 0)),
            ]
            + [anywhere] * len(guards),
            [per_image(slots, model_width), whole(slots, model_width), whole(8, model_width)],
            [
                shape((per_part, slots, model_width), low),
                shape((slots, model_width), f32),
                shape((8, model_width), f32),
            ],
            [
                pltpu.VMEM((3 + hidden_blocks, model_width, model_width), low),
                pltpu.SemaphoreType.DMA((3 + hidden_blocks,)),
            ],
            name="merge_back",
        )(
            live_counts, grad_qkv[part], grad_act, wide_qkv, wide_hidden, merged, grad_stream,
            scale_float[0:1], slot_map, row_weight, column_weight, *guards,
        )
        grad_patches.append(grads.reshape(part_rows, model_width))
        grad_places.append(place_part)
        merge_sums = merge_sums + sums_part
        guards = [grads]
        if part == 0:
            guards += hidden_flow.go(grads) + qkv_flow.go(grads)
        elif part == 1:
            guards += narrow_flow.go(grads)
    guards += hidden_flow.go(grads) + qkv_flow.go(grads)
    grad_scale = jnp.stack([merge_sums[0], out_sums[hidden_blocks + 1], head_sums[0], head_sums[1]])
    grad_bias = jnp.concatenate([out_sums[: hidden_blocks + 1], merge_sums[1:2]]).reshape(
        owners, bias_rows, wide_rows
    )
    grad_bias = jnp.swapaxes(grad_bias, 0, 1).reshape(bias_rows, model_width)
    table = jnp.concatenate([grad_scale, grad_bias])
    table = jnp.pad(table, ((0, padded_rows(table.shape[0]) - table.shape[0]), (0, 0)))
    piece_width = small_piece.shape[1]
    embed_halves = pl.pallas_call(
        lambda core_ref, pixel_ref, *refs: embed_grad_kernel(
            core_ref, pixel_ref, *refs[: 2 * parts + 1], *refs[-2:]
        ),
        grid_spec=pltpu.PrefetchScalarGridSpec(
            num_scalar_prefetch=1,
            grid=(1,),
            in_specs=[whole(rows, patch_size)]
            + [whole(part_rows, model_width)] * parts
            + [whole(slots, model_width)] * parts
            + [whole(*table.shape)]
            + [anywhere] * len(guards),
            out_specs=[whole(chips, wide_rows, piece_width)] * 2,
        ),
        out_shape=halves(wide_rows, piece_width),
        compiler_params=roomy,
        cost_estimate=long,
        name="embed_grad",
    )(core, pixel_rows.reshape(rows, patch_size), *grad_patches, *grad_places, table, *guards)
    embed_flow = Flow(reduce_rows_last(*embed_halves))
    flows = (narrow_flow, hidden_flow, qkv_flow, embed_flow)
    while any(flow.result is None for flow in flows):
        for flow in flows:
            if flow.result is None:
                flow.go()
    shards = [flow.result for flow in flows]
    squares_sum = pl.pallas_call(
        square_kernel,
        out_shape=shape((8, 128), f32),
        compiler_params=roomy,
        name="squares",
    )(*shards)
    squares_sum = sum_over(squares_sum, "fsdp")
    total_norm = jnp.sqrt(squares_sum[0, 0])
    moments = (
        moment_embedder,
        moment_positions,
        moment_widener,
        moment_narrower,
        moment_projector,
        moment_scales,
        moment_biases,
    )
    squares = (
        square_embedder,
        square_positions,
        square_widener,
        square_narrower,
        square_projector,
        square_scales,
        square_biases,
    )
    as_rows = lambda arrays: [
        array.reshape(-1, wide_rows) if array.ndim == 1 else array for array in arrays
    ]
    outs = pl.pallas_call(
        functools.partial(update_kernel, wide_rows=wide_rows),
        out_shape=[shape(array.shape, f32) for array in as_rows(weights) * 2],
        compiler_params=roomy,
        name="update",
    )(squares_sum, *shards, *as_rows(weights), *as_rows(moments), *as_rows(squares))
    outs = [
        out.reshape(array.shape) for out, array in zip(outs, weights * 2, strict=True)
    ]
    return (objective, weight_total_all, total_norm, *outs)


def solution(mesh):
    return jax.shard_map(
        per_device,
        mesh=mesh,
        in_specs=(
            P(None, ("rep", "fsdp"), None, None),
            P(None, ("rep", "fsdp"), None),
            P(None, ("rep", "fsdp"), None),
            P(None, ("rep", "fsdp")),
            P(),
            P(),
            P("fsdp", None),
            P(None, "fsdp"),
            P("fsdp", None),
            P("fsdp", None),
            P("fsdp", None),
            P(None, "fsdp"),
            P("fsdp"),
            P("fsdp", None),
            P(None, "fsdp"),
            P("fsdp", None),
            P("fsdp", None),
            P("fsdp", None),
            P(None, "fsdp"),
            P("fsdp"),
            P("fsdp", None),
            P(None, "fsdp"),
            P("fsdp", None),
            P("fsdp", None),
            P("fsdp", None),
            P(None, "fsdp"),
            P("fsdp"),
        ),
        out_specs=(
            P(),
            P(),
            P(),
            P("fsdp", None),
            P(None, "fsdp"),
            P("fsdp", None),
            P("fsdp", None),
            P("fsdp", None),
            P(None, "fsdp"),
            P("fsdp"),
            P("fsdp", None),
            P(None, "fsdp"),
            P("fsdp", None),
            P("fsdp", None),
            P("fsdp", None),
            P(None, "fsdp"),
            P("fsdp"),
        ),
        check_vma=False,
    )
```

```python
import functools

import jax
import jax.numpy as jnp
from jax import lax
from jax.experimental import pallas as pl
from jax.experimental.pallas import tpu as pltpu
from jax.sharding import PartitionSpec as P

HEADS = 12


norm_eps = 1e-06
clip_bound = 0.1
beta_first = 0.9
beta_second = 0.999
learn_rate = 0.03
weight_decay = 0.1
adam_eps = 1e-08
step_number = 10
logit_temper = 10.0


def product(left, right):
    return jnp.dot(left, right, preferred_element_type=jnp.float32)


def product_across(left, right):
    return lax.dot_general(
        left, right, (((0,), (0,)), ((), ())), preferred_element_type=jnp.float32
    )


def product_along(left, right):
    return lax.dot_general(
        left, right, (((1,), (1,)), ((), ())), preferred_element_type=jnp.float32
    )


def adam_step(weight, gradient, moment, square, factor):
    clipped = gradient * factor
    moment_new = beta_first * moment + (1.0 - beta_first) * clipped
    square_new = beta_second * square + (1.0 - beta_second) * clipped * clipped
    mean_hat = moment_new / (1.0 - beta_first**step_number)
    square_hat = square_new / (1.0 - beta_second**step_number)
    change = -learn_rate * (mean_hat / (jnp.sqrt(square_hat) + adam_eps) + weight_decay * weight)
    return (change, clipped)


def bit_swap(size, bit):
    return [(index, index ^ bit) for index in range(size)]


def ordered_pair(own, other, axis, bit):
    low_side = (lax.axis_index(axis) & bit) == 0
    return jnp.where(low_side, own, other), jnp.where(low_side, other, own)


def combined(first, second, micro_count):
    top_a, top_b = first[:micro_count], second[:micro_count]
    top = jnp.maximum(top_a, top_b)
    parts = slice(micro_count, 2 * micro_count)
    total = first[parts] * jnp.exp(top_a - top) + second[parts] * jnp.exp(top_b - top)
    return jnp.concatenate([top, total, first[2 * micro_count :] + second[2 * micro_count :]])


def column_totals(top, total, sums):
    micro_count = top.shape[0]
    packed = jnp.concatenate([top, total, sums], axis=0)
    owners, reps = lax.axis_size("fsdp"), lax.axis_size("rep")
    steps = [("fsdp", owners, 1), ("fsdp", owners, 2)]
    steps += [("rep", reps, 1 << bit) for bit in range(reps.bit_length() - 1)]
    for axis, size, bit in steps:
        other = lax.ppermute(packed, axis, bit_swap(size, bit))
        packed = combined(*ordered_pair(packed, other, axis, bit), micro_count)
    turns = [packed] + [
        lax.ppermute(packed, "fsdp", bit_swap(owners, turn)) for turn in range(4, owners, 4)
    ]
    bit = 4
    while len(turns) > 1:
        turns = [
            combined(*ordered_pair(first, second, "fsdp", bit), micro_count)
            for first, second in zip(turns[::2], turns[1::2], strict=True)
        ]
        bit *= 2
    packed = turns[0]
    return packed[:micro_count], packed[micro_count : 2 * micro_count], packed[2 * micro_count :]


def sum_over(value, axis):
    size = lax.axis_size(axis)
    for bit in (1, 2):
        value = value + lax.ppermute(value, axis, bit_swap(size, bit))
    turns = [value] + [
        lax.ppermute(value, axis, bit_swap(size, turn)) for turn in range(4, size, 4)
    ]
    while len(turns) > 1:
        turns = [first + second for first, second in zip(turns[::2], turns[1::2], strict=True)]
    return turns[0]


def padded_rows(rows):
    return -(-rows // 16) * 16


def split_two(values):
    high = values.astype(jnp.bfloat16)
    return high, (values - high.astype(jnp.float32)).astype(jnp.bfloat16)


def normal_rows(values):
    center = values - jnp.mean(values, axis=-1, keepdims=True)
    rstd = lax.rsqrt(jnp.mean(center * center, axis=-1, keepdims=True) + norm_eps)
    return center * rstd, rstd


def head_mixer(head_size):
    row = lax.broadcasted_iota(jnp.int32, (256, 256), 0) // head_size
    column = lax.broadcasted_iota(jnp.int32, (256, 256), 1) // head_size
    return jnp.where(row == column, 1.0 / head_size, 0.0).astype(jnp.bfloat16)


def head_mean(values, mixer):
    parts = []
    for at in range(0, values.shape[1], 256):
        high, low = split_two(values[:, at : at + 256])
        parts.append(product(high, mixer) + product(low, mixer))
    return jnp.concatenate(parts, axis=1)


def embed_kernel(
    counts_ref, pixel_ref, map_ref, row_ref, column_ref, embed_ref, place_ref, gain_ref, *refs
):
    merged_ref, normed_ref = refs[-2:]
    live_count = counts_ref[pl.program_id(0)]
    slots = merged_ref.shape[1]
    patches = product(pixel_ref[0], embed_ref[...]) + place_ref[...]
    high, low = split_two(patches * column_ref[0])
    slot = lax.broadcasted_iota(jnp.int32, (slots, slots), 0)
    member = slot == map_ref[0]
    hot = jnp.where(member, 1.0, 0.0).astype(jnp.bfloat16)
    total = jnp.sum(jnp.where(member, row_ref[0], 0.0), axis=1, keepdims=True)
    vacant = lax.broadcasted_iota(jnp.int32, (slots, 1), 0) >= live_count
    total = total + jnp.where(vacant, 1.0, 0.0)
    merged = (product(hot, high) + product(hot, low)) / total
    merged_ref[0] = merged
    unit, _ = normal_rows(merged)
    normed_ref[0] = (unit * gain_ref[...]).astype(jnp.bfloat16)


def gelu_pair(values):
    share = 0.5 + 0.5 * lax.erf(values * 0.7071067811865476)
    bell = jnp.exp(-0.5 * values * values)
    return values * share, share + values * bell * 0.3989422804014327


def widen_heads_kernel(
    place_ref, normed_ref, gain_ref, *refs, found, chunk, head_size
):
    heads_ref, rstd_ref, wide_hbm, held_ref, sem, out_sem = refs[-6:]
    sources = refs[: len(found)]
    step = pl.program_id(0)
    keep = pltpu.make_async_copy(held_ref, wide_hbm, out_sem)

    @pl.when(step == 0)
    def _():
        fetch(place_ref, sources, found, held_ref, sem)
        fetched(place_ref, sources, found, held_ref, sem)
        keep.start()

    chunks = normed_ref.shape[0] // chunk
    mixer = head_mixer(head_size)
    gain = gain_ref[0]
    for index in range(chunks):
        rows = slice(index * chunk, (index + 1) * chunk)
        values = product(normed_ref[rows, :], held_ref[step])
        center = values - head_mean(values, mixer)
        rstd = lax.rsqrt(head_mean(center * center, mixer) + norm_eps)
        rstd_ref[0, rows, :] = rstd
        heads_ref[0, rows, :] = (center * rstd * gain).astype(jnp.bfloat16)

    pl.when(step == pl.num_programs(0) - 1)(keep.wait)


def widen_value_kernel(normed_ref, wide_ref, *refs):
    values_ref = refs[-1]
    values_ref[0] = product(normed_ref[...], wide_ref[0]).astype(jnp.bfloat16)


def widen_hidden_kernel(place_ref, normed_ref, bias_ref, *refs, found, chunk):
    hidden_ref, slope_ref, wide_hbm, held_ref, sem, out_sem = refs[-6:]
    sources = refs[: len(found)]
    step = pl.program_id(0)
    keep = pltpu.make_async_copy(held_ref, wide_hbm, out_sem)

    @pl.when(step == 0)
    def _():
        fetch(place_ref, sources, found, held_ref, sem)
        fetched(place_ref, sources, found, held_ref, sem)
        keep.start()

    for index in range(normed_ref.shape[0] // chunk):
        rows = slice(index * chunk, (index + 1) * chunk)
        values = product(normed_ref[rows, :], held_ref[step]) + bias_ref[0]
        hidden, slope = gelu_pair(values)
        hidden_ref[0, rows, :] = hidden.astype(jnp.bfloat16)
        slope_ref[0, rows, :] = slope.astype(jnp.bfloat16)

    pl.when(step == pl.num_programs(0) - 1)(keep.wait)


def head_groups(width, pair):
    starts = range(0, width, 2 * pair)
    return [[slice(at, at + pair), slice(at + pair, at + 2 * pair)] for at in starts]


def by_head(pairs, first_half):
    items = []
    for both in pairs:
        zero = jnp.zeros_like(both)
        items += [jnp.where(first_half, both, zero), jnp.where(first_half, zero, both)]
    return items


def attend_kernel(counts_ref, heads_ref, values_ref, *refs, head_size):
    attended_ref = refs[-1]
    live_count = counts_ref[pl.program_id(0)]
    slots, width = attended_ref.shape[1:]
    factor = head_size ** (-0.5) * 1.4426950408889634
    key_live = jnp.where(
        lax.broadcasted_iota(jnp.int32, (1, slots), 1) < live_count, 1.0, 0.0
    )
    pair = 2 * head_size
    first_half = lax.broadcasted_iota(jnp.int32, (slots, pair), 1) < head_size
    for columns in head_groups(width, pair):
        queries, keys = ([heads_ref[part, :, at] for at in columns] for part in range(2))
        values = [values_ref[0, :, at] for at in columns]
        own = by_head(queries, first_half)
        each = range(len(own))
        weights = [product_along(own[h], keys[h // 2]) for h in each]
        weights = [jnp.exp2(weights[h] * factor) * key_live for h in each]
        share = [
            weights[h] * (1.0 / jnp.sum(weights[h], axis=1, keepdims=True)) for h in each
        ]
        outs = [product(share[h].astype(jnp.bfloat16), values[h // 2]) for h in each]
        for index, at in enumerate(columns):
            attended_ref[0, :, at] = jnp.where(
                first_half, outs[2 * index], outs[2 * index + 1]
            ).astype(jnp.bfloat16)


def join_kernel(
    counts_ref, place_ref, attended_ref, hidden_ref, merged_ref, bias_ref, gain_ref, *refs, found
):
    stream_ref, pooled_ref, narrow_hbm, held_ref, sem, out_sem = refs[-6:]
    sources = refs[: len(found)]
    image = pl.program_id(0)
    live_count = counts_ref[image]
    slots, width = merged_ref.shape[1:]
    keep = pltpu.make_async_copy(held_ref, narrow_hbm, out_sem)

    @pl.when(image == 0)
    def _():
        fetch(place_ref, sources, found, held_ref, sem)
        fetched(place_ref, sources, found, held_ref, sem)
        keep.start()

    stream = merged_ref[0] + bias_ref[...]
    for k in range(1 + hidden_ref.shape[0]):
        left = attended_ref[0] if k == 0 else hidden_ref[k - 1]
        stream = stream + product(left, held_ref[0, k * width : (k + 1) * width, :])
    stream_ref[0] = stream
    unit, _ = normal_rows(stream)
    live = lax.broadcasted_iota(jnp.int32, (slots, 1), 0) < live_count
    total = jnp.sum(jnp.where(live, unit, 0.0), axis=0, keepdims=True)
    pooled_ref[0] = total * gain_ref[...] / live_count.astype(jnp.float32)

    pl.when(image == pl.num_programs(0) - 1)(keep.wait)


def branch_kernel(
    counts_ref, stream_ref, grad_pooled_ref, gain_ref, slope_ref, narrow_hbm,
    grad_stream_ref, grad_branch_ref, grad_attended_ref, grad_act_ref, sums_ref, narrow_ref, sem,
):
    image = pl.program_id(0)
    live_count = counts_ref[image]
    slots, width = stream_ref.shape[1:]
    copy = pltpu.make_async_copy(narrow_hbm, narrow_ref, sem)

    @pl.when(image == 0)
    def _():
        copy.start()
        sums_ref[...] = jnp.zeros_like(sums_ref)

    unit, rstd = normal_rows(stream_ref[0])
    live = lax.broadcasted_iota(jnp.int32, (slots, 1), 0) < live_count
    above = grad_pooled_ref[0] / live_count.astype(jnp.float32)
    slanted = above * gain_ref[...]
    mean_first = jnp.mean(slanted, axis=-1, keepdims=True)
    mean_second = jnp.mean(slanted * unit, axis=-1, keepdims=True)
    grad_stream = jnp.where(live, rstd * (slanted - mean_first - unit * mean_second), 0.0)
    grad_stream_ref[0] = grad_stream
    grad_branch = grad_stream.astype(jnp.bfloat16)
    grad_branch_ref[0] = grad_branch
    parts = slope_ref.shape[0]
    sums_ref[parts : parts + 1, :] += jnp.sum(grad_stream, axis=0, keepdims=True)
    sums_ref[parts + 1 : parts + 2, :] += above * jnp.sum(
        jnp.where(live, unit, 0.0), axis=0, keepdims=True
    )

    @pl.when(image == 0)
    def _():
        copy.wait()

    grad_attended_ref[0] = product_along(grad_branch, narrow_ref[:width, :]).astype(jnp.bfloat16)
    for part in range(parts):
        grad_act = product_along(
            grad_branch, narrow_ref[(part + 1) * width : (part + 2) * width, :]
        ) * slope_ref[part].astype(jnp.float32)
        grad_act_ref[part] = grad_act.astype(jnp.bfloat16)
        sums_ref[part : part + 1, :] += jnp.sum(grad_act, axis=0, keepdims=True)


def attend_back_kernel(
    counts_ref, heads_ref, values_ref, rstd_ref, grad_attended_ref, gain_ref, *refs, base, head_size
):
    grad_qkv_ref, sums_ref, grad_ref = refs[-3:]
    image = pl.program_id(0)
    live_count = counts_ref[base + image]
    slots, width = grad_attended_ref.shape[1:]

    @pl.when(image == 0)
    def _():
        sums_ref[...] = jnp.zeros_like(sums_ref)

    factor = head_size ** (-0.5)
    key_live = lax.broadcasted_iota(jnp.int32, (slots, 1), 0) < live_count
    pair = 2 * head_size
    first_half = lax.broadcasted_iota(jnp.int32, (slots, pair), 1) < head_size
    for columns in head_groups(width, pair):
        queries, keys = ([heads_ref[part, :, at] for at in columns] for part in range(2))
        values = [values_ref[0, :, at] for at in columns]
        own_queries = by_head(queries, first_half)
        own_above = by_head([grad_attended_ref[0, :, at] for at in columns], first_half)
        each = range(len(own_queries))
        weights = [product_along(keys[h // 2], own_queries[h]) for h in each]
        grad_share = [product_along(values[h // 2], own_above[h]) for h in each]
        weights = [
            jnp.where(key_live, jnp.exp2(weights[h] * (factor * 1.4426950408889634)), 0.0)
            for h in each
        ]
        share = [weights[h] * (1.0 / jnp.sum(weights[h], axis=0, keepdims=True)) for h in each]
        dot_row = [jnp.sum(share[h] * grad_share[h], axis=0, keepdims=True) for h in each]
        grad_raw = [
            (share[h] * (grad_share[h] - dot_row[h]) * factor).astype(jnp.bfloat16) for h in each
        ]
        share = [share[h].astype(jnp.bfloat16) for h in each]
        for index, at in enumerate(columns):
            one, two = 2 * index, 2 * index + 1
            grad_qkv_ref[2, :, at] = (
                product(share[one], own_above[one]) + product(share[two], own_above[two])
            ).astype(jnp.bfloat16)
            grad_ref[1, :, at] = product(grad_raw[one], own_queries[one]) + product(
                grad_raw[two], own_queries[two]
            )
            grad_ref[0, :, at] = jnp.where(
                first_half,
                product_across(grad_raw[one], keys[index]),
                product_across(grad_raw[two], keys[index]),
            )
    mixer = head_mixer(head_size)
    for part in range(2):
        gain = gain_ref[part]
        above = grad_ref[part]
        unit = heads_ref[part].astype(jnp.float32) / gain
        sums_ref[part : part + 1, :] += jnp.sum(above * unit, axis=0, keepdims=True)
        slanted = above * gain
        back = slanted - head_mean(slanted, mixer) - unit * head_mean(slanted * unit, mixer)
        grad_qkv_ref[part] = (rstd_ref[part] * back).astype(jnp.bfloat16)


def hidden_back_kernel(grad_act_ref, wide_ref, *refs):
    out_ref, total_ref = refs[-2:]
    step = pl.program_id(0)
    term = product_along(grad_act_ref[0], wide_ref[0])

    @pl.when(step == 0)
    def _():
        total_ref[...] = term

    @pl.when(step > 0)
    def _():
        total_ref[...] += term

    @pl.when(step == pl.num_programs(0) - 1)
    def _():
        out_ref[...] = total_ref[...]


def merge_back_kernel(
    counts_ref, grad_qkv_ref, grad_hidden_ref, wide_hbm, merged_ref, grad_stream_ref, gain_ref,
    map_ref, row_ref, column_ref, *refs, base,
):
    grad_patch_ref, grad_place_ref, sums_ref, wide_ref, sem = refs[-5:]
    image = pl.program_id(0)
    live_count = counts_ref[base + image]
    slots, width = merged_ref.shape[1:]
    blocks = wide_ref.shape[0]
    copies = [
        pltpu.make_async_copy(wide_hbm.at[part], wide_ref.at[part], sem.at[part])
        for part in range(blocks)
    ]

    @pl.when(image == 0)
    def _():
        for copy in copies:
            copy.start()
        sums_ref[...] = jnp.zeros_like(sums_ref)
        grad_place_ref[...] = jnp.zeros_like(grad_place_ref)

    grad_normed = grad_hidden_ref[...]
    for part in range(blocks):
        pl.when(image == 0)(copies[part].wait)
        grad_normed = grad_normed + product_along(grad_qkv_ref[part], wide_ref[part])
    unit, rstd = normal_rows(merged_ref[0])
    sums_ref[0:1, :] += jnp.sum(grad_normed * unit, axis=0, keepdims=True)
    slanted = grad_normed * gain_ref[...]
    back = (
        slanted
        - jnp.mean(slanted, axis=-1, keepdims=True)
        - unit * jnp.mean(slanted * unit, axis=-1, keepdims=True)
    )
    grad_merged = grad_stream_ref[0] + rstd * back
    slot = lax.broadcasted_iota(jnp.int32, (slots, slots), 0)
    member = slot == map_ref[0]
    hot = jnp.where(member, 1.0, 0.0).astype(jnp.bfloat16)
    total = jnp.sum(jnp.where(member, row_ref[0], 0.0), axis=1, keepdims=True)
    vacant = lax.broadcasted_iota(jnp.int32, (slots, 1), 0) >= live_count
    total = total + jnp.where(vacant, 1.0, 0.0)
    high, low = split_two(grad_merged / total)
    grad_patches = (product_across(hot, high) + product_across(hot, low)) * column_ref[0]
    grad_patch_ref[0] = grad_patches.astype(jnp.bfloat16)
    grad_place_ref[...] += grad_patches
    sums_ref[1:2, :] += jnp.sum(grad_patches, axis=0, keepdims=True)


def block(shape, index_map):
    return pl.BlockSpec(shape, index_map)


def per_image(rows, width):
    return block((1, rows, width), lambda image, counts: (image, 0, 0))


def whole(*shape):
    return block(shape, lambda *_: (0,) * len(shape))


anywhere = pl.BlockSpec(memory_space=pl.ANY)
roomy = pltpu.CompilerParams(vmem_limit_bytes=60 * 1024 * 1024)


long = pl.CostEstimate(flops=60_000_000_000, bytes_accessed=1000, transcendentals=0)


def image_call(kernel, images, in_specs, out_specs, out_shape, scratch=(), name=None):
    return pl.pallas_call(
        kernel,
        grid_spec=pltpu.PrefetchScalarGridSpec(
            num_scalar_prefetch=1,
            grid=(images,),
            in_specs=in_specs,
            out_specs=out_specs,
            scratch_shapes=list(scratch),
        ),
        out_shape=out_shape,
        compiler_params=roomy,
        cost_estimate=long,
        name=name,
    )


def picked(terms, axis, index):
    return [lax.dynamic_index_in_dim(term, index, axis, keepdims=False) for term in terms]


def added(terms):
    total = terms[0].astype(jnp.float32)
    for term in terms[1:]:
        total = total + term.astype(jnp.float32)
    return total


def behind(terms, after):
    if after is None:
        return terms
    return lax.optimization_barrier((terms, after))[0]


def traded(terms, axis, index, count, mesh_axis, stride):
    size = lax.axis_size(mesh_axis)
    sends = [
        added(picked(terms, axis, index ^ turn)).astype(jnp.bfloat16) for turn in range(1, count)
    ]
    after = yield sends
    got = [
        lax.ppermute(send, mesh_axis, bit_swap(size, turn * stride))
        for turn, send in enumerate(sends, 1)
    ]
    return picked(terms, axis, index) + behind(got, after)


def core_terms(mine, other):
    after = yield [other]
    got = behind([core_swap(other)], after)[0]
    return [
        term.reshape(*term.shape[:-3], term.shape[-3] // 2, 2, *term.shape[-2:])
        for term in (mine, got)
    ]


def rep_swap(own):
    return lax.ppermute(own, "rep", bit_swap(2, 1))


def places():
    place = lax.axis_index("fsdp")
    return place // 4, (place // 2) % 2


def column_parts(width):
    reps = lax.axis_size("rep")
    return reps if width % (128 * reps) == 0 else 1


def reduce_columns(mine, other):
    high, middle = places()
    parts, count = mine.shape[0], mine.shape[1] // 2
    terms = yield from core_terms(mine, other)
    if parts > 1:
        terms = yield from traded(terms, 0, lax.axis_index("rep"), parts, "rep", 1)
    else:
        terms = [term[0] for term in terms]
    terms = yield from traded(terms, 1, middle, 2, "fsdp", 2)
    terms = yield from traded(terms, 0, high, count, "fsdp", 4)
    own = added(terms).astype(jnp.bfloat16)
    after = yield [own]
    if parts == 1:
        return lax.psum(own, "rep")
    if parts == 2:
        got = behind([rep_swap(own)], after)[0]
        first, second = ordered_pair(own, got, "rep", 1)
        return jnp.concatenate([first, second], axis=1)
    return lax.all_gather(own, "rep", axis=1, tiled=True)


def reduce_rows_last(mine, other):
    high, middle = places()
    count = mine.shape[0] // 2
    terms = yield from core_terms(mine, other)
    terms = yield from traded(terms, 1, middle, 2, "fsdp", 2)
    terms = yield from traded(terms, 0, high, count, "fsdp", 4)
    own = added(terms).astype(jnp.bfloat16)
    after = yield [own]
    if lax.axis_size("rep") == 2:
        got = behind([rep_swap(own)], after)
        return added([own, *got]).astype(jnp.bfloat16)
    return lax.psum(own, "rep")


def core_swap(own):
    return lax.ppermute(own, "fsdp", bit_swap(lax.axis_size("fsdp"), 1))


def middle_swap(own):
    return lax.ppermute(own, "fsdp", bit_swap(lax.axis_size("fsdp"), 2))


def high_gather(own):
    owners = lax.axis_size("fsdp")
    after = yield [own]
    got = [lax.ppermute(own, "fsdp", bit_swap(owners, turn)) for turn in range(4, owners, 4)]
    return [own] + behind(got, after)


def with_cores(found):
    after = yield [item[0] for item in found]
    got = behind([core_swap(item[0]) for item in found], after)
    return found + [
        (array, [turn + 1 for turn in turns], parts)
        for array, (_, turns, parts) in zip(got, found, strict=True)
    ]


def gather_plain(own):
    after_high = yield from high_gather(own)
    near = jnp.stack(after_high)
    turns = list(range(0, lax.axis_size("fsdp"), 4))
    after = yield [near]
    far = behind([middle_swap(near)], after)[0]
    whole_rows = [None] * len(turns)
    found = [(near, turns, whole_rows), (far, [turn + 2 for turn in turns], whole_rows)]
    return (yield from with_cores(found))


def own_columns(own):
    half = own.shape[-1] // 2
    return lax.dynamic_slice_in_dim(own, lax.axis_index("rep") * half, half, own.ndim - 1)


def gather_split(own):
    if lax.axis_size("rep") != 2:
        return (yield from gather_plain(own))
    after_high = yield from high_gather(own_columns(own))
    turns = list(range(0, lax.axis_size("fsdp"), 4))
    cut = len(turns) // 2
    early, late = jnp.stack(after_high[:cut]), jnp.stack(after_high[cut:])
    after = yield [early, late]
    got = behind([rep_swap(early), middle_swap(late)], after)
    early, late = (jnp.concatenate(pair) for pair in zip((early, late), got, strict=True))
    after = yield [early, late]
    got = [middle_swap(early), rep_swap(late)]
    early, late, *got = behind([early, late, *got], after if after is not None else ())
    far = lambda some: [turn + 2 for turn in some]
    first, second = turns[:cut], turns[cut:]
    near_parts, all_parts = [0] * cut + [1] * cut, [0] * (2 * cut)
    found = [
        (early, first + first, near_parts),
        (got[0], far(first + first), near_parts),
        (late, second + far(second), all_parts),
        (got[1], second + far(second), [1] * (2 * cut)),
    ]
    return (yield from with_cores(found))


def assemble_copies(place_ref, sources, found, out_ref, columns, sem):
    copies = []
    for source, (turns, parts) in zip(sources, found, strict=True):
        rows, width = source.shape[2:]
        for slot, (turn, part) in enumerate(zip(turns, parts, strict=True)):
            owner = place_ref[0] ^ turn
            row = pl.ds(pl.multiple_of(owner * rows, rows), rows)
            if part is None:
                piece, target = source.at[slot, :, :, columns], out_ref.at[:, row, :]
            else:
                side = pl.ds(pl.multiple_of((place_ref[1] ^ part) * width, width), width)
                piece, target = source.at[slot], out_ref.at[:, row, side]
            copies.append(pltpu.make_async_copy(piece, target, sem.at[len(copies)]))
    return copies


def gathered(items):
    arrays = [item[0] for item in items]
    found = tuple((tuple(item[1]), tuple(item[2])) for item in items)
    segments, rows, width = arrays[0].shape[1:]
    if found[0][1][0] is not None:
        width = 2 * width
    owners = sum(len(item[0]) for item in found) * arrays[0].shape[3] // width
    return arrays, found, (segments, owners * rows, width)


def gather_scratch(found, size):
    return [
        pltpu.VMEM(size, jnp.bfloat16),
        pltpu.SemaphoreType.DMA((sum(len(item[0]) for item in found),)),
        pltpu.SemaphoreType.DMA,
    ]


def fetch(place_ref, sources, found, held_ref, sem):
    for copy in assemble_copies(place_ref, sources, found, held_ref, slice(None), sem):
        copy.start()


def fetched(place_ref, sources, found, held_ref, sem):
    for copy in assemble_copies(place_ref, sources, found, held_ref, slice(None), sem):
        copy.wait()


def assemble_small_kernel(place_ref, *refs, found, width):
    embed_ref, beside_out_ref, beside_ref, sem, beside_sem = refs[-5:]
    sources = refs[: len(found)]
    first = slice(0, width)
    second = slice(width, sources[0].shape[3])
    copies = assemble_copies(place_ref, sources, found, embed_ref, first, sem)
    copies += assemble_copies(place_ref, sources, found, beside_ref, second, beside_sem)
    for copy in copies:
        copy.start()
    for copy in copies:
        copy.wait()
    beside_out_ref[...] = beside_ref[0].astype(jnp.float32).T


def assembled_small(place, items, owners, width, guards):
    arrays, found, _ = gathered(items)
    rows, whole_width = arrays[0].shape[2:]
    beside = whole_width - width
    count = sum(len(item[0]) for item in found)
    embed, table = pl.pallas_call(
        lambda place_ref, *refs: assemble_small_kernel(
            place_ref, *refs[: len(arrays)], *refs[-5:], found=found, width=width
        ),
        grid_spec=pltpu.PrefetchScalarGridSpec(
            num_scalar_prefetch=1,
            grid=(1,),
            in_specs=[anywhere] * (len(arrays) + len(guards)),
            out_specs=[whole(1, owners * rows, width), whole(beside, owners * rows)],
            scratch_shapes=[
                pltpu.VMEM((1, owners * rows, beside), jnp.bfloat16),
                pltpu.SemaphoreType.DMA((count,)),
                pltpu.SemaphoreType.DMA((count,)),
            ],
        ),
        out_shape=[
            jax.ShapeDtypeStruct((1, owners * rows, width), jnp.bfloat16),
            jax.ShapeDtypeStruct((beside, owners * rows), jnp.float32),
        ],
        compiler_params=roomy,
        cost_estimate=long,
        name="assemble_small",
    )(place, *arrays, *guards)
    return embed[0], table


def first_behind(value, after):
    return lax.optimization_barrier((value, after))[0]


class Flow:
    def __init__(self, steps):
        self.steps, self.result = steps, None

    def go(self, after=None):
        try:
            return self.steps.send(after)
        except StopIteration as end:
            self.result = end.value
            return []

    def finish(self):
        while self.result is None:
            self.go()
        return self.result


def split_cores(result, core, mine_ref, other_ref):
    chips, rows, width = mine_ref.shape[-3:]
    pairs = result.astype(jnp.bfloat16).reshape(chips, 2, rows, result.shape[1])
    first, second = pairs[:, 0], pairs[:, 1]
    for ref, (left, right) in ((mine_ref, (first, second)), (other_ref, (second, first))):
        values = jnp.where(core == 0, left, right)
        if len(ref.shape) == 3:
            ref[...] = values
        else:
            for part in range(ref.shape[0]):
                ref[part] = values[:, :, part * width : (part + 1) * width]


def narrow_grad_kernel(
    core_ref, attended_ref, hidden_ref, branch_ref, mine_hbm, other_hbm, total_ref, sem
):
    step = pl.program_id(0)
    width = branch_ref.shape[1]
    parts, chips, rows, columns = mine_hbm.shape

    @pl.when(step == 0)
    def _():
        total_ref[:width, :] = product_across(attended_ref[...], branch_ref[...]).astype(
            jnp.bfloat16
        )

    @pl.when(step > 0)
    def _():
        at = pl.multiple_of(step * width, width)
        total_ref[pl.ds(at, width), :] = product_across(hidden_ref[0], branch_ref[...]).astype(
            jnp.bfloat16
        )

    @pl.when(step == pl.num_programs(0) - 1)
    def _():
        core = core_ref[0]
        copies = []
        for chip in range(chips):
            for side, out in enumerate((mine_hbm, other_hbm)):
                owner = 2 * chip + (core ^ side)
                at = pl.ds(pl.multiple_of(owner * rows, rows), rows)
                for part in range(parts):
                    source = total_ref.at[at, part * columns : (part + 1) * columns]
                    copies.append(
                        pltpu.make_async_copy(source, out.at[part, chip], sem.at[len(copies)])
                    )
        for copy in copies:
            copy.start()
        for copy in copies:
            copy.wait()


def wide_grad_kernel(core_ref, normed_ref, *refs):
    *grad_refs, mine_ref, other_ref = refs
    total = None
    for part, grad_ref in enumerate(grad_refs):
        rows = grad_ref.shape[1]
        term = product_across(normed_ref[part * rows : (part + 1) * rows, :], grad_ref[0])
        total = term if total is None else total + term
    split_cores(total, core_ref[0], mine_ref, other_ref)


def wide_project_grad_kernel(
    core_ref, normed_ref, grad_ref, pooled_ref, embeds_ref, mine_ref, other_ref
):
    last = pl.program_id(0) == pl.num_programs(0) - 1

    @pl.when(jnp.logical_not(last))
    def _():
        wide_grad_kernel(core_ref, normed_ref, grad_ref, mine_ref, other_ref)

    @pl.when(last)
    def _():
        split_cores(
            product_across(pooled_ref[...], embeds_ref[...]), core_ref[0], mine_ref, other_ref
        )


def embed_grad_kernel(core_ref, pixel_ref, *refs):
    *grad_refs, table_ref, mine_ref, other_ref = refs
    parts = len(grad_refs) // 2
    total, place = None, None
    for part in range(parts):
        rows = grad_refs[part].shape[0]
        term = product_across(pixel_ref[part * rows : (part + 1) * rows, :], grad_refs[part][...])
        total = term if total is None else total + term
        own = grad_refs[parts + part][...]
        place = own if place is None else place + own
    width = total.shape[1]
    beside = mine_ref.shape[2] - width
    spare = jnp.zeros((beside - place.shape[0] - table_ref.shape[0], width), jnp.float32)
    place = jnp.concatenate([place, table_ref[...], spare], axis=0).T
    split_cores(jnp.concatenate([total, place], axis=1), core_ref[0], mine_ref, other_ref)


def square_kernel(*refs):
    *shard_refs, total_ref = refs
    total = jnp.zeros((1, 1), jnp.float32)
    for shard_ref in shard_refs:
        values = shard_ref[...].astype(jnp.float32)
        columns = jnp.sum(values * values, axis=0, keepdims=True)
        total = total + jnp.sum(columns, axis=1, keepdims=True)
    total_ref[...] = jnp.broadcast_to(total, total_ref.shape)


def update_kernel(
    total_ref, narrow_ref, hidden_ref, qkv_ref, embed_ref, *refs, wide_rows
):
    weights, moments, squares = refs[:7], refs[7:14], refs[14:21]
    changes, clips = refs[21:28], refs[28:35]
    factor = clip_bound / jnp.maximum(jnp.sqrt(total_ref[:1, :1]), clip_bound)
    width = narrow_ref.shape[1]

    def update(index, rows, columns, gradient):
        at = (slice(*rows), slice(*columns))
        change, clipped = adam_step(
            weights[index][at],
            gradient.astype(jnp.float32),
            moments[index][at],
            squares[index][at],
            factor,
        )
        changes[index][at] = change
        clips[index][at] = clipped

    everything = (None,)
    update(0, everything, everything, embed_ref[:, :width])
    blocks = weights[2].shape[1] // width
    for k in range(blocks):
        source, at = (qkv_ref, k) if k < 3 else (hidden_ref, k - 3)
        update(
            2,
            everything,
            (k * width, (k + 1) * width),
            source[at * wide_rows : (at + 1) * wide_rows, :],
        )
    update(3, everything, everything, narrow_ref[...])
    update(4, everything, everything, hidden_ref[(blocks - 3) * wide_rows :, :])
    beside = embed_ref[:, width:].astype(jnp.float32)
    slots = weights[1].shape[1]
    update(1, everything, everything, beside[:, :slots])
    beside = beside.T
    at = padded_rows(slots)
    scale_rows = weights[5].shape[0]
    update(5, everything, everything, beside[at : at + scale_rows, :])
    at += scale_rows
    update(6, everything, everything, beside[at : at + weights[6].shape[0], :])


def per_device(
    pixels,
    merge_map,
    merge_weight,
    counts,
    captions,
    pairing,
    embedder,
    positions,
    widener,
    narrower,
    projector,
    scales,
    biases,
    moment_embedder,
    moment_positions,
    moment_widener,
    moment_narrower,
    moment_projector,
    moment_scales,
    moment_biases,
    square_embedder,
    square_positions,
    square_widener,
    square_narrower,
    square_projector,
    square_scales,
    square_biases,
):
    weights = (embedder, positions, widener, narrower, projector, scales, biases)
    owners = lax.axis_size("fsdp")
    micro_count, images_dev, slot_total, patch_size = pixels.shape
    model_width = embedder.shape[1]
    wide_rows = embedder.shape[0]
    narrow_rows = narrower.shape[0]
    hidden_width = narrow_rows * owners - model_width
    hidden_blocks = hidden_width // model_width
    head_size = model_width // HEADS
    images_all = pairing.shape[1]
    logit_factor = logit_temper * captions.shape[2] ** (-0.5)
    images = micro_count * images_dev
    slots = padded_rows(slot_total)
    spare = slots - slot_total
    rows = images * slots
    pixel_rows = jnp.pad(
        pixels.reshape(images, slot_total, patch_size), ((0, 0), (0, spare), (0, 0))
    )
    slot_map = jnp.pad(
        merge_map.reshape(images, 1, slot_total), ((0, 0), (0, 0), (0, spare)), constant_values=-1
    )
    row_weight = jnp.pad(merge_weight.reshape(images, 1, slot_total), ((0, 0), (0, 0), (0, spare)))
    column_weight = row_weight.reshape(images, slots, 1)
    live_counts = counts.reshape(images)
    f32, low = jnp.float32, jnp.bfloat16
    shape = jax.ShapeDtypeStruct
    place = jnp.stack([lax.axis_index("fsdp"), lax.axis_index("rep")]).astype(jnp.int32)
    bias_rows = biases.shape[0] // wide_rows
    scale_rows = scales.shape[0]
    table_rows = padded_rows(scale_rows + bias_rows)
    small_rows = -(-(slots + table_rows) // 128) * 128
    beside = jnp.concatenate(
        [
            jnp.pad(positions.T, ((0, 0), (0, spare))),
            scales.T,
            biases.reshape(bias_rows, wide_rows).T,
        ],
        axis=1,
    )
    beside = jnp.pad(beside, ((0, 0), (0, small_rows - beside.shape[1]))).astype(low)
    small_piece = jnp.concatenate([embedder.astype(low), beside], axis=1)
    wide_low = widener.astype(low)
    blocks_of = lambda first, count: [
        wide_low[:, k * model_width : (k + 1) * model_width] for k in range(first, first + count)
    ]
    qkv_piece = jnp.stack(blocks_of(0, 3))
    hidden_piece = jnp.stack(blocks_of(3, hidden_blocks) + [projector.astype(low)])
    narrow_piece = narrower.astype(low)[None]
    small_get = Flow(gather_plain(small_piece[None]))
    small_get.go()
    sent = small_get.go()
    qkv_get = Flow(gather_split(first_behind(qkv_piece, sent)))
    sent = qkv_get.go()
    sent = small_get.go()
    guards = qkv_get.go(sent)
    embed_full, table = assembled_small(place, small_get.finish(), owners, model_width, guards)
    scale_float = table[slots : slots + scale_rows]
    bias_float = jnp.swapaxes(
        table[slots + scale_rows : slots + scale_rows + bias_rows].reshape(
            bias_rows, owners, wide_rows
        ),
        0,
        1,
    ).reshape(-1)
    out_bias = bias_float[hidden_width : hidden_width + model_width].reshape(1, model_width)
    place_bias = table[:slots] + bias_float[hidden_width + model_width :]
    guards = qkv_get.go()
    hidden_get = Flow(gather_split(first_behind(hidden_piece, guards)))
    guards += hidden_get.go()
    merged, normed = image_call(
        embed_kernel,
        images,
        [
            per_image(slots, patch_size),
            per_image(1, slots),
            per_image(1, slots),
            per_image(slots, 1),
            whole(patch_size, model_width),
            whole(slots, model_width),
            whole(1, model_width),
        ]
        + [anywhere] * len(guards),
        [per_image(slots, model_width)] * 2,
        [shape((images, slots, model_width), f32), shape((images, slots, model_width), low)],
        name="embed",
    )(
        live_counts, pixel_rows, slot_map, row_weight, column_weight, embed_full, place_bias,
        scale_float[0:1], *guards,
    )
    qkv_get.go()
    qkv_parts = qkv_get.finish()
    guards = hidden_get.go(qkv_parts[-1][0])
    narrow_get = Flow(gather_split(first_behind(narrow_piece, guards)))
    guards += narrow_get.go()
    arrays, found, size = gathered(qkv_parts)
    normed_rows = normed.reshape(rows, model_width)
    column_block = lambda index_map: block((1, rows, model_width), index_map)
    heads, rstd, wide_qkv = pl.pallas_call(
        functools.partial(widen_heads_kernel, found=found, chunk=slots, head_size=head_size),
        grid_spec=pltpu.PrefetchScalarGridSpec(
            num_scalar_prefetch=1,
            grid=(2,),
            in_specs=[whole(rows, model_width), block((1, 1, model_width), lambda k, _: (k, 0, 0))]
            + [anywhere] * (len(arrays) + len(guards)),
            out_specs=[column_block(lambda k, _: (k, 0, 0))] * 2 + [anywhere],
            scratch_shapes=gather_scratch(found, size),
        ),
        out_shape=[
            shape((2, rows, model_width), low), shape((2, rows, model_width), f32), shape(size, low)
        ],
        compiler_params=roomy,
        cost_estimate=long,
        name="widen_heads",
    )(place, normed_rows, scale_float[2:4].reshape(2, 1, model_width), *arrays, *guards)
    guards = hidden_get.go(heads)
    values = pl.pallas_call(
        widen_value_kernel,
        grid=(1,),
        in_specs=[whole(rows, model_width), block((1, model_width, model_width), lambda k: (2, 0, 0))]
        + [anywhere] * (1 + len(guards)),
        out_specs=column_block(lambda k: (0, 0, 0)),
        out_shape=shape((1, rows, model_width), low),
        compiler_params=roomy,
        cost_estimate=long,
        name="widen_values",
    )(normed_rows, wide_qkv, heads, *guards)
    image_columns = lambda parts: block(
        (parts, slots, model_width), lambda image, counts: (0, image, 0)
    )
    guards = narrow_get.go(heads)
    (attended,) = image_call(
        functools.partial(attend_kernel, head_size=head_size),
        images,
        [image_columns(2), image_columns(1)] + [anywhere] * len(guards),
        [per_image(slots, model_width)],
        [shape((images, slots, model_width), low)],
        name="attend",
    )(live_counts, heads, values, *guards)
    guards = narrow_get.go() + [attended]
    hidden_get.go(guards)
    arrays, found, size = gathered(hidden_get.finish())
    hidden, slope, wide_hidden = pl.pallas_call(
        functools.partial(widen_hidden_kernel, found=found, chunk=slots),
        grid_spec=pltpu.PrefetchScalarGridSpec(
            num_scalar_prefetch=1,
            grid=(hidden_blocks,),
            in_specs=[whole(rows, model_width), block((1, 1, model_width), lambda k, _: (k, 0, 0))]
            + [anywhere] * (len(arrays) + len(guards)),
            out_specs=[column_block(lambda k, _: (k, 0, 0))] * 2 + [anywhere],
            scratch_shapes=gather_scratch(found, size),
        ),
        out_shape=[shape((hidden_blocks, rows, model_width), low)] * 2 + [shape(size, low)],
        compiler_params=roomy,
        cost_estimate=long,
        name="widen_hidden",
    )(
        place, normed_rows, bias_float[:hidden_width].reshape(hidden_blocks, 1, model_width),
        *arrays, *guards,
    )
    project_full = wide_hidden[hidden_blocks]
    narrow_get.go(hidden)
    arrays, found, size = gathered(narrow_get.finish())
    narrow_scratch = [
        pltpu.VMEM((hidden_width + model_width, model_width), low), pltpu.SemaphoreType.DMA
    ]
    stream, pooled, narrow_full = pl.pallas_call(
        functools.partial(join_kernel, found=found),
        grid_spec=pltpu.PrefetchScalarGridSpec(
            num_scalar_prefetch=2,
            grid=(images,),
            in_specs=[
                block((1, slots, model_width), lambda image, *_: (image, 0, 0)),
                block((hidden_blocks, slots, model_width), lambda image, *_: (0, image, 0)),
                block((1, slots, model_width), lambda image, *_: (image, 0, 0)),
                whole(1, model_width),
                whole(1, model_width),
            ]
            + [anywhere] * len(arrays),
            out_specs=[
                block((1, slots, model_width), lambda image, *_: (image, 0, 0)),
                block((1, 1, model_width), lambda image, *_: (image, 0, 0)),
                anywhere,
            ],
            scratch_shapes=gather_scratch(found, size),
        ),
        out_shape=[
            shape((images, slots, model_width), f32),
            shape((images, 1, model_width), f32),
            shape(size, low),
        ],
        compiler_params=roomy,
        cost_estimate=long,
        name="join",
    )(live_counts, place, attended, hidden, merged, out_bias, scale_float[1:2], *arrays)
    narrow_full = narrow_full[0]
    pooled_low = pooled.reshape(images, model_width).astype(low)
    embeds = product(pooled_low, project_full).astype(low)
    embeds = embeds.reshape(micro_count, images_dev, -1)
    logits = jnp.einsum("mie,mje->mij", embeds, captions, preferred_element_type=f32) * logit_factor
    image_ids = jnp.arange(images_all, dtype=jnp.int32)
    first_row = (lax.axis_index("rep") * owners + lax.axis_index("fsdp")) * images_dev
    own_pairs = lax.dynamic_slice_in_dim(pairing, first_row, images_dev, 1)
    target = (own_pairs[:, :, None] == image_ids[None, None, :]).astype(jnp.float32)
    row_top = jnp.max(logits, axis=2, keepdims=True)
    row_logsum = row_top[:, :, 0] + jnp.log(jnp.sum(jnp.exp(logits - row_top), axis=2))
    own_top = jnp.max(logits, axis=1)
    own_total = jnp.sum(jnp.exp(logits - own_top[:, None, :]), axis=1)
    picked = jnp.sum(logits * target, axis=2)
    counts_float = counts.astype(jnp.float32)
    scalars = jnp.concatenate(
        [
            jnp.sum(counts_float * (picked - row_logsum), axis=1),
            jnp.sum(picked, axis=1),
            jnp.sum(counts_float, axis=1),
        ]
    )
    sums = jnp.pad(scalars[None, :], ((0, 0), (0, images_all - scalars.shape[0])))
    column_top, column_total, sums = column_totals(own_top, own_total, sums)
    column_logsum = column_top + jnp.log(column_total)
    row_terms = sums[0, :micro_count]
    picked_sums = sums[0, micro_count : 2 * micro_count]
    weight_totals = sums[0, 2 * micro_count : 3 * micro_count]
    weight_total_all = jnp.sum(weight_totals)
    part_losses = 0.5 * (
        -row_terms / weight_totals - (picked_sums - jnp.sum(column_logsum, axis=1)) / images_all
    )
    objective = jnp.sum(part_losses) / micro_count
    row_soft = jnp.exp(logits - row_logsum[:, :, None])
    column_soft = jnp.exp(logits - column_logsum[:, None, :])
    all_grad_logits = (
        0.5
        / micro_count
        * (
            (counts_float / weight_totals[:, None])[:, :, None] * (row_soft - target)
            + (column_soft - target) / images_all
        )
    )
    grad_product = (all_grad_logits * logit_factor).astype(low)
    grad_embeds = (
        jnp.einsum("mij,mje->mie", grad_product, captions, preferred_element_type=f32)
        .astype(low)
        .reshape(images, -1)
    )
    grad_pooled = product_along(grad_embeds, project_full)
    grad_stream, grad_branch, grad_attended, grad_act, out_sums = image_call(
        branch_kernel,
        images,
        [
            per_image(slots, model_width),
            per_image(1, model_width),
            whole(1, model_width),
            image_columns(hidden_blocks),
            anywhere,
        ],
        [
            per_image(slots, model_width),
            per_image(slots, model_width),
            per_image(slots, model_width),
            image_columns(hidden_blocks),
            whole(8, model_width),
        ],
        [
            shape((images, slots, model_width), f32),
            shape((images, slots, model_width), low),
            shape((images, slots, model_width), low),
            shape((hidden_blocks, rows, model_width), low),
            shape((8, model_width), f32),
        ],
        narrow_scratch,
        name="branch",
    )(
        live_counts, stream, grad_pooled.reshape(images, 1, model_width), scale_float[1:2], slope,
        narrow_full,
    )
    core = (lax.axis_index("fsdp") % 2).reshape(1)
    chips = owners // 2
    branch_rows = grad_branch.reshape(rows, model_width)
    halves = lambda count, width: [shape((chips, count, width), low)] * 2
    parts_wide = column_parts(model_width)
    part_width = model_width // parts_wide
    split_halves = lambda count: [shape((parts_wide, chips, count, part_width), low)] * 2
    narrow_halves = pl.pallas_call(
        narrow_grad_kernel,
        grid_spec=pltpu.PrefetchScalarGridSpec(
            num_scalar_prefetch=1,
            grid=(1 + hidden_blocks,),
            in_specs=[
                whole(rows, model_width),
                block((1, rows, model_width), lambda k, _: (jnp.maximum(k - 1, 0), 0, 0)),
                whole(rows, model_width),
            ],
            out_specs=[anywhere] * 2,
            scratch_shapes=[
                pltpu.VMEM((hidden_width + model_width, model_width), low),
                pltpu.SemaphoreType.DMA((2 * parts_wide * chips,)),
            ],
        ),
        out_shape=split_halves(narrow_rows),
        compiler_params=roomy,
        cost_estimate=long,
        name="narrow_grad",
    )(core, attended.reshape(rows, model_width), hidden, branch_rows)
    narrow_flow = Flow(reduce_columns(*narrow_halves))
    narrow_flow.go()
    owner_block = block((chips, wide_rows, model_width), lambda k, _: (0, k, 0))
    few = padded_rows(images)
    hidden_halves = pl.pallas_call(
        wide_project_grad_kernel,
        grid_spec=pltpu.PrefetchScalarGridSpec(
            num_scalar_prefetch=1,
            grid=(hidden_blocks + 1,),
            in_specs=[
                whole(rows, model_width),
                block(
                    (1, rows, model_width), lambda k, _: (jnp.minimum(k, hidden_blocks - 1), 0, 0)
                ),
                whole(few, model_width),
                whole(few, model_width),
            ],
            out_specs=[owner_block] * 2,
        ),
        out_shape=halves((hidden_blocks + 1) * wide_rows, model_width),
        compiler_params=roomy,
        cost_estimate=long,
        name="hidden_grad",
    )(
        core, normed_rows, grad_act, jnp.pad(pooled_low, ((0, few - images), (0, 0))),
        jnp.pad(grad_embeds, ((0, few - images), (0, 0))),
    )
    hidden_flow = Flow(reduce_rows_last(*hidden_halves))
    hidden_flow.go()
    parts = images_dev
    per_part = images // parts
    part_rows = per_part * slots

    def shifted(base, rows_count):
        return block((1, rows_count, model_width), lambda image, counts: (base + image, 0, 0))

    def shifted_columns(base, count):
        return block((count, slots, model_width), lambda image, counts: (0, base + image, 0))

    head_gains = scale_float[2:4].reshape(2, 1, model_width)
    guards = narrow_flow.go()
    grad_hidden = pl.pallas_call(
        hidden_back_kernel,
        grid=(hidden_blocks,),
        in_specs=[
            block((1, rows, model_width), lambda k: (k, 0, 0)),
            block((1, model_width, model_width), lambda k: (k, 0, 0)),
        ]
        + [anywhere] * len(guards),
        out_specs=whole(rows, model_width),
        out_shape=shape((rows, model_width), f32),
        scratch_shapes=[pltpu.VMEM((rows, model_width), f32)],
        compiler_params=roomy,
        cost_estimate=long,
        name="hidden_back",
    )(grad_act, wide_hidden, *guards)
    guards = [grad_hidden] + hidden_flow.go()
    grad_qkv, head_sums = [], 0.0
    for part in range(parts):
        base = part * per_part
        grads, sums_part = image_call(
            functools.partial(attend_back_kernel, base=base, head_size=head_size),
            per_part,
            [
                shifted_columns(base, 2),
                shifted_columns(base, 1),
                shifted_columns(base, 2),
                shifted(base, slots),
                whole(2, 1, model_width),
            ]
            + [anywhere] * len(guards),
            [image_columns(3), whole(8, model_width)],
            [shape((3, part_rows, model_width), low), shape((8, model_width), f32)],
            [pltpu.VMEM((2, slots, model_width), f32)],
            name="attend_back",
        )(live_counts, heads, values, rstd, grad_attended, head_gains, *guards)
        grad_qkv.append(grads)
        head_sums = head_sums + sums_part
        guards = [grads]
    guards += narrow_flow.go(grads)
    qkv_halves = pl.pallas_call(
        lambda core_ref, normed_ref, *refs: wide_grad_kernel(
            core_ref, normed_ref, *refs[:parts], *refs[-2:]
        ),
        grid_spec=pltpu.PrefetchScalarGridSpec(
            num_scalar_prefetch=1,
            grid=(3,),
            in_specs=[whole(rows, model_width)]
            + [block((1, part_rows, model_width), lambda k, _: (k, 0, 0))] * parts
            + [anywhere] * len(guards),
            out_specs=[block((parts_wide, chips, wide_rows, part_width), lambda k, _: (0, 0, k, 0))] * 2,
        ),
        out_shape=split_halves(3 * wide_rows),
        compiler_params=roomy,
        cost_estimate=long,
        name="qkv_grad",
    )(core, normed_rows, *grad_qkv, *guards)
    qkv_flow = Flow(reduce_columns(*qkv_halves))
    guards = qkv_flow.go()
    grad_patches, grad_places, merge_sums = [], [], 0.0
    for part in range(parts):
        base = part * per_part
        grads, place_part, sums_part = image_call(
            functools.partial(merge_back_kernel, base=base),
            per_part,
            [
                image_columns(3),
                block((slots, model_width), lambda image, counts, base=base: (base + image, 0)),
                anywhere,
                shifted(base, slots),
                shifted(base, slots),
                whole(1, model_width),
                block((1, 1, slots), lambda image, counts, base=base: (base + image, 0, 0)),
                block((1, 1, slots), lambda image, counts, base=base: (base + image, 0, 0)),
                block((1, slots, 1), lambda image, counts, base=base: (base + image, 0, 0)),
            ]
            + [anywhere] * len(guards),
            [per_image(slots, model_width), whole(slots, model_width), whole(8, model_width)],
            [
                shape((per_part, slots, model_width), low),
                shape((slots, model_width), f32),
                shape((8, model_width), f32),
            ],
            [
                pltpu.VMEM((3, model_width, model_width), low),
                pltpu.SemaphoreType.DMA((3,)),
            ],
            name="merge_back",
        )(
            live_counts, grad_qkv[part], grad_hidden, wide_qkv, merged, grad_stream,
            scale_float[0:1], slot_map, row_weight, column_weight, *guards,
        )
        grad_patches.append(grads.reshape(part_rows, model_width))
        grad_places.append(place_part)
        merge_sums = merge_sums + sums_part
        guards = [grads]
        if part == 0:
            guards += hidden_flow.go(grads) + qkv_flow.go(grads)
        elif part == 1:
            guards += narrow_flow.go(grads)
    guards += hidden_flow.go(grads) + qkv_flow.go(grads) + narrow_flow.go(grads)
    grad_scale = jnp.stack([merge_sums[0], out_sums[hidden_blocks + 1], head_sums[0], head_sums[1]])
    grad_bias = jnp.concatenate([out_sums[: hidden_blocks + 1], merge_sums[1:2]]).reshape(
        owners, bias_rows, wide_rows
    )
    grad_bias = jnp.swapaxes(grad_bias, 0, 1).reshape(bias_rows, model_width)
    table = jnp.concatenate([grad_scale, grad_bias])
    table = jnp.pad(table, ((0, padded_rows(table.shape[0]) - table.shape[0]), (0, 0)))
    piece_width = small_piece.shape[1]
    embed_halves = pl.pallas_call(
        lambda core_ref, pixel_ref, *refs: embed_grad_kernel(
            core_ref, pixel_ref, *refs[: 2 * parts + 1], *refs[-2:]
        ),
        grid_spec=pltpu.PrefetchScalarGridSpec(
            num_scalar_prefetch=1,
            grid=(1,),
            in_specs=[whole(rows, patch_size)]
            + [whole(part_rows, model_width)] * parts
            + [whole(slots, model_width)] * parts
            + [whole(*table.shape)]
            + [anywhere] * len(guards),
            out_specs=[whole(chips, wide_rows, piece_width)] * 2,
        ),
        out_shape=halves(wide_rows, piece_width),
        compiler_params=roomy,
        cost_estimate=long,
        name="embed_grad",
    )(core, pixel_rows.reshape(rows, patch_size), *grad_patches, *grad_places, table, *guards)
    embed_flow = Flow(reduce_rows_last(*embed_halves))
    embed_flow.go()
    sent = embed_flow.go()
    sent = qkv_flow.go(sent)
    narrow_flow.go(sent)
    hidden_flow.go(sent)
    embed_flow.go()
    sent = embed_flow.go(qkv_flow.go())
    qkv_flow.go(sent)
    flows = (narrow_flow, hidden_flow, qkv_flow, embed_flow)
    shards = [flow.finish() for flow in flows]
    squares_sum = pl.pallas_call(
        square_kernel,
        out_shape=shape((8, 128), f32),
        compiler_params=roomy,
        name="squares",
    )(*shards)
    squares_sum = sum_over(squares_sum, "fsdp")
    total_norm = jnp.sqrt(squares_sum[0, 0])
    moments = (
        moment_embedder,
        moment_positions,
        moment_widener,
        moment_narrower,
        moment_projector,
        moment_scales,
        moment_biases,
    )
    squares = (
        square_embedder,
        square_positions,
        square_widener,
        square_narrower,
        square_projector,
        square_scales,
        square_biases,
    )
    as_rows = lambda arrays: [
        array.reshape(-1, wide_rows) if array.ndim == 1 else array.T if index % 7 == 1 else array
        for index, array in enumerate(arrays)
    ]
    outs = pl.pallas_call(
        functools.partial(update_kernel, wide_rows=wide_rows),
        out_shape=[shape(array.shape, f32) for array in as_rows(weights) * 2],
        compiler_params=roomy,
        name="update",
    )(squares_sum, *shards, *as_rows(weights), *as_rows(moments), *as_rows(squares))
    outs = [
        out.T if index % 7 == 1 else out.reshape(array.shape)
        for index, (out, array) in enumerate(zip(outs, weights * 2, strict=True))
    ]
    return (objective, weight_total_all, total_norm, *outs)


def solution(mesh):
    return jax.shard_map(
        per_device,
        mesh=mesh,
        in_specs=(
            P(None, ("rep", "fsdp"), None, None),
            P(None, ("rep", "fsdp"), None),
            P(None, ("rep", "fsdp"), None),
            P(None, ("rep", "fsdp")),
            P(),
            P(),
            P("fsdp", None),
            P(None, "fsdp"),
            P("fsdp", None),
            P("fsdp", None),
            P("fsdp", None),
            P(None, "fsdp"),
            P("fsdp"),
            P("fsdp", None),
            P(None, "fsdp"),
            P("fsdp", None),
            P("fsdp", None),
            P("fsdp", None),
            P(None, "fsdp"),
            P("fsdp"),
            P("fsdp", None),
            P(None, "fsdp"),
            P("fsdp", None),
            P("fsdp", None),
            P("fsdp", None),
            P(None, "fsdp"),
            P("fsdp"),
        ),
        out_specs=(
            P(),
            P(),
            P(),
            P("fsdp", None),
            P(None, "fsdp"),
            P("fsdp", None),
            P("fsdp", None),
            P("fsdp", None),
            P(None, "fsdp"),
            P("fsdp"),
            P("fsdp", None),
            P(None, "fsdp"),
            P("fsdp", None),
            P("fsdp", None),
            P("fsdp", None),
            P(None, "fsdp"),
            P("fsdp"),
        ),
        check_vma=False,
    )
```

```python
import functools

import jax
import jax.numpy as jnp
from jax import lax
from jax.experimental import pallas as pl
from jax.experimental.pallas import tpu as pltpu
from jax.sharding import PartitionSpec as P

HEADS = 12


norm_eps = 1e-06
clip_bound = 0.1
beta_first = 0.9
beta_second = 0.999
learn_rate = 0.03
weight_decay = 0.1
adam_eps = 1e-08
step_number = 10
logit_temper = 10.0


def product(left, right):
    return jnp.dot(left, right, preferred_element_type=jnp.float32)


def product_across(left, right):
    return lax.dot_general(
        left, right, (((0,), (0,)), ((), ())), preferred_element_type=jnp.float32
    )


def product_along(left, right):
    return lax.dot_general(
        left, right, (((1,), (1,)), ((), ())), preferred_element_type=jnp.float32
    )


def adam_step(weight, gradient, moment, square, factor):
    clipped = gradient * factor
    moment_new = beta_first * moment + (1.0 - beta_first) * clipped
    square_new = beta_second * square + (1.0 - beta_second) * clipped * clipped
    mean_hat = moment_new / (1.0 - beta_first**step_number)
    square_hat = square_new / (1.0 - beta_second**step_number)
    change = -learn_rate * (mean_hat / (jnp.sqrt(square_hat) + adam_eps) + weight_decay * weight)
    return (change, clipped)


def bit_swap(size, bit):
    return [(index, index ^ bit) for index in range(size)]


def ordered_pair(own, other, axis, bit):
    low_side = (lax.axis_index(axis) & bit) == 0
    return jnp.where(low_side, own, other), jnp.where(low_side, other, own)


def combined(first, second, micro_count):
    top_a, top_b = first[:micro_count], second[:micro_count]
    top = jnp.maximum(top_a, top_b)
    parts = slice(micro_count, 2 * micro_count)
    total = first[parts] * jnp.exp(top_a - top) + second[parts] * jnp.exp(top_b - top)
    return jnp.concatenate([top, total, first[2 * micro_count :] + second[2 * micro_count :]])


def column_totals(top, total, sums):
    micro_count = top.shape[0]
    packed = jnp.concatenate([top, total, sums], axis=0)
    owners, reps = lax.axis_size("fsdp"), lax.axis_size("rep")
    steps = [("fsdp", owners, 1), ("fsdp", owners, 2)]
    steps += [("rep", reps, 1 << bit) for bit in range(reps.bit_length() - 1)]
    for axis, size, bit in steps:
        other = lax.ppermute(packed, axis, bit_swap(size, bit))
        packed = combined(*ordered_pair(packed, other, axis, bit), micro_count)
    turns = [packed] + [
        lax.ppermute(packed, "fsdp", bit_swap(owners, turn)) for turn in range(4, owners, 4)
    ]
    bit = 4
    while len(turns) > 1:
        turns = [
            combined(*ordered_pair(first, second, "fsdp", bit), micro_count)
            for first, second in zip(turns[::2], turns[1::2], strict=True)
        ]
        bit *= 2
    packed = turns[0]
    return packed[:micro_count], packed[micro_count : 2 * micro_count], packed[2 * micro_count :]


def sum_over(value, axis):
    size = lax.axis_size(axis)
    for bit in (1, 2):
        value = value + lax.ppermute(value, axis, bit_swap(size, bit))
    turns = [value] + [
        lax.ppermute(value, axis, bit_swap(size, turn)) for turn in range(4, size, 4)
    ]
    while len(turns) > 1:
        turns = [first + second for first, second in zip(turns[::2], turns[1::2], strict=True)]
    return turns[0]


def padded_rows(rows):
    return -(-rows // 16) * 16


def split_two(values):
    high = values.astype(jnp.bfloat16)
    return high, (values - high.astype(jnp.float32)).astype(jnp.bfloat16)


def normal_rows(values):
    center = values - jnp.mean(values, axis=-1, keepdims=True)
    rstd = lax.rsqrt(jnp.mean(center * center, axis=-1, keepdims=True) + norm_eps)
    return center * rstd, rstd


def head_mixer(head_size):
    row = lax.broadcasted_iota(jnp.int32, (256, 256), 0) // head_size
    column = lax.broadcasted_iota(jnp.int32, (256, 256), 1) // head_size
    return jnp.where(row == column, 1.0 / head_size, 0.0).astype(jnp.bfloat16)


def head_mean(values, mixer, fine=True):
    parts = []
    for at in range(0, values.shape[1], 256):
        if fine:
            high, low = split_two(values[:, at : at + 256])
            parts.append(product(high, mixer) + product(low, mixer))
        else:
            parts.append(product(values[:, at : at + 256].astype(jnp.bfloat16), mixer))
    return jnp.concatenate(parts, axis=1)


def embed_kernel(
    counts_ref, pixel_ref, map_ref, row_ref, column_ref, embed_ref, place_ref, gain_ref, *refs
):
    merged_ref, normed_ref = refs[-2:]
    live_count = counts_ref[pl.program_id(0)]
    slots = merged_ref.shape[1]
    patches = product(pixel_ref[0], embed_ref[...]) + place_ref[...]
    high, low = split_two(patches * column_ref[0])
    slot = lax.broadcasted_iota(jnp.int32, (slots, slots), 0)
    member = slot == map_ref[0]
    hot = jnp.where(member, 1.0, 0.0).astype(jnp.bfloat16)
    total = jnp.sum(jnp.where(member, row_ref[0], 0.0), axis=1, keepdims=True)
    vacant = lax.broadcasted_iota(jnp.int32, (slots, 1), 0) >= live_count
    total = total + jnp.where(vacant, 1.0, 0.0)
    merged = (product(hot, high) + product(hot, low)) / total
    merged_ref[0] = merged
    unit, _ = normal_rows(merged)
    normed_ref[0] = (unit * gain_ref[...]).astype(jnp.bfloat16)


def gelu_pair(values):
    share = 0.5 + 0.5 * lax.erf(values * 0.7071067811865476)
    bell = jnp.exp(-0.5 * values * values)
    return values * share, share + values * bell * 0.3989422804014327


def widen_heads_kernel(
    place_ref, normed_ref, gain_ref, *refs, found, chunk, head_size
):
    heads_ref, rstd_ref, wide_hbm, held_ref, sem, out_sem = refs[-6:]
    sources = refs[: len(found)]
    step = pl.program_id(0)
    keep = pltpu.make_async_copy(held_ref, wide_hbm, out_sem)

    @pl.when(step == 0)
    def _():
        fetch(place_ref, sources, found, held_ref, sem)
        fetched(place_ref, sources, found, held_ref, sem)
        keep.start()

    chunks = normed_ref.shape[0] // chunk
    mixer = head_mixer(head_size)
    gain = gain_ref[0]
    for index in range(chunks):
        rows = slice(index * chunk, (index + 1) * chunk)
        values = product(normed_ref[rows, :], held_ref[step])
        center = values - head_mean(values, mixer)
        rstd = lax.rsqrt(head_mean(center * center, mixer, False) + norm_eps)
        rstd_ref[0, rows, :] = rstd
        heads_ref[0, rows, :] = (center * rstd * gain).astype(jnp.bfloat16)

    pl.when(step == pl.num_programs(0) - 1)(keep.wait)


def widen_value_kernel(normed_ref, wide_ref, *refs):
    values_ref = refs[-1]
    values_ref[0] = product(normed_ref[...], wide_ref[0]).astype(jnp.bfloat16)


def widen_hidden_kernel(place_ref, normed_ref, bias_ref, *refs, found, chunk):
    hidden_ref, slope_ref, wide_hbm, held_ref, sem, out_sem = refs[-6:]
    sources = refs[: len(found)]
    step = pl.program_id(0)
    keep = pltpu.make_async_copy(held_ref, wide_hbm, out_sem)

    @pl.when(step == 0)
    def _():
        fetch(place_ref, sources, found, held_ref, sem)
        fetched(place_ref, sources, found, held_ref, sem)
        keep.start()

    for index in range(normed_ref.shape[0] // chunk):
        rows = slice(index * chunk, (index + 1) * chunk)
        values = product(normed_ref[rows, :], held_ref[step]) + bias_ref[0]
        hidden, slope = gelu_pair(values)
        hidden_ref[0, rows, :] = hidden.astype(jnp.bfloat16)
        slope_ref[0, rows, :] = slope.astype(jnp.bfloat16)

    pl.when(step == pl.num_programs(0) - 1)(keep.wait)


def head_groups(width, pair):
    starts = range(0, width, 2 * pair)
    return [[slice(at, at + pair), slice(at + pair, at + 2 * pair)] for at in starts]


def by_head(pairs, first_half):
    items = []
    for both in pairs:
        zero = jnp.zeros_like(both)
        items += [jnp.where(first_half, both, zero), jnp.where(first_half, zero, both)]
    return items


def attend_kernel(counts_ref, heads_ref, values_ref, *refs, head_size):
    attended_ref = refs[-1]
    live_count = counts_ref[pl.program_id(0)]
    slots, width = attended_ref.shape[1:]
    factor = head_size ** (-0.5) * 1.4426950408889634
    key_live = jnp.where(
        lax.broadcasted_iota(jnp.int32, (1, slots), 1) < live_count, 1.0, 0.0
    )
    pair = 2 * head_size
    first_half = lax.broadcasted_iota(jnp.int32, (slots, pair), 1) < head_size
    for columns in head_groups(width, pair):
        queries, keys = ([heads_ref[part, :, at] for at in columns] for part in range(2))
        values = [values_ref[0, :, at] for at in columns]
        own = by_head(queries, first_half)
        each = range(len(own))
        weights = [product_along(own[h], keys[h // 2]) for h in each]
        weights = [jnp.exp2(weights[h] * factor) * key_live for h in each]
        share = [
            weights[h] * (1.0 / jnp.sum(weights[h], axis=1, keepdims=True)) for h in each
        ]
        outs = [product(share[h].astype(jnp.bfloat16), values[h // 2]) for h in each]
        for index, at in enumerate(columns):
            attended_ref[0, :, at] = jnp.where(
                first_half, outs[2 * index], outs[2 * index + 1]
            ).astype(jnp.bfloat16)


def join_kernel(
    counts_ref, place_ref, attended_ref, hidden_ref, merged_ref, bias_ref, gain_ref, *refs, found
):
    stream_ref, pooled_ref, narrow_hbm, held_ref, sem, out_sem = refs[-6:]
    sources = refs[: len(found)]
    image = pl.program_id(0)
    live_count = counts_ref[image]
    slots, width = merged_ref.shape[1:]
    keep = pltpu.make_async_copy(held_ref, narrow_hbm, out_sem)

    @pl.when(image == 0)
    def _():
        fetch(place_ref, sources, found, held_ref, sem)
        fetched(place_ref, sources, found, held_ref, sem)
        keep.start()

    stream = merged_ref[0] + bias_ref[...]
    for k in range(1 + hidden_ref.shape[0]):
        left = attended_ref[0] if k == 0 else hidden_ref[k - 1]
        stream = stream + product(left, held_ref[0, k * width : (k + 1) * width, :])
    stream_ref[0] = stream
    unit, _ = normal_rows(stream)
    live = lax.broadcasted_iota(jnp.int32, (slots, 1), 0) < live_count
    total = jnp.sum(jnp.where(live, unit, 0.0), axis=0, keepdims=True)
    pooled_ref[0] = total * gain_ref[...] / live_count.astype(jnp.float32)

    pl.when(image == pl.num_programs(0) - 1)(keep.wait)


def branch_kernel(
    counts_ref, stream_ref, grad_pooled_ref, gain_ref, slope_ref, narrow_hbm,
    grad_stream_ref, grad_branch_ref, grad_attended_ref, grad_act_ref, sums_ref, narrow_ref, sem,
):
    image = pl.program_id(0)
    live_count = counts_ref[image]
    slots, width = stream_ref.shape[1:]
    copy = pltpu.make_async_copy(narrow_hbm, narrow_ref, sem)

    @pl.when(image == 0)
    def _():
        copy.start()
        sums_ref[...] = jnp.zeros_like(sums_ref)

    unit, rstd = normal_rows(stream_ref[0])
    live = lax.broadcasted_iota(jnp.int32, (slots, 1), 0) < live_count
    above = grad_pooled_ref[0] / live_count.astype(jnp.float32)
    slanted = above * gain_ref[...]
    mean_first = jnp.mean(slanted, axis=-1, keepdims=True)
    mean_second = jnp.mean(slanted * unit, axis=-1, keepdims=True)
    grad_stream = jnp.where(live, rstd * (slanted - mean_first - unit * mean_second), 0.0)
    grad_stream_ref[0] = grad_stream
    grad_branch = grad_stream.astype(jnp.bfloat16)
    grad_branch_ref[0] = grad_branch
    parts = slope_ref.shape[0]
    sums_ref[parts : parts + 1, :] += jnp.sum(grad_stream, axis=0, keepdims=True)
    sums_ref[parts + 1 : parts + 2, :] += above * jnp.sum(
        jnp.where(live, unit, 0.0), axis=0, keepdims=True
    )

    @pl.when(image == 0)
    def _():
        copy.wait()

    grad_attended_ref[0] = product_along(grad_branch, narrow_ref[:width, :]).astype(jnp.bfloat16)
    for part in range(parts):
        grad_act = product_along(
            grad_branch, narrow_ref[(part + 1) * width : (part + 2) * width, :]
        ) * slope_ref[part].astype(jnp.float32)
        grad_act_ref[part] = grad_act.astype(jnp.bfloat16)
        sums_ref[part : part + 1, :] += jnp.sum(grad_act, axis=0, keepdims=True)


def attend_back_kernel(
    counts_ref, heads_ref, values_ref, rstd_ref, grad_attended_ref, gain_ref, *refs, base, head_size
):
    grad_qkv_ref, sums_ref, grad_ref = refs[-3:]
    image = pl.program_id(0)
    live_count = counts_ref[base + image]
    slots, width = grad_attended_ref.shape[1:]

    @pl.when(image == 0)
    def _():
        sums_ref[...] = jnp.zeros_like(sums_ref)

    factor = head_size ** (-0.5)
    key_live = lax.broadcasted_iota(jnp.int32, (slots, 1), 0) < live_count
    pair = 2 * head_size
    first_half = lax.broadcasted_iota(jnp.int32, (slots, pair), 1) < head_size
    for columns in head_groups(width, pair):
        queries, keys = ([heads_ref[part, :, at] for at in columns] for part in range(2))
        values = [values_ref[0, :, at] for at in columns]
        own_queries = by_head(queries, first_half)
        own_above = by_head([grad_attended_ref[0, :, at] for at in columns], first_half)
        each = range(len(own_queries))
        weights = [product_along(keys[h // 2], own_queries[h]) for h in each]
        grad_share = [product_along(values[h // 2], own_above[h]) for h in each]
        weights = [
            jnp.where(key_live, jnp.exp2(weights[h] * (factor * 1.4426950408889634)), 0.0)
            for h in each
        ]
        share = [weights[h] * (1.0 / jnp.sum(weights[h], axis=0, keepdims=True)) for h in each]
        dot_row = [jnp.sum(share[h] * grad_share[h], axis=0, keepdims=True) for h in each]
        grad_raw = [
            (share[h] * (grad_share[h] - dot_row[h]) * factor).astype(jnp.bfloat16) for h in each
        ]
        share = [share[h].astype(jnp.bfloat16) for h in each]
        for index, at in enumerate(columns):
            one, two = 2 * index, 2 * index + 1
            grad_qkv_ref[2, :, at] = (
                product(share[one], own_above[one]) + product(share[two], own_above[two])
            ).astype(jnp.bfloat16)
            grad_ref[1, :, at] = product(grad_raw[one], own_queries[one]) + product(
                grad_raw[two], own_queries[two]
            )
            grad_ref[0, :, at] = jnp.where(
                first_half,
                product_across(grad_raw[one], keys[index]),
                product_across(grad_raw[two], keys[index]),
            )
    mixer = head_mixer(head_size)
    for part in range(2):
        gain = gain_ref[part]
        above = grad_ref[part]
        unit = heads_ref[part].astype(jnp.float32) / gain
        sums_ref[part : part + 1, :] += jnp.sum(above * unit, axis=0, keepdims=True)
        slanted = above * gain
        back = (
            slanted
            - head_mean(slanted, mixer, False)
            - unit * head_mean(slanted * unit, mixer, False)
        )
        grad_qkv_ref[part] = (rstd_ref[part] * back).astype(jnp.bfloat16)


def hidden_back_kernel(grad_act_ref, wide_ref, *refs):
    out_ref, total_ref = refs[-2:]
    step = pl.program_id(0)
    term = product_along(grad_act_ref[0], wide_ref[0])

    @pl.when(step == 0)
    def _():
        total_ref[...] = term

    @pl.when(step > 0)
    def _():
        total_ref[...] += term

    @pl.when(step == pl.num_programs(0) - 1)
    def _():
        out_ref[...] = total_ref[...]


def merge_back_kernel(
    counts_ref, grad_qkv_ref, grad_hidden_ref, wide_hbm, merged_ref, grad_stream_ref, gain_ref,
    map_ref, row_ref, column_ref, *refs, base,
):
    grad_patch_ref, grad_place_ref, sums_ref, wide_ref, sem = refs[-5:]
    image = pl.program_id(0)
    live_count = counts_ref[base + image]
    slots, width = merged_ref.shape[1:]
    blocks = wide_ref.shape[0]
    copies = [
        pltpu.make_async_copy(wide_hbm.at[part], wide_ref.at[part], sem.at[part])
        for part in range(blocks)
    ]

    @pl.when(image == 0)
    def _():
        for copy in copies:
            copy.start()
        sums_ref[...] = jnp.zeros_like(sums_ref)
        grad_place_ref[...] = jnp.zeros_like(grad_place_ref)

    grad_normed = grad_hidden_ref[...]
    for part in range(blocks):
        pl.when(image == 0)(copies[part].wait)
        grad_normed = grad_normed + product_along(grad_qkv_ref[part], wide_ref[part])
    unit, rstd = normal_rows(merged_ref[0])
    sums_ref[0:1, :] += jnp.sum(grad_normed * unit, axis=0, keepdims=True)
    slanted = grad_normed * gain_ref[...]
    back = (
        slanted
        - jnp.mean(slanted, axis=-1, keepdims=True)
        - unit * jnp.mean(slanted * unit, axis=-1, keepdims=True)
    )
    grad_merged = grad_stream_ref[0] + rstd * back
    slot = lax.broadcasted_iota(jnp.int32, (slots, slots), 0)
    member = slot == map_ref[0]
    hot = jnp.where(member, 1.0, 0.0).astype(jnp.bfloat16)
    total = jnp.sum(jnp.where(member, row_ref[0], 0.0), axis=1, keepdims=True)
    vacant = lax.broadcasted_iota(jnp.int32, (slots, 1), 0) >= live_count
    total = total + jnp.where(vacant, 1.0, 0.0)
    high, low = split_two(grad_merged / total)
    grad_patches = (product_across(hot, high) + product_across(hot, low)) * column_ref[0]
    grad_patch_ref[0] = grad_patches.astype(jnp.bfloat16)
    grad_place_ref[...] += grad_patches
    sums_ref[1:2, :] += jnp.sum(grad_patches, axis=0, keepdims=True)


def block(shape, index_map):
    return pl.BlockSpec(shape, index_map)


def per_image(rows, width):
    return block((1, rows, width), lambda image, counts: (image, 0, 0))


def whole(*shape):
    return block(shape, lambda *_: (0,) * len(shape))


anywhere = pl.BlockSpec(memory_space=pl.ANY)
roomy = pltpu.CompilerParams(vmem_limit_bytes=60 * 1024 * 1024)


long = pl.CostEstimate(flops=60_000_000_000, bytes_accessed=1000, transcendentals=0)


def image_call(kernel, images, in_specs, out_specs, out_shape, scratch=(), name=None):
    return pl.pallas_call(
        kernel,
        grid_spec=pltpu.PrefetchScalarGridSpec(
            num_scalar_prefetch=1,
            grid=(images,),
            in_specs=in_specs,
            out_specs=out_specs,
            scratch_shapes=list(scratch),
        ),
        out_shape=out_shape,
        compiler_params=roomy,
        cost_estimate=long,
        name=name,
    )


def picked(terms, axis, index):
    return [lax.dynamic_index_in_dim(term, index, axis, keepdims=False) for term in terms]


def added(terms):
    total = terms[0].astype(jnp.float32)
    for term in terms[1:]:
        total = total + term.astype(jnp.float32)
    return total


def behind(terms, after):
    if after is None:
        return terms
    return lax.optimization_barrier((terms, after))[0]


def traded(terms, axis, index, count, mesh_axis, stride):
    size = lax.axis_size(mesh_axis)
    sends = [
        added(picked(terms, axis, index ^ turn)).astype(jnp.bfloat16) for turn in range(1, count)
    ]
    after = yield sends
    got = [
        lax.ppermute(send, mesh_axis, bit_swap(size, turn * stride))
        for turn, send in enumerate(sends, 1)
    ]
    return picked(terms, axis, index) + behind(got, after)


def core_terms(mine, other):
    after = yield [other]
    got = behind([core_swap(other)], after)[0]
    return [
        term.reshape(*term.shape[:-3], term.shape[-3] // 2, 2, *term.shape[-2:])
        for term in (mine, got)
    ]


def rep_swap(own):
    return lax.ppermute(own, "rep", bit_swap(2, 1))


def places():
    place = lax.axis_index("fsdp")
    return place // 4, (place // 2) % 2


def column_parts(width):
    reps = lax.axis_size("rep")
    return reps if width % (128 * reps) == 0 else 1


def reduce_columns(mine, other):
    high, middle = places()
    parts, count = mine.shape[0], mine.shape[1] // 2
    terms = yield from core_terms(mine, other)
    if parts > 1:
        terms = yield from traded(terms, 0, lax.axis_index("rep"), parts, "rep", 1)
    else:
        terms = [term[0] for term in terms]
    terms = yield from traded(terms, 1, middle, 2, "fsdp", 2)
    terms = yield from traded(terms, 0, high, count, "fsdp", 4)
    own = added(terms).astype(jnp.bfloat16)
    after = yield [own]
    if parts == 1:
        return lax.psum(own, "rep")
    if parts == 2:
        got = behind([rep_swap(own)], after)[0]
        first, second = ordered_pair(own, got, "rep", 1)
        return jnp.concatenate([first, second], axis=1)
    return lax.all_gather(own, "rep", axis=1, tiled=True)


def reduce_rows_last(mine, other):
    high, middle = places()
    count = mine.shape[0] // 2
    terms = yield from core_terms(mine, other)
    terms = yield from traded(terms, 1, middle, 2, "fsdp", 2)
    terms = yield from traded(terms, 0, high, count, "fsdp", 4)
    own = added(terms).astype(jnp.bfloat16)
    after = yield [own]
    if lax.axis_size("rep") == 2:
        got = behind([rep_swap(own)], after)
        return added([own, *got]).astype(jnp.bfloat16)
    return lax.psum(own, "rep")


def core_swap(own):
    return lax.ppermute(own, "fsdp", bit_swap(lax.axis_size("fsdp"), 1))


def middle_swap(own):
    return lax.ppermute(own, "fsdp", bit_swap(lax.axis_size("fsdp"), 2))


def high_gather(own):
    owners = lax.axis_size("fsdp")
    after = yield [own]
    got = [lax.ppermute(own, "fsdp", bit_swap(owners, turn)) for turn in range(4, owners, 4)]
    return [own] + behind(got, after)


def with_cores(found):
    after = yield [item[0] for item in found]
    got = behind([core_swap(item[0]) for item in found], after)
    return found + [
        (array, [turn + 1 for turn in turns], parts)
        for array, (_, turns, parts) in zip(got, found, strict=True)
    ]


def gather_plain(own):
    after_high = yield from high_gather(own)
    near = jnp.stack(after_high)
    turns = list(range(0, lax.axis_size("fsdp"), 4))
    after = yield [near]
    far = behind([middle_swap(near)], after)[0]
    whole_rows = [None] * len(turns)
    found = [(near, turns, whole_rows), (far, [turn + 2 for turn in turns], whole_rows)]
    return (yield from with_cores(found))


def own_columns(own):
    half = own.shape[-1] // 2
    return lax.dynamic_slice_in_dim(own, lax.axis_index("rep") * half, half, own.ndim - 1)


def gather_split(own):
    if lax.axis_size("rep") != 2:
        return (yield from gather_plain(own))
    after_high = yield from high_gather(own_columns(own))
    turns = list(range(0, lax.axis_size("fsdp"), 4))
    cut = len(turns) // 2
    early, late = jnp.stack(after_high[:cut]), jnp.stack(after_high[cut:])
    after = yield [early, late]
    got = behind([rep_swap(early), middle_swap(late)], after)
    early, late = (jnp.concatenate(pair) for pair in zip((early, late), got, strict=True))
    after = yield [early, late]
    got = [middle_swap(early), rep_swap(late)]
    early, late, *got = behind([early, late, *got], after if after is not None else ())
    far = lambda some: [turn + 2 for turn in some]
    first, second = turns[:cut], turns[cut:]
    near_parts, all_parts = [0] * cut + [1] * cut, [0] * (2 * cut)
    found = [
        (early, first + first, near_parts),
        (got[0], far(first + first), near_parts),
        (late, second + far(second), all_parts),
        (got[1], second + far(second), [1] * (2 * cut)),
    ]
    return (yield from with_cores(found))


def assemble_copies(place_ref, sources, found, out_ref, columns, sem):
    copies = []
    for source, (turns, parts) in zip(sources, found, strict=True):
        rows, width = source.shape[2:]
        for slot, (turn, part) in enumerate(zip(turns, parts, strict=True)):
            owner = place_ref[0] ^ turn
            row = pl.ds(pl.multiple_of(owner * rows, rows), rows)
            if part is None:
                piece, target = source.at[slot, :, :, columns], out_ref.at[:, row, :]
            else:
                side = pl.ds(pl.multiple_of((place_ref[1] ^ part) * width, width), width)
                piece, target = source.at[slot], out_ref.at[:, row, side]
            copies.append(pltpu.make_async_copy(piece, target, sem.at[len(copies)]))
    return copies


def gathered(items):
    arrays = [item[0] for item in items]
    found = tuple((tuple(item[1]), tuple(item[2])) for item in items)
    segments, rows, width = arrays[0].shape[1:]
    if found[0][1][0] is not None:
        width = 2 * width
    owners = sum(len(item[0]) for item in found) * arrays[0].shape[3] // width
    return arrays, found, (segments, owners * rows, width)


def gather_scratch(found, size):
    return [
        pltpu.VMEM(size, jnp.bfloat16),
        pltpu.SemaphoreType.DMA((sum(len(item[0]) for item in found),)),
        pltpu.SemaphoreType.DMA,
    ]


def fetch(place_ref, sources, found, held_ref, sem):
    for copy in assemble_copies(place_ref, sources, found, held_ref, slice(None), sem):
        copy.start()


def fetched(place_ref, sources, found, held_ref, sem):
    for copy in assemble_copies(place_ref, sources, found, held_ref, slice(None), sem):
        copy.wait()


def assemble_small_kernel(place_ref, *refs, found, width):
    embed_ref, beside_out_ref, beside_ref, sem, beside_sem = refs[-5:]
    sources = refs[: len(found)]
    first = slice(0, width)
    second = slice(width, sources[0].shape[3])
    copies = assemble_copies(place_ref, sources, found, embed_ref, first, sem)
    copies += assemble_copies(place_ref, sources, found, beside_ref, second, beside_sem)
    for copy in copies:
        copy.start()
    for copy in copies:
        copy.wait()
    beside_out_ref[...] = beside_ref[0].astype(jnp.float32).T


def assembled_small(place, items, owners, width, guards):
    arrays, found, _ = gathered(items)
    rows, whole_width = arrays[0].shape[2:]
    beside = whole_width - width
    count = sum(len(item[0]) for item in found)
    embed, table = pl.pallas_call(
        lambda place_ref, *refs: assemble_small_kernel(
            place_ref, *refs[: len(arrays)], *refs[-5:], found=found, width=width
        ),
        grid_spec=pltpu.PrefetchScalarGridSpec(
            num_scalar_prefetch=1,
            grid=(1,),
            in_specs=[anywhere] * (len(arrays) + len(guards)),
            out_specs=[whole(1, owners * rows, width), whole(beside, owners * rows)],
            scratch_shapes=[
                pltpu.VMEM((1, owners * rows, beside), jnp.bfloat16),
                pltpu.SemaphoreType.DMA((count,)),
                pltpu.SemaphoreType.DMA((count,)),
            ],
        ),
        out_shape=[
            jax.ShapeDtypeStruct((1, owners * rows, width), jnp.bfloat16),
            jax.ShapeDtypeStruct((beside, owners * rows), jnp.float32),
        ],
        compiler_params=roomy,
        cost_estimate=long,
        name="assemble_small",
    )(place, *arrays, *guards)
    return embed[0], table


def first_behind(value, after):
    return lax.optimization_barrier((value, after))[0]


class Flow:
    def __init__(self, steps):
        self.steps, self.result = steps, None

    def go(self, after=None):
        try:
            return self.steps.send(after)
        except StopIteration as end:
            self.result = end.value
            return []

    def finish(self):
        while self.result is None:
            self.go()
        return self.result


def split_cores(result, core, mine_ref, other_ref):
    chips, rows, width = mine_ref.shape[-3:]
    pairs = result.astype(jnp.bfloat16).reshape(chips, 2, rows, result.shape[1])
    first, second = pairs[:, 0], pairs[:, 1]
    for ref, (left, right) in ((mine_ref, (first, second)), (other_ref, (second, first))):
        values = jnp.where(core == 0, left, right)
        if len(ref.shape) == 3:
            ref[...] = values
        else:
            for part in range(ref.shape[0]):
                ref[part] = values[:, :, part * width : (part + 1) * width]


def narrow_grad_kernel(
    core_ref, attended_ref, hidden_ref, branch_ref, mine_hbm, other_hbm, total_ref, sem
):
    step = pl.program_id(0)
    width = branch_ref.shape[1]
    parts, chips, rows, columns = mine_hbm.shape

    @pl.when(step == 0)
    def _():
        total_ref[:width, :] = product_across(attended_ref[...], branch_ref[...]).astype(
            jnp.bfloat16
        )

    @pl.when(step > 0)
    def _():
        at = pl.multiple_of(step * width, width)
        total_ref[pl.ds(at, width), :] = product_across(hidden_ref[0], branch_ref[...]).astype(
            jnp.bfloat16
        )

    @pl.when(step == pl.num_programs(0) - 1)
    def _():
        core = core_ref[0]
        copies = []
        for chip in range(chips):
            for side, out in enumerate((mine_hbm, other_hbm)):
                owner = 2 * chip + (core ^ side)
                at = pl.ds(pl.multiple_of(owner * rows, rows), rows)
                for part in range(parts):
                    source = total_ref.at[at, part * columns : (part + 1) * columns]
                    copies.append(
                        pltpu.make_async_copy(source, out.at[part, chip], sem.at[len(copies)])
                    )
        for copy in copies:
            copy.start()
        for copy in copies:
            copy.wait()


def wide_grad_kernel(core_ref, normed_ref, *refs):
    *grad_refs, mine_ref, other_ref = refs
    total = None
    for part, grad_ref in enumerate(grad_refs):
        rows = grad_ref.shape[1]
        term = product_across(normed_ref[part * rows : (part + 1) * rows, :], grad_ref[0])
        total = term if total is None else total + term
    split_cores(total, core_ref[0], mine_ref, other_ref)


def wide_project_grad_kernel(
    core_ref, normed_ref, grad_ref, pooled_ref, embeds_ref, mine_ref, other_ref
):
    last = pl.program_id(0) == pl.num_programs(0) - 1

    @pl.when(jnp.logical_not(last))
    def _():
        wide_grad_kernel(core_ref, normed_ref, grad_ref, mine_ref, other_ref)

    @pl.when(last)
    def _():
        split_cores(
            product_across(pooled_ref[...], embeds_ref[...]), core_ref[0], mine_ref, other_ref
        )


def embed_grad_kernel(core_ref, pixel_ref, *refs):
    *grad_refs, table_ref, mine_ref, other_ref = refs
    parts = len(grad_refs) // 2
    total, place = None, None
    for part in range(parts):
        rows = grad_refs[part].shape[0]
        term = product_across(pixel_ref[part * rows : (part + 1) * rows, :], grad_refs[part][...])
        total = term if total is None else total + term
        own = grad_refs[parts + part][...]
        place = own if place is None else place + own
    width = total.shape[1]
    beside = mine_ref.shape[2] - width
    spare = jnp.zeros((beside - place.shape[0] - table_ref.shape[0], width), jnp.float32)
    place = jnp.concatenate([place, table_ref[...], spare], axis=0).T
    split_cores(jnp.concatenate([total, place], axis=1), core_ref[0], mine_ref, other_ref)


def square_kernel(*refs):
    *shard_refs, total_ref = refs
    total = jnp.zeros((1, 1), jnp.float32)
    for shard_ref in shard_refs:
        values = shard_ref[...].astype(jnp.float32)
        columns = jnp.sum(values * values, axis=0, keepdims=True)
        total = total + jnp.sum(columns, axis=1, keepdims=True)
    total_ref[...] = jnp.broadcast_to(total, total_ref.shape)


def update_kernel(
    total_ref, narrow_ref, hidden_ref, qkv_ref, embed_ref, *refs, wide_rows
):
    weights, moments, squares = refs[:7], refs[7:14], refs[14:21]
    changes, clips = refs[21:28], refs[28:35]
    factor = clip_bound / jnp.maximum(jnp.sqrt(total_ref[:1, :1]), clip_bound)
    width = narrow_ref.shape[1]

    def update(index, rows, columns, gradient):
        at = (slice(*rows), slice(*columns))
        change, clipped = adam_step(
            weights[index][at],
            gradient.astype(jnp.float32),
            moments[index][at],
            squares[index][at],
            factor,
        )
        changes[index][at] = change
        clips[index][at] = clipped

    everything = (None,)
    update(0, everything, everything, embed_ref[:, :width])
    blocks = weights[2].shape[1] // width
    for k in range(blocks):
        source, at = (qkv_ref, k) if k < 3 else (hidden_ref, k - 3)
        update(
            2,
            everything,
            (k * width, (k + 1) * width),
            source[at * wide_rows : (at + 1) * wide_rows, :],
        )
    update(3, everything, everything, narrow_ref[...])
    update(4, everything, everything, hidden_ref[(blocks - 3) * wide_rows :, :])
    beside = embed_ref[:, width:].astype(jnp.float32)
    slots = weights[1].shape[1]
    update(1, everything, everything, beside[:, :slots])
    beside = beside.T
    at = padded_rows(slots)
    scale_rows = weights[5].shape[0]
    update(5, everything, everything, beside[at : at + scale_rows, :])
    at += scale_rows
    update(6, everything, everything, beside[at : at + weights[6].shape[0], :])


def per_device(
    pixels,
    merge_map,
    merge_weight,
    counts,
    captions,
    pairing,
    embedder,
    positions,
    widener,
    narrower,
    projector,
    scales,
    biases,
    moment_embedder,
    moment_positions,
    moment_widener,
    moment_narrower,
    moment_projector,
    moment_scales,
    moment_biases,
    square_embedder,
    square_positions,
    square_widener,
    square_narrower,
    square_projector,
    square_scales,
    square_biases,
):
    weights = (embedder, positions, widener, narrower, projector, scales, biases)
    owners = lax.axis_size("fsdp")
    micro_count, images_dev, slot_total, patch_size = pixels.shape
    model_width = embedder.shape[1]
    wide_rows = embedder.shape[0]
    narrow_rows = narrower.shape[0]
    hidden_width = narrow_rows * owners - model_width
    hidden_blocks = hidden_width // model_width
    head_size = model_width // HEADS
    images_all = pairing.shape[1]
    logit_factor = logit_temper * captions.shape[2] ** (-0.5)
    images = micro_count * images_dev
    slots = padded_rows(slot_total)
    spare = slots - slot_total
    rows = images * slots
    pixel_rows = jnp.pad(
        pixels.reshape(images, slot_total, patch_size), ((0, 0), (0, spare), (0, 0))
    )
    slot_map = jnp.pad(
        merge_map.reshape(images, 1, slot_total), ((0, 0), (0, 0), (0, spare)), constant_values=-1
    )
    row_weight = jnp.pad(merge_weight.reshape(images, 1, slot_total), ((0, 0), (0, 0), (0, spare)))
    column_weight = row_weight.reshape(images, slots, 1)
    live_counts = counts.reshape(images)
    f32, low = jnp.float32, jnp.bfloat16
    shape = jax.ShapeDtypeStruct
    place = jnp.stack([lax.axis_index("fsdp"), lax.axis_index("rep")]).astype(jnp.int32)
    bias_rows = biases.shape[0] // wide_rows
    scale_rows = scales.shape[0]
    table_rows = padded_rows(scale_rows + bias_rows)
    small_rows = -(-(slots + table_rows) // 128) * 128
    beside = jnp.concatenate(
        [
            jnp.pad(positions.T, ((0, 0), (0, spare))),
            scales.T,
            biases.reshape(bias_rows, wide_rows).T,
        ],
        axis=1,
    )
    beside = jnp.pad(beside, ((0, 0), (0, small_rows - beside.shape[1]))).astype(low)
    small_piece = jnp.concatenate([embedder.astype(low), beside], axis=1)
    wide_low = widener.astype(low)
    blocks_of = lambda first, count: [
        wide_low[:, k * model_width : (k + 1) * model_width] for k in range(first, first + count)
    ]
    qkv_piece = jnp.stack(blocks_of(0, 3))
    hidden_piece = jnp.stack(blocks_of(3, hidden_blocks) + [projector.astype(low)])
    narrow_piece = narrower.astype(low)[None]
    small_get = Flow(gather_plain(small_piece[None]))
    small_get.go()
    sent = small_get.go()
    qkv_get = Flow(gather_split(first_behind(qkv_piece, sent)))
    sent = qkv_get.go()
    sent = small_get.go()
    guards = qkv_get.go(sent)
    embed_full, table = assembled_small(place, small_get.finish(), owners, model_width, guards)
    scale_float = table[slots : slots + scale_rows]
    bias_float = jnp.swapaxes(
        table[slots + scale_rows : slots + scale_rows + bias_rows].reshape(
            bias_rows, owners, wide_rows
        ),
        0,
        1,
    ).reshape(-1)
    out_bias = bias_float[hidden_width : hidden_width + model_width].reshape(1, model_width)
    place_bias = table[:slots] + bias_float[hidden_width + model_width :]
    guards = qkv_get.go()
    hidden_get = Flow(gather_split(first_behind(hidden_piece, (guards, table))))
    guards += hidden_get.go()
    merged, normed = image_call(
        embed_kernel,
        images,
        [
            per_image(slots, patch_size),
            per_image(1, slots),
            per_image(1, slots),
            per_image(slots, 1),
            whole(patch_size, model_width),
            whole(slots, model_width),
            whole(1, model_width),
        ]
        + [anywhere] * len(guards),
        [per_image(slots, model_width)] * 2,
        [shape((images, slots, model_width), f32), shape((images, slots, model_width), low)],
        name="embed",
    )(
        live_counts, pixel_rows, slot_map, row_weight, column_weight, embed_full, place_bias,
        scale_float[0:1], *guards,
    )
    qkv_get.go()
    qkv_parts = qkv_get.finish()
    guards = hidden_get.go(qkv_parts[-1][0])
    narrow_get = Flow(gather_split(first_behind(narrow_piece, guards)))
    guards += narrow_get.go()
    arrays, found, size = gathered(qkv_parts)
    normed_rows = normed.reshape(rows, model_width)
    column_block = lambda index_map: block((1, rows, model_width), index_map)
    heads, rstd, wide_qkv = pl.pallas_call(
        functools.partial(widen_heads_kernel, found=found, chunk=slots, head_size=head_size),
        grid_spec=pltpu.PrefetchScalarGridSpec(
            num_scalar_prefetch=1,
            grid=(2,),
            in_specs=[whole(rows, model_width), block((1, 1, model_width), lambda k, _: (k, 0, 0))]
            + [anywhere] * (len(arrays) + len(guards)),
            out_specs=[column_block(lambda k, _: (k, 0, 0))] * 2 + [anywhere],
            scratch_shapes=gather_scratch(found, size),
        ),
        out_shape=[
            shape((2, rows, model_width), low), shape((2, rows, model_width), f32), shape(size, low)
        ],
        compiler_params=roomy,
        cost_estimate=long,
        name="widen_heads",
    )(place, normed_rows, scale_float[2:4].reshape(2, 1, model_width), *arrays, *guards)
    guards = hidden_get.go(heads)
    values = pl.pallas_call(
        widen_value_kernel,
        grid=(1,),
        in_specs=[whole(rows, model_width), block((1, model_width, model_width), lambda k: (2, 0, 0))]
        + [anywhere] * (1 + len(guards)),
        out_specs=column_block(lambda k: (0, 0, 0)),
        out_shape=shape((1, rows, model_width), low),
        compiler_params=roomy,
        cost_estimate=long,
        name="widen_values",
    )(normed_rows, wide_qkv, heads, *guards)
    image_columns = lambda parts: block(
        (parts, slots, model_width), lambda image, counts: (0, image, 0)
    )
    guards = narrow_get.go(heads)
    (attended,) = image_call(
        functools.partial(attend_kernel, head_size=head_size),
        images,
        [image_columns(2), image_columns(1)] + [anywhere] * len(guards),
        [per_image(slots, model_width)],
        [shape((images, slots, model_width), low)],
        name="attend",
    )(live_counts, heads, values, *guards)
    guards = narrow_get.go() + [attended]
    hidden_get.go(guards)
    arrays, found, size = gathered(hidden_get.finish())
    hidden, slope, wide_hidden = pl.pallas_call(
        functools.partial(widen_hidden_kernel, found=found, chunk=slots),
        grid_spec=pltpu.PrefetchScalarGridSpec(
            num_scalar_prefetch=1,
            grid=(hidden_blocks,),
            in_specs=[whole(rows, model_width), block((1, 1, model_width), lambda k, _: (k, 0, 0))]
            + [anywhere] * (len(arrays) + len(guards)),
            out_specs=[column_block(lambda k, _: (k, 0, 0))] * 2 + [anywhere],
            scratch_shapes=gather_scratch(found, size),
        ),
        out_shape=[shape((hidden_blocks, rows, model_width), low)] * 2 + [shape(size, low)],
        compiler_params=roomy,
        cost_estimate=long,
        name="widen_hidden",
    )(
        place, normed_rows, bias_float[:hidden_width].reshape(hidden_blocks, 1, model_width),
        *arrays, *guards,
    )
    project_full = wide_hidden[hidden_blocks]
    narrow_get.go(hidden)
    arrays, found, size = gathered(narrow_get.finish())
    narrow_scratch = [
        pltpu.VMEM((hidden_width + model_width, model_width), low), pltpu.SemaphoreType.DMA
    ]
    stream, pooled, narrow_full = pl.pallas_call(
        functools.partial(join_kernel, found=found),
        grid_spec=pltpu.PrefetchScalarGridSpec(
            num_scalar_prefetch=2,
            grid=(images,),
            in_specs=[
                block((1, slots, model_width), lambda image, *_: (image, 0, 0)),
                block((hidden_blocks, slots, model_width), lambda image, *_: (0, image, 0)),
                block((1, slots, model_width), lambda image, *_: (image, 0, 0)),
                whole(1, model_width),
                whole(1, model_width),
            ]
            + [anywhere] * len(arrays),
            out_specs=[
                block((1, slots, model_width), lambda image, *_: (image, 0, 0)),
                block((1, 1, model_width), lambda image, *_: (image, 0, 0)),
                anywhere,
            ],
            scratch_shapes=gather_scratch(found, size),
        ),
        out_shape=[
            shape((images, slots, model_width), f32),
            shape((images, 1, model_width), f32),
            shape(size, low),
        ],
        compiler_params=roomy,
        cost_estimate=long,
        name="join",
    )(live_counts, place, attended, hidden, merged, out_bias, scale_float[1:2], *arrays)
    narrow_full = narrow_full[0]
    pooled_low = pooled.reshape(images, model_width).astype(low)
    embeds = product(pooled_low, project_full).astype(low)
    embeds = embeds.reshape(micro_count, images_dev, -1)
    logits = jnp.einsum("mie,mje->mij", embeds, captions, preferred_element_type=f32) * logit_factor
    image_ids = jnp.arange(images_all, dtype=jnp.int32)
    first_row = (lax.axis_index("rep") * owners + lax.axis_index("fsdp")) * images_dev
    own_pairs = lax.dynamic_slice_in_dim(pairing, first_row, images_dev, 1)
    target = (own_pairs[:, :, None] == image_ids[None, None, :]).astype(jnp.float32)
    row_top = jnp.max(logits, axis=2, keepdims=True)
    row_logsum = row_top[:, :, 0] + jnp.log(jnp.sum(jnp.exp(logits - row_top), axis=2))
    own_top = jnp.max(logits, axis=1)
    own_total = jnp.sum(jnp.exp(logits - own_top[:, None, :]), axis=1)
    picked = jnp.sum(logits * target, axis=2)
    counts_float = counts.astype(jnp.float32)
    scalars = jnp.concatenate(
        [
            jnp.sum(counts_float * (picked - row_logsum), axis=1),
            jnp.sum(picked, axis=1),
            jnp.sum(counts_float, axis=1),
        ]
    )
    sums = jnp.pad(scalars[None, :], ((0, 0), (0, images_all - scalars.shape[0])))
    column_top, column_total, sums = column_totals(own_top, own_total, sums)
    column_logsum = column_top + jnp.log(column_total)
    row_terms = sums[0, :micro_count]
    picked_sums = sums[0, micro_count : 2 * micro_count]
    weight_totals = sums[0, 2 * micro_count : 3 * micro_count]
    weight_total_all = jnp.sum(weight_totals)
    part_losses = 0.5 * (
        -row_terms / weight_totals - (picked_sums - jnp.sum(column_logsum, axis=1)) / images_all
    )
    objective = jnp.sum(part_losses) / micro_count
    row_soft = jnp.exp(logits - row_logsum[:, :, None])
    column_soft = jnp.exp(logits - column_logsum[:, None, :])
    all_grad_logits = (
        0.5
        / micro_count
        * (
            (counts_float / weight_totals[:, None])[:, :, None] * (row_soft - target)
            + (column_soft - target) / images_all
        )
    )
    grad_product = (all_grad_logits * logit_factor).astype(low)
    grad_embeds = (
        jnp.einsum("mij,mje->mie", grad_product, captions, preferred_element_type=f32)
        .astype(low)
        .reshape(images, -1)
    )
    grad_pooled = product_along(grad_embeds, project_full)
    grad_stream, grad_branch, grad_attended, grad_act, out_sums = image_call(
        branch_kernel,
        images,
        [
            per_image(slots, model_width),
            per_image(1, model_width),
            whole(1, model_width),
            image_columns(hidden_blocks),
            anywhere,
        ],
        [
            per_image(slots, model_width),
            per_image(slots, model_width),
            per_image(slots, model_width),
            image_columns(hidden_blocks),
            whole(8, model_width),
        ],
        [
            shape((images, slots, model_width), f32),
            shape((images, slots, model_width), low),
            shape((images, slots, model_width), low),
            shape((hidden_blocks, rows, model_width), low),
            shape((8, model_width), f32),
        ],
        narrow_scratch,
        name="branch",
    )(
        live_counts, stream, grad_pooled.reshape(images, 1, model_width), scale_float[1:2], slope,
        narrow_full,
    )
    core = (lax.axis_index("fsdp") % 2).reshape(1)
    chips = owners // 2
    branch_rows = grad_branch.reshape(rows, model_width)
    halves = lambda count, width: [shape((chips, count, width), low)] * 2
    parts_wide = column_parts(model_width)
    part_width = model_width // parts_wide
    split_halves = lambda count: [shape((parts_wide, chips, count, part_width), low)] * 2
    narrow_halves = pl.pallas_call(
        narrow_grad_kernel,
        grid_spec=pltpu.PrefetchScalarGridSpec(
            num_scalar_prefetch=1,
            grid=(1 + hidden_blocks,),
            in_specs=[
                whole(rows, model_width),
                block((1, rows, model_width), lambda k, _: (jnp.maximum(k - 1, 0), 0, 0)),
                whole(rows, model_width),
            ],
            out_specs=[anywhere] * 2,
            scratch_shapes=[
                pltpu.VMEM((hidden_width + model_width, model_width), low),
                pltpu.SemaphoreType.DMA((2 * parts_wide * chips,)),
            ],
        ),
        out_shape=split_halves(narrow_rows),
        compiler_params=roomy,
        cost_estimate=long,
        name="narrow_grad",
    )(core, attended.reshape(rows, model_width), hidden, branch_rows)
    narrow_flow = Flow(reduce_columns(*narrow_halves))
    narrow_flow.go()
    owner_block = block((chips, wide_rows, model_width), lambda k, _: (0, k, 0))
    few = padded_rows(images)
    hidden_halves = pl.pallas_call(
        wide_project_grad_kernel,
        grid_spec=pltpu.PrefetchScalarGridSpec(
            num_scalar_prefetch=1,
            grid=(hidden_blocks + 1,),
            in_specs=[
                whole(rows, model_width),
                block(
                    (1, rows, model_width), lambda k, _: (jnp.minimum(k, hidden_blocks - 1), 0, 0)
                ),
                whole(few, model_width),
                whole(few, model_width),
            ],
            out_specs=[owner_block] * 2,
        ),
        out_shape=halves((hidden_blocks + 1) * wide_rows, model_width),
        compiler_params=roomy,
        cost_estimate=long,
        name="hidden_grad",
    )(
        core, normed_rows, grad_act, jnp.pad(pooled_low, ((0, few - images), (0, 0))),
        jnp.pad(grad_embeds, ((0, few - images), (0, 0))),
    )
    hidden_flow = Flow(reduce_rows_last(*hidden_halves))
    hidden_flow.go()
    parts = images_dev
    per_part = images // parts
    part_rows = per_part * slots

    def shifted(base, rows_count):
        return block((1, rows_count, model_width), lambda image, counts: (base + image, 0, 0))

    def shifted_columns(base, count):
        return block((count, slots, model_width), lambda image, counts: (0, base + image, 0))

    head_gains = scale_float[2:4].reshape(2, 1, model_width)
    guards = narrow_flow.go()
    grad_qkv, head_sums = [], 0.0
    for part in range(parts):
        base = part * per_part
        grads, sums_part = image_call(
            functools.partial(attend_back_kernel, base=base, head_size=head_size),
            per_part,
            [
                shifted_columns(base, 2),
                shifted_columns(base, 1),
                shifted_columns(base, 2),
                shifted(base, slots),
                whole(2, 1, model_width),
            ]
            + [anywhere] * len(guards),
            [image_columns(3), whole(8, model_width)],
            [shape((3, part_rows, model_width), low), shape((8, model_width), f32)],
            [pltpu.VMEM((2, slots, model_width), f32)],
            name="attend_back",
        )(live_counts, heads, values, rstd, grad_attended, head_gains, *guards)
        grad_qkv.append(grads)
        head_sums = head_sums + sums_part
        guards = [grads]
        if part == 0:
            guards += hidden_flow.go(grads)
    guards += narrow_flow.go(grads)
    qkv_halves = pl.pallas_call(
        lambda core_ref, normed_ref, *refs: wide_grad_kernel(
            core_ref, normed_ref, *refs[:parts], *refs[-2:]
        ),
        grid_spec=pltpu.PrefetchScalarGridSpec(
            num_scalar_prefetch=1,
            grid=(3,),
            in_specs=[whole(rows, model_width)]
            + [block((1, part_rows, model_width), lambda k, _: (k, 0, 0))] * parts
            + [anywhere] * len(guards),
            out_specs=[block((parts_wide, chips, wide_rows, part_width), lambda k, _: (0, 0, k, 0))] * 2,
        ),
        out_shape=split_halves(3 * wide_rows),
        compiler_params=roomy,
        cost_estimate=long,
        name="qkv_grad",
    )(core, normed_rows, *grad_qkv, *guards)
    qkv_flow = Flow(reduce_columns(*qkv_halves))
    guards = qkv_flow.go()
    grad_hidden = pl.pallas_call(
        hidden_back_kernel,
        grid=(hidden_blocks,),
        in_specs=[
            block((1, rows, model_width), lambda k: (k, 0, 0)),
            block((1, model_width, model_width), lambda k: (k, 0, 0)),
        ]
        + [anywhere] * len(guards),
        out_specs=whole(rows, model_width),
        out_shape=shape((rows, model_width), f32),
        scratch_shapes=[pltpu.VMEM((rows, model_width), f32)],
        compiler_params=roomy,
        cost_estimate=long,
        name="hidden_back",
    )(grad_act, wide_hidden, *guards)
    guards = hidden_flow.go(grad_hidden) + qkv_flow.go(grad_hidden)
    grad_patches, grad_places, merge_sums = [], [], 0.0
    for part in range(parts):
        base = part * per_part
        grads, place_part, sums_part = image_call(
            functools.partial(merge_back_kernel, base=base),
            per_part,
            [
                image_columns(3),
                block((slots, model_width), lambda image, counts, base=base: (base + image, 0)),
                anywhere,
                shifted(base, slots),
                shifted(base, slots),
                whole(1, model_width),
                block((1, 1, slots), lambda image, counts, base=base: (base + image, 0, 0)),
                block((1, 1, slots), lambda image, counts, base=base: (base + image, 0, 0)),
                block((1, slots, 1), lambda image, counts, base=base: (base + image, 0, 0)),
            ]
            + [anywhere] * len(guards),
            [per_image(slots, model_width), whole(slots, model_width), whole(8, model_width)],
            [
                shape((per_part, slots, model_width), low),
                shape((slots, model_width), f32),
                shape((8, model_width), f32),
            ],
            [
                pltpu.VMEM((3, model_width, model_width), low),
                pltpu.SemaphoreType.DMA((3,)),
            ],
            name="merge_back",
        )(
            live_counts, grad_qkv[part], grad_hidden, wide_qkv, merged, grad_stream,
            scale_float[0:1], slot_map, row_weight, column_weight, *guards,
        )
        grad_patches.append(grads.reshape(part_rows, model_width))
        grad_places.append(place_part)
        merge_sums = merge_sums + sums_part
        guards = [grads]
        if part == 1:
            guards += qkv_flow.go(grads)
    guards += hidden_flow.go(grads) + narrow_flow.go(grads)
    grad_scale = jnp.stack([merge_sums[0], out_sums[hidden_blocks + 1], head_sums[0], head_sums[1]])
    grad_bias = jnp.concatenate([out_sums[: hidden_blocks + 1], merge_sums[1:2]]).reshape(
        owners, bias_rows, wide_rows
    )
    grad_bias = jnp.swapaxes(grad_bias, 0, 1).reshape(bias_rows, model_width)
    table = jnp.concatenate([grad_scale, grad_bias])
    table = jnp.pad(table, ((0, padded_rows(table.shape[0]) - table.shape[0]), (0, 0)))
    piece_width = small_piece.shape[1]
    embed_halves = pl.pallas_call(
        lambda core_ref, pixel_ref, *refs: embed_grad_kernel(
            core_ref, pixel_ref, *refs[: 2 * parts + 1], *refs[-2:]
        ),
        grid_spec=pltpu.PrefetchScalarGridSpec(
            num_scalar_prefetch=1,
            grid=(1,),
            in_specs=[whole(rows, patch_size)]
            + [whole(part_rows, model_width)] * parts
            + [whole(slots, model_width)] * parts
            + [whole(*table.shape)]
            + [anywhere] * len(guards),
            out_specs=[whole(chips, wide_rows, piece_width)] * 2,
        ),
        out_shape=halves(wide_rows, piece_width),
        compiler_params=roomy,
        cost_estimate=long,
        name="embed_grad",
    )(core, pixel_rows.reshape(rows, patch_size), *grad_patches, *grad_places, table, *guards)
    embed_flow = Flow(reduce_rows_last(*embed_halves))
    embed_flow.go()
    sent = embed_flow.go()
    hidden_flow.go(sent)
    sent = qkv_flow.go(sent) + narrow_flow.go(sent)
    sent = embed_flow.go(sent)
    narrow_flow.go(sent)
    sent = qkv_flow.go(sent)
    sent = embed_flow.go(sent)
    qkv_flow.go(sent)
    flows = (narrow_flow, hidden_flow, qkv_flow, embed_flow)
    shards = [flow.finish() for flow in flows]
    squares_sum = pl.pallas_call(
        square_kernel,
        out_shape=shape((8, 128), f32),
        compiler_params=roomy,
        name="squares",
    )(*shards)
    squares_sum = sum_over(squares_sum, "fsdp")
    total_norm = jnp.sqrt(squares_sum[0, 0])
    moments = (
        moment_embedder,
        moment_positions,
        moment_widener,
        moment_narrower,
        moment_projector,
        moment_scales,
        moment_biases,
    )
    squares = (
        square_embedder,
        square_positions,
        square_widener,
        square_narrower,
        square_projector,
        square_scales,
        square_biases,
    )
    as_rows = lambda arrays: [
        array.reshape(-1, wide_rows) if array.ndim == 1 else array.T if index % 7 == 1 else array
        for index, array in enumerate(arrays)
    ]
    outs = pl.pallas_call(
        functools.partial(update_kernel, wide_rows=wide_rows),
        out_shape=[shape(array.shape, f32) for array in as_rows(weights) * 2],
        compiler_params=roomy,
        name="update",
    )(squares_sum, *shards, *as_rows(weights), *as_rows(moments), *as_rows(squares))
    outs = [
        out.T if index % 7 == 1 else out.reshape(array.shape)
        for index, (out, array) in enumerate(zip(outs, weights * 2, strict=True))
    ]
    return (objective, weight_total_all, total_norm, *outs)


def solution(mesh):
    return jax.shard_map(
        per_device,
        mesh=mesh,
        in_specs=(
            P(None, ("rep", "fsdp"), None, None),
            P(None, ("rep", "fsdp"), None),
            P(None, ("rep", "fsdp"), None),
            P(None, ("rep", "fsdp")),
            P(),
            P(),
            P("fsdp", None),
            P(None, "fsdp"),
            P("fsdp", None),
            P("fsdp", None),
            P("fsdp", None),
            P(None, "fsdp"),
            P("fsdp"),
            P("fsdp", None),
            P(None, "fsdp"),
            P("fsdp", None),
            P("fsdp", None),
            P("fsdp", None),
            P(None, "fsdp"),
            P("fsdp"),
            P("fsdp", None),
            P(None, "fsdp"),
            P("fsdp", None),
            P("fsdp", None),
            P("fsdp", None),
            P(None, "fsdp"),
            P("fsdp"),
        ),
        out_specs=(
            P(),
            P(),
            P(),
            P("fsdp", None),
            P(None, "fsdp"),
            P("fsdp", None),
            P("fsdp", None),
            P("fsdp", None),
            P(None, "fsdp"),
            P("fsdp"),
            P("fsdp", None),
            P(None, "fsdp"),
            P("fsdp", None),
            P("fsdp", None),
            P("fsdp", None),
            P(None, "fsdp"),
            P("fsdp"),
        ),
        check_vma=False,
    )
```
